512 devices in a mesh: gy: 32 (over x_lo, z, core), gx: 16 (over x_hi, y).
Axes of the slice: x: 4 (x_hi: 2, x_lo: 2; x = x_hi * 2 + x_lo), y: 8, z: 8, core: 2. Of those that a mesh axis runs over, the one named last changes fastest.
Arguments:
- features: bfloat16 [2048, 256, 128], P('gy', 'gx'), may hold values from -40 to 40
- attention_gain: float32 [2, 128], replicated, may hold values from 0.25 to 1.75
- triple_weight: bfloat16 [2, 128, 384], replicated, may hold values from -0.5 to 0.5
- output_weight: bfloat16 [2, 128, 128], replicated, may hold values from -0.5 to 0.5
- position_bias: float32 [2, 4, 225], replicated, may hold values from -2 to 262
- hidden_gain: float32 [2, 128], replicated, may hold values from 0.25 to 1.75
- expand_weight: bfloat16 [2, 128, 512], replicated, may hold values from -0.5 to 0.5
- shrink_weight: bfloat16 [2, 512, 128], replicated, may hold values from -0.25 to 0.25
Outputs:
- result: float32 [2048, 256, 128], P('gy', 'gx')
The draws below stay inside these ranges and needn't reach their ends.
All inputs are finite; a program needn't handle non-finite values.
Results may differ from the reference program's by a relative error of at most 0.0033.
Values may be sent and summed in bfloat16 or wider, within the bound.
No kernel may reach another device: no remote copies, remote signals or barrier semaphores. Data moves between devices by JAX's collectives and lax.ppermute only.
A program may use at most 64 MiB of HBM per device.

```python
import math
import jax
import jax.numpy as jnp
from jax import lax

C = 128
HEADS = 4
HID = 512
WIN = 8
HD = 32
SHIFT = 4
ROWS = 2048
COLS = 256


def draw_features(key, part):
    key = jax.random.fold_in(key, 5)
    subkeys = jax.random.split(key, 3)
    channel_scale = jnp.exp(jax.random.uniform(subkeys[0], (C,), jnp.float32, 0.0, math.log(10.0)))
    token_scale = jnp.exp(jax.random.uniform(subkeys[1], (ROWS, COLS, 1), jnp.float32, 0.0, math.log(10.0)))
    raw_values = jax.random.truncated_normal(subkeys[2], -4.0, 4.0, (ROWS, COLS, C), jnp.float32)
    return (0.1 * raw_values * channel_scale * token_scale).astype(jnp.bfloat16)


def draw_position_bias(key, part):
    key = jax.random.fold_in(key, 9)
    subkeys = jax.random.split(key, 1)
    extent = 2 * WIN - 1
    values_table = jax.random.uniform(subkeys[0], (2, HEADS, extent * extent), jnp.float32, -2.0, 2.0)
    return values_table


def centred(key, dims, deviation, most, held_as=jnp.bfloat16):
    return jnp.clip(deviation * jax.random.normal(key, dims, jnp.float32), -most, most).astype(held_as)


def setup_inputs(seed: int = 0) -> dict:
    key_of = jax.random.split(jax.random.key(seed), 9)
    return {
        "features": draw_features(jax.random.fold_in(key_of[8], 71), 0),
        "attention_gain": jnp.clip(1.0 + 0.15 * jax.random.normal(key_of[1], (2, C), jnp.float32), 0.25, 1.75),
        "triple_weight": centred(key_of[2], (2, C, 3 * C), C ** -0.5, 0.5),
        "output_weight": centred(key_of[3], (2, C, C), C ** -0.5, 0.5),
        "position_bias": draw_position_bias(jax.random.fold_in(key_of[8], 71), 0),
        "hidden_gain": jnp.clip(1.0 + 0.15 * jax.random.normal(key_of[5], (2, C), jnp.float32), 0.25, 1.75),
        "expand_weight": centred(key_of[6], (2, C, HID), C ** -0.5, 0.5),
        "shrink_weight": centred(key_of[7], (2, HID, C), HID ** -0.5, 0.25),
    }


EPSILON = 1e-05

def layer_norm(values, gain_vector):
    center = values - lax.optimization_barrier(jnp.mean(values, axis=-1, keepdims=True))
    spread = lax.optimization_barrier(jnp.mean(center * center, axis=-1, keepdims=True))
    return (center * lax.rsqrt(spread + EPSILON) * gain_vector).astype(jnp.bfloat16)

def window_attention(triple, band_labels, bias_block, out_weight):
    breadth = triple.shape[1]
    windows = breadth // WIN
    pieces = triple.reshape(WIN, windows, WIN, 3, HEADS, HD).transpose(3, 1, 4, 0, 2, 5)
    pieces = pieces.reshape(3, windows, HEADS, WIN * WIN, HD).astype(jnp.float32)
    scores = jnp.einsum('whqd,whkd->whqk', pieces[0], pieces[1]) * HD ** (-0.5) + bias_block[None]
    labels_win = band_labels.reshape(WIN, windows, WIN).transpose(1, 0, 2).reshape(windows, WIN * WIN)
    scores = scores + jnp.where(labels_win[:, None, :, None] != labels_win[:, None, None, :], -100.0, 0.0).astype(jnp.float32)
    row_max = lax.optimization_barrier(jnp.max(scores, axis=-1, keepdims=True))
    powers = jnp.exp(scores - row_max)
    probabilities = (powers / lax.optimization_barrier(jnp.sum(powers, axis=-1, keepdims=True))).astype(jnp.bfloat16)
    context = jnp.einsum('whqk,whkd->whqd', probabilities.astype(jnp.float32), pieces[2]).astype(jnp.bfloat16)
    context = context.reshape(windows, HEADS, WIN, WIN, HD).transpose(2, 0, 3, 1, 4).reshape(WIN * breadth, C)
    branch = jnp.dot(context, out_weight, preferred_element_type=jnp.float32).astype(jnp.bfloat16)
    return branch.reshape(WIN, breadth, C)

def reference(features, attention_gain, triple_weight, output_weight, position_bias, hidden_gain, expand_weight, shrink_weight):
    extent = 2 * WIN - 1
    places = jnp.arange(WIN * WIN, dtype=jnp.int32)
    along_y = places // WIN
    along_x = places % WIN
    offset = (along_y[:, None] - along_y[None, :] + WIN - 1) * extent + along_x[:, None] - along_x[None, :] + WIN - 1
    tables = position_bias[:, :, offset]

    def run_block(inputs, labels, block_index):

        def one_band(packed):
            band_values, band_labels = packed
            normed = layer_norm(band_values, attention_gain[block_index])
            triple = jnp.dot(normed.reshape(-1, C), triple_weight[block_index], preferred_element_type=jnp.float32)
            triple = triple.astype(jnp.bfloat16).reshape(WIN, COLS, 3 * C)
            branch = window_attention(triple, band_labels, tables[block_index], output_weight[block_index])
            middle = band_values + branch.astype(jnp.float32)
            normed_mid = layer_norm(middle, hidden_gain[block_index])
            hidden = jax.nn.gelu(jnp.dot(normed_mid.reshape(-1, C), expand_weight[block_index], preferred_element_type=jnp.float32), approximate=False).astype(jnp.bfloat16)
            return middle + jnp.dot(hidden, shrink_weight[block_index], preferred_element_type=jnp.float32).reshape(WIN, COLS, C)
        outputs = lax.map(one_band, (inputs.reshape(ROWS // WIN, WIN, COLS, C), labels.reshape(ROWS // WIN, WIN, COLS)))
        return outputs.reshape(ROWS, COLS, C)
    first_out = run_block(features.astype(jnp.float32), jnp.zeros((ROWS, COLS), jnp.int32), 0)
    frame_rows = jnp.arange(ROWS, dtype=jnp.int32)
    frame_cols = jnp.arange(COLS, dtype=jnp.int32)
    row_label = (frame_rows >= ROWS - WIN).astype(jnp.int32) + (frame_rows >= ROWS - SHIFT).astype(jnp.int32)
    col_label = (frame_cols >= COLS - WIN).astype(jnp.int32) + (frame_cols >= COLS - SHIFT).astype(jnp.int32)
    labels = row_label[:, None] * 3 + col_label[None, :]
    rolled = jnp.roll(first_out, (-SHIFT, -SHIFT), axis=(0, 1))
    second = run_block(rolled, labels, 1)
    return jnp.roll(second, (SHIFT, SHIFT), axis=(0, 1))
```

```python
import math

import jax
import jax.numpy as jnp
from jax import lax
from jax.experimental import pallas as pl
from jax.experimental.pallas import tpu as pltpu
from jax.sharding import PartitionSpec as P

C = 128
HEADS = 4
HID = 512
WIN = 8
HD = 32
SHIFT = 4
EPSILON = 1e-05
LOG2E = math.log2(math.e)
SCALE = HD ** (-0.5) * LOG2E
F32 = jnp.float32
BF16 = jnp.bfloat16
NT = (((1,), (1,)), ((), ()))
TN = (((0,), (0,)), ((), ()))


def from_behind(x, axis, by):
    length = lax.axis_size(axis)
    return lax.ppermute(x, axis, [(i, (i + by) % length) for i in range(length)])


def iota(shape, dim):
    return lax.broadcasted_iota(jnp.int32, shape, dim)


def layer_norm(x, gain):
    center = x - jnp.mean(x, axis=-1, keepdims=True)
    spread = jnp.mean(center * center, axis=-1, keepdims=True)
    return center * lax.rsqrt(spread + EPSILON) * gain


def gelu(x):
    half = 0.5 * x
    return half + half * lax.erf(x * (0.5**0.5))


def fill_bias(pb_ref, block, store):
    sub = iota((8, 128), 0)
    lane = iota((8, 128), 1)
    place = lax.min((lane >> 3) * 15 + 7 + (lane & 7) - sub, 224)
    for head in range(HEADS):
        low = jnp.broadcast_to(pb_ref[block, head : head + 1, 0:128], (8, 128))
        high = jnp.broadcast_to(pb_ref[block, head : head + 1, 97:225], (8, 128))
        strip = jnp.where(
            place < 128,
            jnp.take_along_axis(low, lax.min(place, 127), axis=1),
            jnp.take_along_axis(high, lax.max(place - 97, 0), axis=1),
        )
        strip = strip * LOG2E
        for yj in range(8):
            turn = (128 - (7 - yj) * 8) % 128
            first = pltpu.roll(strip, turn, 1) if turn else strip
            second = pltpu.roll(strip, (turn + 64) % 128, 1)
            store(head, yj, jnp.where(lane < 64, first, second))


def lane_masks(rows):
    lane = iota((rows, 128), 1)
    left = jnp.where(lane < 64, 1.0, 0.0).astype(BF16)
    right = jnp.where(lane >= 64, 1.0, 0.0).astype(BF16)
    return left, right


def fill_weights(w_ref, block, wqv, wk):
    wqv[0:128, :] = jnp.transpose(w_ref[block, :, 0:128].astype(F32)).astype(BF16)
    wqv[128:256, :] = jnp.transpose(w_ref[block, :, 256:384].astype(F32)).astype(BF16)
    keys = w_ref[block, :, 128:256].astype(F32)
    turned = pltpu.roll(keys, 64, 1)
    lane = iota((128, 128), 1)
    zero = jnp.zeros((128, 128), F32)
    wk[0:128, 0:128] = jnp.where(lane < 64, keys, zero).astype(BF16)
    wk[0:128, 128:256] = jnp.where(lane < 64, turned, zero).astype(BF16)
    wk[128:256, 0:128] = jnp.where(lane >= 64, turned, zero).astype(BF16)
    wk[128:256, 128:256] = jnp.where(lane >= 64, keys, zero).astype(BF16)


def softmax_columns(s):
    p = jnp.exp2(s - jnp.max(s, axis=0, keepdims=True))
    return (p * (1.0 / jnp.sum(p, axis=0, keepdims=True))).astype(BF16)


def dot(a, b, dims=None):
    if dims is None:
        return jnp.dot(a, b, preferred_element_type=F32)
    return lax.dot_general(a, b, dims, preferred_element_type=F32)


def attention(query_tokens, key_tokens, masks, wqv, wk, bias_of):
    windows = len(key_tokens)
    if windows == 2:
        vt = dot(wqv[128:256, :], jnp.concatenate(key_tokens, axis=0), NT).astype(BF16)
        keys = dot(jnp.concatenate(key_tokens, axis=1), wk[...]).astype(BF16)
        keys = [keys[:, 0:128], keys[:, 128:256]]
        values = vt
    else:
        vt = dot(wqv[128:256, :], jnp.concatenate(key_tokens[0:2], axis=0), NT).astype(BF16)
        third = dot(
            wqv[128:256, :], jnp.concatenate([key_tokens[2], key_tokens[2]], axis=0), NT
        ).astype(BF16)
        values = jnp.concatenate([vt, third], axis=1)
        keys = dot(jnp.concatenate(key_tokens[0:2], axis=1), wk[...]).astype(BF16)
        last = dot(key_tokens[2], wk[0:128, :]).astype(BF16)
        keys = [
            jnp.concatenate([keys[:, 0:128], last[:, 0:128]], axis=1),
            jnp.concatenate([keys[:, 128:256], last[:, 128:256]], axis=1),
        ]
    qt = dot(wqv[0:128, :], query_tokens, NT).astype(BF16)
    zero = jnp.zeros((32, 128), BF16)
    out = []
    for pair in range(2):
        r = 64 * pair
        rows = []
        for mask in masks:
            rows.append(jnp.concatenate([qt[r : r + 32] * mask[0:32], zero], axis=1))
            rows.append(jnp.concatenate([zero, qt[r + 32 : r + 64] * mask[0:32]], axis=1))
        if windows == 3:
            rows.append(jnp.zeros((64, 256), BF16))
        s = dot(keys[pair], jnp.concatenate(rows, axis=0))
        p = softmax_columns(s * SCALE + bias_of(pair))
        seen = [
            jnp.concatenate([p[:, 0:128] * mask, p[:, 128:256] * mask], axis=1) for mask in masks
        ]
        if windows == 3:
            seen.append(jnp.zeros((64, 256), BF16))
        ct = dot(values[r : r + 64], jnp.concatenate(seen, axis=0))
        out += [ct[0:32, 0:128], ct[32:64, 128:256]]
    return jnp.concatenate(out, axis=0)


def finish(z, ctx, wo, gain, we, ws):
    branch = dot(ctx, wo, TN).astype(BF16)
    middle = z + branch.astype(F32)
    hidden = gelu(dot(layer_norm(middle, gain).astype(BF16), we)).astype(BF16)
    return middle + dot(hidden, ws)


def swap_halves(first, second):
    rows = first.shape[0]
    a = pltpu.roll(first.reshape(rows // 8, 8, 128), 4, 1)
    b = pltpu.roll(second.reshape(rows // 8, 8, 128), 4, 1)
    return jnp.where(iota(a.shape, 1) < 4, a, b).reshape(rows, 128)


def regular_kernel(
    x_ref, up_ref, down_ref, ag_ref, w_ref, wo_ref, pb_ref, hg_ref, we_ref, ws_ref,
    fa_ref, fb_ref, na_ref, nb_ref, sl_ref, sr_ref,
    bias, wqv, wk, xs,
):
    def store(head, yj, values):
        bias[yj * 8 : yj * 8 + 8, head * 128 : head * 128 + 128] = values

    fill_bias(pb_ref, 0, store)
    fill_weights(w_ref, 0, wqv, wk)
    xs[0:8] = up_ref[...]
    xs[8:72] = x_ref[...]
    xs[72:80] = down_ref[...]
    masks = lane_masks(64)
    wo = wo_ref[0]

    def step(w, carry):
        block = xs[pl.ds(w * 8, 8)].astype(F32).reshape(8, 2, 8, 128)
        z = jnp.concatenate([block[:, 0].reshape(64, 128), block[:, 1].reshape(64, 128)], axis=0)
        n = layer_norm(z, ag_ref[0:1, :]).astype(BF16)
        ctx = attention(
            n, [n[0:64], n[64:128]], masks, wqv, wk,
            lambda pair: bias[:, pair * 256 : pair * 256 + 256],
        )
        out = finish(z, ctx.astype(BF16), wo, hg_ref[0:1, :], we_ref[0], ws_ref[0])
        n1 = layer_norm(out, ag_ref[1:2, :])
        at = pl.multiple_of(w * 64, 64)
        fa_ref[pl.ds(at, 64), :] = swap_halves(out[0:64], out[64:128])
        fb_ref[pl.ds(at, 64), :] = swap_halves(out[64:128], out[0:64])
        na_ref[pl.ds(at, 64), :] = swap_halves(n1[0:64], n1[64:128]).astype(BF16)
        nb = swap_halves(n1[64:128], n1[0:64])
        nb_ref[pl.ds(at, 64), :] = nb.astype(BF16)
        pairs = nb.reshape(4, 2, 8, 128)
        even, odd = pairs[:, 0], pairs[:, 1]
        low = iota((4, 8, 128), 1) < 4
        half = pl.multiple_of(w * 32, 32)
        sr_ref[pl.ds(half, 32), :] = (
            jnp.where(low, even, pltpu.roll(odd, 4, 1)).reshape(32, 128).astype(BF16)
        )
        sl_ref[pl.ds(half, 32), :] = (
            jnp.where(low, pltpu.roll(even, 4, 1), odd).reshape(32, 128).astype(BF16)
        )
        return carry

    lax.fori_loop(0, 10, step, 0)


def shifted_kernel(
    flag_ref, fa_ref, fb_ref, na_ref, nb_ref, hl_ref, hr_ref,
    w_ref, wo_ref, pb_ref, hg_ref, we_ref, ws_ref,
    out_ref,
    bias, wqv, wk,
):
    sub = iota((8, 128), 0)
    lane = iota((8, 128), 1)
    last_col = jnp.where((lane & 7) < 4, flag_ref[3], flag_ref[2])
    cut_col = (lane >= 64) & (last_col > 0) & (((lane & 7) < 4) != (sub < 4))
    query_low = ((lane >> 3) & 7) < 4

    def store(head, yj, values):
        cut = values - 100.0 * LOG2E
        rows = slice(yj * 8, yj * 8 + 8)
        cols = slice(head * 128, head * 128 + 128)
        bias[0, rows, cols] = jnp.where(cut_col, cut, values)
        cut_row = jnp.logical_not(query_low) if yj < 4 else query_low
        bias[1, rows, cols] = jnp.where(cut_col | cut_row, cut, values)

    fill_bias(pb_ref, 1, store)
    fill_weights(w_ref, 1, wqv, wk)
    mask_a, _ = lane_masks(64)
    lanes = iota((64, 128), 1)
    mask_2 = jnp.where((lanes >= 64) & ((lanes & 7) < 4), 1.0, 0.0).astype(BF16)
    mask_0 = jnp.where((lanes >= 64) & ((lanes & 7) >= 4), 1.0, 0.0).astype(BF16)
    masks = [mask_a, mask_2, mask_0]
    wo = wo_ref[1]
    low = iota((8, 8, 128), 1) < 4
    low4 = iota((4, 8, 128), 1) < 4

    def attend(w, which):
        at = pl.multiple_of(w * 64 + 32, 32)
        half = pl.multiple_of(w * 32 + 16, 16)
        na = na_ref[pl.ds(at, 64), :]
        nb = nb_ref[pl.ds(at, 64), :]
        hl = hl_ref[pl.ds(half, 32), :].astype(F32).reshape(4, 8, 128)
        hr = hr_ref[pl.ds(half, 32), :].astype(F32).reshape(4, 8, 128)
        even = jnp.where(low4, hl, pltpu.roll(hr, 4, 1))
        odd = jnp.where(low4, pltpu.roll(hl, 4, 1), hr)
        halo = jnp.stack([even, odd], axis=1).reshape(8, 8, 128)
        own = nb.astype(F32).reshape(8, 8, 128)
        k2 = jnp.where(low, own, halo).reshape(64, 128).astype(BF16)
        k0 = jnp.where(low, halo, own).reshape(64, 128).astype(BF16)
        return attention(
            jnp.concatenate([na, nb], axis=0), [na, k2, k0], masks, wqv, wk,
            lambda pair: bias[which, :, pair * 256 : pair * 256 + 256],
        )

    def end(z, ctx):
        out = finish(z, ctx.astype(BF16), wo, hg_ref[1:2, :], we_ref[1], ws_ref[1])
        left = swap_halves(out[64:128], out[0:64]).reshape(8, 1, 8, 128)
        right = swap_halves(out[0:64], out[64:128]).reshape(8, 1, 8, 128)
        return jnp.concatenate([left, right], axis=1).reshape(8, 16, 128)

    def step(w, carry):
        at = pl.multiple_of(w * 64 + 32, 32)
        z = jnp.concatenate([fa_ref[pl.ds(at, 64), :], fb_ref[pl.ds(at, 64), :]], axis=0)
        out_ref[pl.ds(w * 8 - 4, 8)] = end(z, attend(w, 0))
        return carry

    lax.fori_loop(1, 8, step, 0)
    top = attend(0, flag_ref[0])
    bottom = attend(8, flag_ref[1])
    ctx = jnp.where(((iota((128, 128), 1) >> 3) & 7) < 4, bottom, top)
    z = jnp.concatenate(
        [fa_ref[544:576, :], fa_ref[64:96, :], fb_ref[544:576, :], fb_ref[64:96, :]], axis=0
    )
    ends = end(z, ctx)
    out_ref[60:64] = ends[0:4]
    out_ref[0:4] = ends[4:8]


def vmem():
    return pl.BlockSpec(memory_space=pltpu.VMEM)


def on_device(x, ag, tw, ow, pb, hg, ew, sw):
    height, breadth = x.shape[0], x.shape[1]
    up = from_behind(x[height - WIN :], "gy", 1)
    down = from_behind(x[:WIN], "gy", -1)
    tokens = (height + 2 * WIN) * WIN
    shape = jax.ShapeDtypeStruct
    fa, fb, na, nb, sl, sr = pl.pallas_call(
        regular_kernel,
        out_shape=[
            shape((tokens, C), F32),
            shape((tokens, C), F32),
            shape((tokens, C), BF16),
            shape((tokens, C), BF16),
            shape((tokens // 2, C), BF16),
            shape((tokens // 2, C), BF16),
        ],
        in_specs=[vmem()] * 10,
        out_specs=[vmem()] * 6,
        scratch_shapes=[
            pltpu.VMEM((64, HEADS * 128), F32),
            pltpu.VMEM((256, 128), BF16),
            pltpu.VMEM((256, 256), BF16),
            pltpu.VMEM((height + 2 * WIN, breadth, C), BF16),
        ],
        compiler_params=pltpu.CompilerParams(vmem_limit_bytes=32 * 1024 * 1024),
        name="regular",
    )(x, up, down, ag, tw, ow, pb, hg, ew, sw)
    hr = from_behind(sl, "gx", -1)
    hl = from_behind(sr, "gx", 1)
    row, col = lax.axis_index("gy"), lax.axis_index("gx")
    flags = jnp.stack(
        [row == 0, row == lax.axis_size("gy") - 1, col == 0, col == lax.axis_size("gx") - 1]
    ).astype(jnp.int32)
    return pl.pallas_call(
        shifted_kernel,
        out_shape=shape((height, breadth, C), F32),
        in_specs=[pl.BlockSpec(memory_space=pltpu.SMEM)] + [vmem()] * 12,
        out_specs=vmem(),
        scratch_shapes=[
            pltpu.VMEM((2, 64, HEADS * 128), F32),
            pltpu.VMEM((256, 128), BF16),
            pltpu.VMEM((256, 256), BF16),
        ],
        compiler_params=pltpu.CompilerParams(vmem_limit_bytes=32 * 1024 * 1024),
        name="shifted",
    )(flags, fa, fb, na, nb, hl, hr, tw, ow, pb, hg, ew, sw)


def solution(mesh):
    return jax.shard_map(
        on_device,
        mesh=mesh,
        in_specs=(P("gy", "gx", None), P(), P(), P(), P(), P(), P(), P()),
        out_specs=P("gy", "gx", None),
        check_vma=False,
    )
```

```python
import math

import jax
import jax.numpy as jnp
from jax import lax
from jax.experimental import pallas as pl
from jax.experimental.pallas import tpu as pltpu
from jax.sharding import PartitionSpec as P

C = 128
HEADS = 4
HID = 512
WIN = 8
HD = 32
SHIFT = 4
EPSILON = 1e-05
ROWS_1 = 10
ROWS_2 = 9
ROWS_3 = 8
LOG2E = math.log2(math.e)
SCALE = HD ** (-0.5) * LOG2E
F32 = jnp.float32
BF16 = jnp.bfloat16
NT = (((1,), (1,)), ((), ()))
TN = (((0,), (0,)), ((), ()))


def from_behind(x, axis, by):
    length = lax.axis_size(axis)
    return lax.ppermute(x, axis, [(i, (i + by) % length) for i in range(length)])


def iota(shape, dim):
    return lax.broadcasted_iota(jnp.int32, shape, dim)


def layer_norm(x, gain):
    center = x - jnp.mean(x, axis=-1, keepdims=True)
    spread = jnp.mean(center * center, axis=-1, keepdims=True)
    return center * lax.rsqrt(spread + EPSILON) * gain


def gelu(x):
    half = 0.5 * x
    return half + half * lax.erf(x * (0.5**0.5))


def fill_bias(pb_ref, block, store):
    sub = iota((8, 128), 0)
    lane = iota((8, 128), 1)
    place = lax.min((lane >> 3) * 15 + 7 + (lane & 7) - sub, 224)
    for head in range(HEADS):
        low = jnp.broadcast_to(pb_ref[block, head : head + 1, 0:128], (8, 128))
        high = jnp.broadcast_to(pb_ref[block, head : head + 1, 97:225], (8, 128))
        strip = jnp.where(
            place < 128,
            jnp.take_along_axis(low, lax.min(place, 127), axis=1),
            jnp.take_along_axis(high, lax.max(place - 97, 0), axis=1),
        )
        strip = strip * LOG2E
        for yj in range(8):
            turn = (128 - (7 - yj) * 8) % 128
            first = pltpu.roll(strip, turn, 1) if turn else strip
            second = pltpu.roll(strip, (turn + 64) % 128, 1)
            store(head, yj, jnp.where(lane < 64, first, second))


def lane_masks(rows):
    lane = iota((rows, 128), 1)
    left = jnp.where(lane < 64, 1.0, 0.0).astype(BF16)
    right = jnp.where(lane >= 64, 1.0, 0.0).astype(BF16)
    return left, right


def fill_weights(w_ref, block, wqv, wk):
    wqv[0:128, :] = jnp.transpose(w_ref[block, :, 0:128].astype(F32)).astype(BF16)
    wqv[128:256, :] = jnp.transpose(w_ref[block, :, 256:384].astype(F32)).astype(BF16)
    keys = w_ref[block, :, 128:256].astype(F32)
    turned = pltpu.roll(keys, 64, 1)
    lane = iota((128, 128), 1)
    zero = jnp.zeros((128, 128), F32)
    wk[0:128, 0:128] = jnp.where(lane < 64, keys, zero).astype(BF16)
    wk[0:128, 128:256] = jnp.where(lane < 64, turned, zero).astype(BF16)
    wk[128:256, 0:128] = jnp.where(lane >= 64, turned, zero).astype(BF16)
    wk[128:256, 128:256] = jnp.where(lane >= 64, keys, zero).astype(BF16)


def dot(a, b, dims=None):
    if dims is None:
        return jnp.dot(a, b, preferred_element_type=F32)
    return lax.dot_general(a, b, dims, preferred_element_type=F32)


def attention(query_tokens, key_tokens, masks, wqv, wk, bias_of):
    windows = len(key_tokens)
    qt = dot(wqv[0:128, :], query_tokens, NT).astype(BF16)
    if windows == 2:
        vt = dot(wqv[128:256, :], jnp.concatenate(key_tokens, axis=0), NT).astype(BF16)
        keys = dot(jnp.concatenate(key_tokens, axis=1), wk[...]).astype(BF16)
        keys = [keys[:, 0:128], keys[:, 128:256]]
        values = vt
    else:
        vt = dot(wqv[128:256, :], jnp.concatenate(key_tokens[0:2], axis=0), NT).astype(BF16)
        third = dot(
            wqv[128:256, :], jnp.concatenate([key_tokens[2], key_tokens[2]], axis=0), NT
        ).astype(BF16)
        values = jnp.concatenate([vt, third], axis=1)
        keys = dot(jnp.concatenate(key_tokens[0:2], axis=1), wk[...]).astype(BF16)
        last = dot(key_tokens[2], wk[0:128, :]).astype(BF16)
        keys = [
            jnp.concatenate([keys[:, 0:128], last[:, 0:128]], axis=1),
            jnp.concatenate([keys[:, 128:256], last[:, 128:256]], axis=1),
        ]
    yield
    zero = jnp.zeros((32, 128), BF16)
    scores = []
    for pair in range(2):
        r = 64 * pair
        rows = []
        for mask in masks:
            rows.append(jnp.concatenate([qt[r : r + 32] * mask[0:32], zero], axis=1))
            rows.append(jnp.concatenate([zero, qt[r + 32 : r + 64] * mask[0:32]], axis=1))
        if windows == 3:
            rows.append(jnp.zeros((64, 256), BF16))
        scores.append(dot(keys[pair], jnp.concatenate(rows, axis=0)))
    yield
    tops = []
    for pair in range(2):
        scores[pair] = scores[pair] * SCALE + bias_of(pair)
        tops.append(jnp.max(scores[pair], axis=0, keepdims=True))
    yield
    out = []
    for pair in range(2):
        r = 64 * pair
        p = jnp.exp2(scores[pair] - tops[pair])
        p = (p * (1.0 / jnp.sum(p, axis=0, keepdims=True))).astype(BF16)
        seen = [
            jnp.concatenate([p[:, 0:128] * mask, p[:, 128:256] * mask], axis=1) for mask in masks
        ]
        if windows == 3:
            seen.append(jnp.zeros((64, 256), BF16))
        ct = dot(values[r : r + 64], jnp.concatenate(seen, axis=0))
        out += [ct[0:32, 0:128], ct[32:64, 128:256]]
    yield
    return jnp.concatenate(out, axis=0).astype(BF16)


def finish(z, ctx, wo, gain, we, ws):
    branch = dot(ctx, wo, TN).astype(BF16)
    yield
    middle = z + branch.astype(F32)
    normed = layer_norm(middle, gain).astype(BF16)
    yield
    hidden = dot(normed, we)
    yield
    hidden = gelu(hidden).astype(BF16)
    yield
    out = middle + dot(hidden, ws)
    yield
    return out


def together(chains):
    results = [None] * len(chains)
    live = list(range(len(chains)))
    while live:
        for i in list(live):
            try:
                next(chains[i])
            except StopIteration as stop:
                results[i] = stop.value
                live.remove(i)
    return results


def swap_halves(first, second):
    rows = first.shape[0]
    a = pltpu.roll(first.reshape(rows // 8, 8, 128), 4, 1)
    b = pltpu.roll(second.reshape(rows // 8, 8, 128), 4, 1)
    return jnp.where(iota(a.shape, 1) < 4, a, b).reshape(rows, 128)


def regular_kernel(
    x_ref, up_ref, down_ref, ag_ref, w_ref, wo_ref, pb_ref, hg_ref, we_ref, ws_ref,
    fa_ref, fb_ref, na_ref, nb_ref, sl_ref, sr_ref,
    bias, wqv, wk, xs,
):
    def store(head, yj, values):
        bias[yj * 8 : yj * 8 + 8, head * 128 : head * 128 + 128] = values

    fill_bias(pb_ref, 0, store)
    fill_weights(w_ref, 0, wqv, wk)
    xs[0:8] = up_ref[...]
    xs[8:72] = x_ref[...]
    xs[72:80] = down_ref[...]
    masks = lane_masks(64)
    wo = wo_ref[0]

    def chain(w):
        block = xs[pl.ds(w * 8, 8)].astype(F32).reshape(8, 2, 8, 128)
        z = jnp.concatenate([block[:, 0].reshape(64, 128), block[:, 1].reshape(64, 128)], axis=0)
        n = layer_norm(z, ag_ref[0:1, :]).astype(BF16)
        yield
        ctx = yield from attention(
            n, [n[0:64], n[64:128]], masks, wqv, wk,
            lambda pair: bias[:, pair * 256 : pair * 256 + 256],
        )
        out = yield from finish(z, ctx, wo, hg_ref[0:1, :], we_ref[0], ws_ref[0])
        n1 = layer_norm(out, ag_ref[1:2, :])
        yield
        return out, n1

    def step(i, carry):
        rows = [i * ROWS_1 + u for u in range(ROWS_1)]
        for w, (out, n1) in zip(rows, together([chain(w) for w in rows])):
            save(w, out, n1)
        return carry

    def save(w, out, n1):
        at = pl.multiple_of(w * 64, 64)
        fa_ref[pl.ds(at, 64), :] = swap_halves(out[0:64], out[64:128])
        fb_ref[pl.ds(at, 64), :] = swap_halves(out[64:128], out[0:64])
        na_ref[pl.ds(at, 64), :] = swap_halves(n1[0:64], n1[64:128]).astype(BF16)
        nb = swap_halves(n1[64:128], n1[0:64])
        nb_ref[pl.ds(at, 64), :] = nb.astype(BF16)
        pairs = nb.reshape(4, 2, 8, 128)
        even, odd = pairs[:, 0], pairs[:, 1]
        low = iota((4, 8, 128), 1) < 4
        half = pl.multiple_of(w * 32, 32)
        sr_ref[pl.ds(half, 32), :] = (
            jnp.where(low, even, pltpu.roll(odd, 4, 1)).reshape(32, 128).astype(BF16)
        )
        sl_ref[pl.ds(half, 32), :] = (
            jnp.where(low, pltpu.roll(even, 4, 1), odd).reshape(32, 128).astype(BF16)
        )

    lax.fori_loop(0, 10 // ROWS_1, step, 0)


def shifted_kernel(
    flag_ref, fa_ref, fb_ref, na_ref, nb_ref, hl_ref, hr_ref,
    w_ref, wo_ref, pb_ref, hg_ref, we_ref, ws_ref,
    out_ref,
    bias, wqv, wk, context,
):
    sub = iota((8, 128), 0)
    lane = iota((8, 128), 1)
    last_col = jnp.where((lane & 7) < 4, flag_ref[3], flag_ref[2])
    cut_col = (lane >= 64) & (last_col > 0) & (((lane & 7) < 4) != (sub < 4))
    query_low = ((lane >> 3) & 7) < 4

    def store(head, yj, values):
        cut = values - 100.0 * LOG2E
        rows = slice(yj * 8, yj * 8 + 8)
        cols = slice(head * 128, head * 128 + 128)
        bias[0, rows, cols] = jnp.where(cut_col, cut, values)
        cut_row = jnp.logical_not(query_low) if yj < 4 else query_low
        bias[1, rows, cols] = jnp.where(cut_col | cut_row, cut, values)

    fill_bias(pb_ref, 1, store)
    fill_weights(w_ref, 1, wqv, wk)
    mask_a, _ = lane_masks(64)
    lanes = iota((64, 128), 1)
    mask_2 = jnp.where((lanes >= 64) & ((lanes & 7) < 4), 1.0, 0.0).astype(BF16)
    mask_0 = jnp.where((lanes >= 64) & ((lanes & 7) >= 4), 1.0, 0.0).astype(BF16)
    masks = [mask_a, mask_2, mask_0]
    wo = wo_ref[1]
    low = iota((8, 8, 128), 1) < 4
    low4 = iota((4, 8, 128), 1) < 4

    def attend(w, which):
        at = pl.multiple_of(w * 64 + 32, 32)
        half = pl.multiple_of(w * 32 + 16, 16)
        na = na_ref[pl.ds(at, 64), :]
        nb = nb_ref[pl.ds(at, 64), :]
        hl = hl_ref[pl.ds(half, 32), :].astype(F32).reshape(4, 8, 128)
        hr = hr_ref[pl.ds(half, 32), :].astype(F32).reshape(4, 8, 128)
        even = jnp.where(low4, hl, pltpu.roll(hr, 4, 1))
        odd = jnp.where(low4, pltpu.roll(hl, 4, 1), hr)
        halo = jnp.stack([even, odd], axis=1).reshape(8, 8, 128)
        own = nb.astype(F32).reshape(8, 8, 128)
        k2 = jnp.where(low, own, halo).reshape(64, 128).astype(BF16)
        k0 = jnp.where(low, halo, own).reshape(64, 128).astype(BF16)
        ctx = yield from attention(
            jnp.concatenate([na, nb], axis=0), [na, k2, k0], masks, wqv, wk,
            lambda pair: bias[which, :, pair * 256 : pair * 256 + 256],
        )

        return ctx

    def attend_step(i, carry):
        rows = [i * ROWS_2 + u for u in range(ROWS_2)]
        chains = []
        for w in rows:
            which = jnp.where(w == 0, flag_ref[0], jnp.where(w == 8, flag_ref[1], 0))
            chains.append(attend(w, which))
        for w, ctx in zip(rows, together(chains)):
            context[w] = ctx
        return carry

    lax.fori_loop(0, 9 // ROWS_2, attend_step, 0)
    swapped = ((iota((128, 128), 1) >> 3) & 7) < 4
    context[0] = jnp.where(swapped, context[8].astype(F32), context[0].astype(F32)).astype(BF16)

    def end(w):
        low = pl.multiple_of(jnp.where(w == 0, 544, w * 64 + 32), 32)
        high = pl.multiple_of(w * 64 + 64, 64)
        parts = [f[pl.ds(at, 32), :] for f in (fa_ref, fb_ref) for at in (low, high)]
        z = jnp.concatenate(parts, axis=0)
        out = yield from finish(z, context[w], wo, hg_ref[1:2, :], we_ref[1], ws_ref[1])
        left = swap_halves(out[64:128], out[0:64]).reshape(8, 1, 8, 128)
        right = swap_halves(out[0:64], out[64:128]).reshape(8, 1, 8, 128)
        return jnp.concatenate([left, right], axis=1).reshape(8, 16, 128)

    def end_step(i, carry):
        rows = [i * ROWS_3 + u for u in range(ROWS_3)]
        for w, out in zip(rows, together([end(w) for w in rows])):
            out_ref[pl.ds(jnp.where(w == 0, 60, w * 8 - 4), 4)] = out[0:4]
            out_ref[pl.ds(w * 8, 4)] = out[4:8]
        return carry

    lax.fori_loop(0, 8 // ROWS_3, end_step, 0)


def vmem():
    return pl.BlockSpec(memory_space=pltpu.VMEM)


def on_device(x, ag, tw, ow, pb, hg, ew, sw):
    height, breadth = x.shape[0], x.shape[1]
    up = from_behind(x[height - WIN :], "gy", 1)
    down = from_behind(x[:WIN], "gy", -1)
    tokens = (height + 2 * WIN) * WIN
    shape = jax.ShapeDtypeStruct
    fa, fb, na, nb, sl, sr = pl.pallas_call(
        regular_kernel,
        out_shape=[
            shape((tokens, C), F32),
            shape((tokens, C), F32),
            shape((tokens, C), BF16),
            shape((tokens, C), BF16),
            shape((tokens // 2, C), BF16),
            shape((tokens // 2, C), BF16),
        ],
        in_specs=[vmem()] * 10,
        out_specs=[vmem()] * 6,
        scratch_shapes=[
            pltpu.VMEM((64, HEADS * 128), F32),
            pltpu.VMEM((256, 128), BF16),
            pltpu.VMEM((256, 256), BF16),
            pltpu.VMEM((height + 2 * WIN, breadth, C), BF16),
        ],
        compiler_params=pltpu.CompilerParams(vmem_limit_bytes=32 * 1024 * 1024),
        name="regular",
    )(x, up, down, ag, tw, ow, pb, hg, ew, sw)
    hr = from_behind(sl, "gx", -1)
    hl = from_behind(sr, "gx", 1)
    row, col = lax.axis_index("gy"), lax.axis_index("gx")
    flags = jnp.stack(
        [row == 0, row == lax.axis_size("gy") - 1, col == 0, col == lax.axis_size("gx") - 1]
    ).astype(jnp.int32)
    return pl.pallas_call(
        shifted_kernel,
        out_shape=shape((height, breadth, C), F32),
        in_specs=[pl.BlockSpec(memory_space=pltpu.SMEM)] + [vmem()] * 12,
        out_specs=vmem(),
        scratch_shapes=[
            pltpu.VMEM((2, 64, HEADS * 128), F32),
            pltpu.VMEM((256, 128), BF16),
            pltpu.VMEM((256, 256), BF16),
            pltpu.VMEM((9, 128, 128), BF16),
        ],
        compiler_params=pltpu.CompilerParams(vmem_limit_bytes=32 * 1024 * 1024),
        name="shifted",
    )(flags, fa, fb, na, nb, hl, hr, tw, ow, pb, hg, ew, sw)


def solution(mesh):
    return jax.shard_map(
        on_device,
        mesh=mesh,
        in_specs=(P("gy", "gx", None), P(), P(), P(), P(), P(), P(), P()),
        out_specs=P("gy", "gx", None),
        check_vma=False,
    )
```

```python
import math

import jax
import jax.numpy as jnp
from jax import lax
from jax.experimental import pallas as pl
from jax.experimental.pallas import tpu as pltpu
from jax.sharding import PartitionSpec as P

C = 128
HEADS = 4
HID = 512
WIN = 8
HD = 32
EPSILON = 1e-05
LOG2E = math.log2(math.e)
SCALE = HD ** (-0.5) * LOG2E
F32 = jnp.float32
BF16 = jnp.bfloat16
NT = (((1,), (1,)), ((), ()))
TN = (((0,), (0,)), ((), ()))
CHUNK = 256
EDGE_ROOM = 32 * 1024


def from_behind(x, axis, by):
    length = lax.axis_size(axis)
    return lax.ppermute(x, axis, [(i, (i + by) % length) for i in range(length)])


def iota(shape, dim):
    return lax.broadcasted_iota(jnp.int32, shape, dim)


def dot(a, b, dims=None):
    if dims is None:
        return jnp.dot(a, b, preferred_element_type=F32)
    return lax.dot_general(a, b, dims, preferred_element_type=F32)


def cat(parts, axis=0):
    return jnp.concatenate(parts, axis=axis)


def layer_norm(x, gain):
    center = x - jnp.mean(x, axis=-1, keepdims=True)
    spread = jnp.sum(center * center, axis=-1, keepdims=True)
    return center * lax.rsqrt(spread + C * EPSILON) * (gain * C**0.5)


def twice_gelu(x):
    return x + x * lax.erf(x * (0.5**0.5))


def bias_rows(pb_ref, block):
    sub = iota((8, 128), 0)
    lane = iota((8, 128), 1)
    place = lax.min((lane >> 3) * 15 + 7 + (lane & 7) - sub, 224)
    for head in range(HEADS):
        low = jnp.broadcast_to(pb_ref[block, head : head + 1, 0:128], (8, 128))
        high = jnp.broadcast_to(pb_ref[block, head : head + 1, 97:225], (8, 128))
        strip = jnp.where(
            place < 128,
            jnp.take_along_axis(low, lax.min(place, 127), axis=1),
            jnp.take_along_axis(high, lax.max(place - 97, 0), axis=1),
        )
        strip = strip * LOG2E
        for yj in range(8):
            turn = (128 - (7 - yj) * 8) % 128
            first = pltpu.roll(strip, turn, 1) if turn else strip
            second = pltpu.roll(strip, (turn + 64) % 128, 1)
            yield head, yj, jnp.where(lane < 64, first, second)


def fill_weights(w, wqv, wk):
    wqv[0:128, :] = jnp.transpose(w[:, 0:128].astype(F32)).astype(BF16)
    wqv[128:256, :] = jnp.transpose(w[:, 256:384].astype(F32)).astype(BF16)
    keys = w[:, 128:256].astype(F32)
    turned = pltpu.roll(keys, 64, 1)
    lane = iota((128, 128), 1)
    zero = jnp.zeros((128, 128), F32)
    wk[0:128, 0:128] = jnp.where(lane < 64, keys, zero).astype(BF16)
    wk[0:128, 128:256] = jnp.where(lane < 64, turned, zero).astype(BF16)
    wk[128:256, 0:128] = jnp.where(lane >= 64, turned, zero).astype(BF16)
    wk[128:256, 128:256] = jnp.where(lane >= 64, keys, zero).astype(BF16)


def mask(*conditions):
    lane = iota((64, 128), 1)
    sides = {"1": lane < 64, "2": lane >= 64, "up": (lane & 32) == 0, "down": (lane & 32) > 0}
    sides |= {"left": (lane & 4) == 0, "right": (lane & 4) > 0}
    keep = sides[conditions[0]]
    for name in conditions[1:]:
        keep = keep & sides[name]
    return jnp.where(keep, 1.0, 0.0).astype(BF16)


def side_by_side(tokens, wk):
    pairs = tokens.reshape(-1, 2, 64, 128)
    lanes = cat([cat([pairs[p, 0], pairs[p, 1]], 1) for p in range(pairs.shape[0])])
    return dot(lanes, wk).astype(BF16)


def attention(queries, keys, values, units):
    zero = jnp.zeros((32, 128), BF16)
    scores = []
    for u, (pairs, masks, bias) in enumerate(units):
        q = queries[:, 128 * u : 128 * u + 128]
        for half in range(2):
            r = 64 * half
            rows = []
            for m in masks:
                rows.append(cat([q[r : r + 32] * m[0:32], zero], 1))
                rows.append(cat([zero, q[r + 32 : r + 64] * m[0:32]], 1))
            k = cat([keys[64 * p : 64 * p + 64, 128 * half : 128 * half + 128] for p in pairs], 1)
            scores.append(dot(k, cat(rows)))
    for u, (pairs, masks, bias) in enumerate(units):
        for half in range(2):
            s = scores[2 * u + half] * SCALE + bias[:, 256 * half : 256 * half + 256]
            p = jnp.exp2(s - jnp.max(s, axis=0, keepdims=True))
            part = 1.0 / jnp.sum(p, axis=0, keepdims=True)
            scores[2 * u + half] = (p * part).astype(BF16)
    context = []
    for u, (pairs, masks, bias) in enumerate(units):
        out = []
        for half in range(2):
            r = 64 * half
            p = scores[2 * u + half]
            seen = cat([cat([p[:, 0:128] * m, p[:, 128:256] * m], 1) for m in masks])
            v = cat([values[r : r + 64, 128 * j : 128 * j + 128] for j in pairs], 1)
            ct = dot(v, seen)
            out += [ct[0:32, 0:128], ct[32:64, 128:256]]
        context.append(cat(out).astype(BF16))
    return cat(context, 1)


def finish(z, context, wo, gain, we, ws):
    middle = z + dot(context, wo, TN).astype(BF16).astype(F32)
    normed = layer_norm(middle, gain).astype(BF16)
    size = min(CHUNK, z.shape[0])
    hidden = [dot(normed[i : i + size], we) for i in range(0, z.shape[0], size)]
    hidden = [twice_gelu(h).astype(BF16) for h in hidden]
    return middle + 0.5 * cat([dot(h, ws) for h in hidden])


def half_turn(x):
    return pltpu.roll(x.reshape(-1, 8, 128), 4, 1)


def low_half(shape):
    return iota(shape, 1) < 4


def windows_of(block):
    parts = block.astype(F32).reshape(8, 2, 8, 128)
    return [parts[:, 0].reshape(64, 128), parts[:, 1].reshape(64, 128)]


def shifted_columns(tokens):
    pairs = tokens.reshape(-1, 2, 64, 128)
    a, b = half_turn(pairs[:, 0]), half_turn(pairs[:, 1])
    low = low_half(a.shape)
    return jnp.where(low, a, b).reshape(-1, 128), jnp.where(low, b, a).reshape(-1, 128)


def edges(outer):
    pairs = outer.reshape(-1, 2, 8, 128)
    even, odd = pairs[:, 0], pairs[:, 1]
    low = low_half(even.shape)
    right = jnp.where(low, even, pltpu.roll(odd, 4, 1)).reshape(-1, 128)
    left = jnp.where(low, pltpu.roll(even, 4, 1), odd).reshape(-1, 128)
    return right.astype(BF16), left.astype(BF16)


def edge_rows_kernel(x_ref, first_ref, last_ref, sems):
    height = x_ref.shape[0]
    copies = [
        pltpu.make_async_copy(x_ref.at[pl.ds(0, WIN)], first_ref, sems.at[0]),
        pltpu.make_async_copy(x_ref.at[pl.ds(height - WIN, WIN)], last_ref, sems.at[1]),
    ]
    for copy in copies:
        copy.start()
    for copy in copies:
        copy.wait()


def own_kernel(
    x_hbm, w_hbm, wo_hbm, we_hbm, ws_hbm, ag_ref, pb_ref, hg_ref,
    fa_ref, fb_ref, na_ref, nb_ref, right_ref, left_ref, bias_ref, wqv_ref, wk_ref, w_ref, wo_ref, we_ref, ws_ref,
    x_ref, sems,
):
    copies = [
        pltpu.make_async_copy(a, b, sems.at[i])
        for i, (a, b) in enumerate(
            [(w_hbm, w_ref), (x_hbm, x_ref), (wo_hbm, wo_ref), (we_hbm, we_ref), (ws_hbm, ws_ref)]
        )
    ]
    for copy in copies:
        copy.start()
    for head, yj, values in bias_rows(pb_ref, 0):
        bias_ref[yj * 8 : yj * 8 + 8, head * 128 : head * 128 + 128] = values
    copies[0].wait()
    fill_weights(w_ref[0], wqv_ref, wk_ref)
    copies[1].wait()
    bands = x_ref.shape[0] // WIN
    z = cat([t for b in range(bands) for t in windows_of(x_ref[WIN * b : WIN * b + WIN])])
    normed = layer_norm(z, ag_ref[0:1, :]).astype(BF16)
    qv = dot(wqv_ref[...], normed, NT).astype(BF16)
    keys = side_by_side(normed, wk_ref[...])
    masks = [mask("1"), mask("2")]
    units = [([b], masks, bias_ref[...]) for b in range(bands)]
    context = attention(qv[0:128], keys, qv[128:256], units)
    for copy in copies[2:]:
        copy.wait()
    out = finish(z, context, wo_ref[0], hg_ref[0:1, :], we_ref[0], ws_ref[0])
    fa_ref[...], fb_ref[...] = shifted_columns(out)
    na, nb = shifted_columns(layer_norm(out, ag_ref[1:2, :]))
    na_ref[...] = na.astype(BF16)
    nb_ref[...] = nb.astype(BF16)
    right_ref[...], left_ref[...] = edges(nb)


def halo_kernel(
    up_ref, down_ref, own_right_ref, own_left_ref, bias_ref, wqv_ref, wk_ref, wo_ref, we_ref, ws_ref, ag_ref, hg_ref,
    na_ref, nb_ref, right_ref, left_ref,
):
    z = cat(windows_of(down_ref[...]) + windows_of(up_ref[...]))
    normed = layer_norm(z, ag_ref[0:1, :]).astype(BF16)
    keys = side_by_side(normed, wk_ref[...])
    values = dot(wqv_ref[128:256, :], normed, NT).astype(BF16)

    def wanted(t):
        return cat([t[0:32], t[160:192], t[64:96], t[224:256]])

    queries = dot(wqv_ref[0:128, :], wanted(normed), NT).astype(BF16)
    masks = [mask("1", "up"), mask("2", "up"), mask("1", "down"), mask("2", "down")]
    context = attention(queries, keys, values, [([0, 1], masks, bias_ref[...])])
    out = finish(wanted(z), context, wo_ref[0], hg_ref[0:1, :], we_ref[0], ws_ref[0])
    na, nb = shifted_columns(layer_norm(out, ag_ref[1:2, :]))
    na_ref[...] = na.astype(BF16)
    nb_ref[...] = nb.astype(BF16)
    right, left = edges(nb)
    n = own_right_ref.shape[0]
    right_ref[0:n, :] = own_right_ref[...]
    left_ref[0:n, :] = own_left_ref[...]
    right_ref[n : n + 32, :] = right
    left_ref[n : n + 32, :] = left


def middle_kernel(
    flag_ref, fa_ref, na_ref, va_ref, pb_ref, w_ref, wo_ref, we_ref, ws_ref, hg_ref,
    out_ref, bias_b, bias_bv, wqv_ref, wk_ref,
    bias_a, bias_av,
):
    sub = iota((8, 128), 0)
    lane = iota((8, 128), 1)
    query_left = (lane & 4) == 0
    query_up = (lane & 32) == 0
    last_col = jnp.where(query_left, flag_ref[3], flag_ref[2]) > 0
    last_row = jnp.where(query_up, flag_ref[1], flag_ref[0]) > 0
    cut_col = last_col & (query_left != (sub < 4))
    for head, yj, values in bias_rows(pb_ref, 1):
        at = (slice(yj * 8, yj * 8 + 8), slice(head * 128, head * 128 + 128))
        cut = values - 100.0 * LOG2E
        cut_row = (lane >= 64) & last_row & (jnp.logical_not(query_up) if yj < 4 else query_up)
        bias_a[at] = values
        bias_av[at] = jnp.where(cut_row, cut, values)
        bias_b[at] = jnp.where(cut_col, cut, values)
        bias_bv[at] = jnp.where(cut_row | cut_col, cut, values)
    fill_weights(w_ref[1], wqv_ref, wk_ref)
    n = na_ref.shape[0]
    inner = na_ref[32 : n - 32, :]
    first = cat([va_ref[32:64, :], na_ref[0:32, :]])
    last = cat([na_ref[n - 32 : n, :], va_ref[0:32, :]])
    looked_at = cat([inner, last, first, first])
    keys = side_by_side(looked_at, wk_ref[...])
    values = dot(wqv_ref[128:256, :], looked_at, NT).astype(BF16)
    wanted = cat([na_ref[32:n, :], na_ref[0:32, :]])
    queries = dot(wqv_ref[0:128, :], wanted, NT).astype(BF16)
    last_unit = n // 128 - 1
    masks = [mask("1"), mask("2")]
    units = [([u], masks, bias_a[...]) for u in range(last_unit)]
    masks = [mask("1"), mask("2", "up"), mask("2", "down"), jnp.zeros((64, 128), BF16)]
    units.append(([last_unit, last_unit + 1], masks, bias_av[...]))
    context = attention(queries, keys, values, units)
    z = cat([fa_ref[32:n, :], fa_ref[0:32, :]])
    out = finish(z, context, wo_ref[1], hg_ref[1:2, :], we_ref[1], ws_ref[1])
    out = half_turn(out).reshape(n, 128)
    out_ref[32:n, :] = out[0 : n - 32]
    out_ref[0:32, :] = out[n - 32 : n]


def outer_kernel(
    fb_ref, nb_ref, vb_ref, hl_ref, hr_ref, oa_ref, bias_b, bias_bv, wqv_ref, wk_ref, wo_ref, we_ref, ws_ref, hg_ref,
    out_ref,
):
    n = nb_ref.shape[0]
    h = n // 2

    def in_order(ref, end, size):
        rows = cat([ref[end + size : end + 2 * size, :], ref[0:end, :], ref[end : end + size, :]])
        return rows.astype(F32).reshape(-1, 8, 128)

    own = cat([vb_ref[32:64, :], nb_ref[...], vb_ref[0:32, :]]).astype(F32).reshape(-1, 8, 128)
    hl, hr = in_order(hl_ref, h, 16), in_order(hr_ref, h, 16)
    low = low_half(hl.shape)
    even = jnp.where(low, hl, pltpu.roll(hr, 4, 1))
    odd = jnp.where(low, pltpu.roll(hl, 4, 1), hr)
    halo = jnp.stack([even, odd], axis=1).reshape(own.shape)
    low = low_half(own.shape)
    right = jnp.where(low, own, halo).reshape(-1, 64, 128).astype(BF16)
    left = jnp.where(low, halo, own).reshape(-1, 64, 128).astype(BF16)
    count = right.shape[0]
    looked_at = cat([t for w in range(count) for t in (right[w], left[w])])
    keys = side_by_side(looked_at, wk_ref[...])
    values = dot(wqv_ref[128:256, :], looked_at, NT).astype(BF16)
    wanted = cat([nb_ref[32:n, :], nb_ref[0:32, :]])
    queries = dot(wqv_ref[0:128, :], wanted, NT).astype(BF16)
    masks = [mask(w, s) for w in "12" for s in ("left", "right")]
    units = [([w, w + 1], masks, bias_b[...]) for w in range(1, count - 2, 2)]
    masks = masks[0:2] + [mask("2", v, s) for v in ("up", "down") for s in ("left", "right")]
    units.append(([count - 2, count - 1, 0], masks, bias_bv[...]))
    context = attention(queries, keys, values, units)
    z = cat([fb_ref[32:n, :], fb_ref[0:32, :]])
    out = finish(z, context, wo_ref[1], hg_ref[1:2, :], we_ref[1], ws_ref[1])
    out = half_turn(out)
    rows = n // 8
    out = cat([out[rows - 4 :], out[: rows - 4]])
    inner = oa_ref[...].reshape(rows, 8, 128)
    low = low_half(out.shape)
    out_ref[:, 0:8, :] = jnp.where(low, out, inner)
    out_ref[:, 8:16, :] = jnp.where(low, inner, out)


def vmem(count):
    return [pl.BlockSpec(memory_space=pltpu.VMEM)] * count


def call(kernel, name, operands, specs, outs, scratch=(), flops=0, room=32 * 1024):
    shapes = [jax.ShapeDtypeStruct(shape, dtype) for shape, dtype in outs]
    return pl.pallas_call(
        kernel,
        out_shape=shapes,
        in_specs=specs,
        out_specs=vmem(len(outs)),
        scratch_shapes=list(scratch),
        compiler_params=pltpu.CompilerParams(vmem_limit_bytes=room * 1024),
        cost_estimate=pl.CostEstimate(flops=flops, bytes_accessed=1 << 20, transcendentals=0),
        name=name,
    )(*operands)


def on_device(x, ag, tw, ow, pb, hg, ew, sw):
    height, breadth = x.shape[0], x.shape[1]
    n = height * WIN
    hbm = [pl.BlockSpec(memory_space=pltpu.HBM)]
    first, last = call(
        edge_rows_kernel, "edge_rows", (x,), hbm,
        [((WIN, breadth, C), BF16)] * 2, [pltpu.SemaphoreType.DMA((2,))], 4 * 10**10, EDGE_ROOM,
    )
    up = from_behind(last, "gy", 1)
    down = from_behind(first, "gy", -1)
    table = ((64, HEADS * 128), F32)
    prepared = [((256, 128), BF16), ((256, 256), BF16)]
    fa, fb, na, nb, right, left, bias, wqv, wk, w, wo, we, ws = call(
        own_kernel, "own", (x, tw, ow, ew, sw, ag, pb, hg), hbm * 5 + vmem(3),
        [((n, C), F32)] * 2 + [((n, C), BF16)] * 2 + [((n // 2, C), BF16)] * 2 + [table] + prepared
        + [(tw.shape, BF16), (ow.shape, BF16), (ew.shape, BF16), (sw.shape, BF16)],
        [pltpu.VMEM(x.shape, BF16), pltpu.SemaphoreType.DMA((5,))], 4 * 10**9,
    )
    va, vb, right, left = call(
        halo_kernel, "halo", (up, down, right, left, bias, wqv, wk, wo, we, ws, ag, hg), vmem(12),
        [((64, C), BF16)] * 2 + [((n // 2 + 32, C), BF16)] * 2, (), 10**9,
    )
    hr = from_behind(left, "gx", -1)
    hl = from_behind(right, "gx", 1)
    row, col = lax.axis_index("gy"), lax.axis_index("gx")
    flags = jnp.stack(
        [row == 0, row == lax.axis_size("gy") - 1, col == 0, col == lax.axis_size("gx") - 1]
    ).astype(jnp.int32)
    oa, bias_b, bias_bv, wqv, wk = call(
        middle_kernel, "middle", (flags, fa, na, va, pb, w, wo, we, ws, hg),
        [pl.BlockSpec(memory_space=pltpu.SMEM)] + vmem(9),
        [((n, C), F32), table, table] + prepared,
        [pltpu.VMEM(*table)] * 2, 2 * 10**9,
    )
    return call(
        outer_kernel, "outer", (fb, nb, vb, hl, hr, oa, bias_b, bias_bv, wqv, wk, wo, we, ws, hg), vmem(14),
        [((height, breadth, C), F32)], (), 2 * 10**9,
    )[0]


def solution(mesh):
    return jax.shard_map(
        on_device,
        mesh=mesh,
        in_specs=(P("gy", "gx", None), P(), P(), P(), P(), P(), P(), P()),
        out_specs=P("gy", "gx", None),
        check_vma=False,
    )
```

```python
import math

import jax
import jax.numpy as jnp
from jax import lax
from jax.experimental import pallas as pl
from jax.experimental.pallas import tpu as pltpu
from jax.sharding import PartitionSpec as P

C = 128
HEADS = 4
HID = 512
WIN = 8
HD = 32
EPSILON = 1e-05
LOG2E = math.log2(math.e)
SCALE = HD ** (-0.5) * LOG2E
F32 = jnp.float32
BF16 = jnp.bfloat16
NT = (((1,), (1,)), ((), ()))
TN = (((0,), (0,)), ((), ()))
CHUNK = 256


def swap(x, axis, first):
    length = lax.axis_size(axis)
    there = [(i, (i + 1) % length) for i in range(first, length, 2)]
    return lax.ppermute(x, axis, there + [(b, a) for a, b in there])


def iota(shape, dim):
    return lax.broadcasted_iota(jnp.int32, shape, dim)


def dot(a, b, dims=None):
    if dims is None:
        return jnp.dot(a, b, preferred_element_type=F32)
    return lax.dot_general(a, b, dims, preferred_element_type=F32)


def cat(parts, axis=0):
    return jnp.concatenate(parts, axis=axis)


def layer_norm(x, gain):
    center = x - jnp.mean(x, axis=-1, keepdims=True)
    spread = jnp.sum(center * center, axis=-1, keepdims=True)
    return center * lax.rsqrt(spread + C * EPSILON) * (gain * C**0.5)


def twice_gelu(x):
    return x + x * lax.erf(x * (0.5**0.5))


def bias_rows(pb_ref, block):
    sub = iota((8, 128), 0)
    lane = iota((8, 128), 1)
    place = lax.min((lane >> 3) * 15 + 7 + (lane & 7) - sub, 224)
    for head in range(HEADS):
        low = jnp.broadcast_to(pb_ref[block, head : head + 1, 0:128], (8, 128))
        high = jnp.broadcast_to(pb_ref[block, head : head + 1, 97:225], (8, 128))
        strip = jnp.where(
            place < 128,
            jnp.take_along_axis(low, lax.min(place, 127), axis=1),
            jnp.take_along_axis(high, lax.max(place - 97, 0), axis=1),
        )
        strip = strip * LOG2E
        for yj in range(8):
            turn = (128 - (7 - yj) * 8) % 128
            first = pltpu.roll(strip, turn, 1) if turn else strip
            second = pltpu.roll(strip, (turn + 64) % 128, 1)
            yield head, yj, jnp.where(lane < 64, first, second)


def fill_weights(w, wqv, wk):
    wqv[0:128, :] = jnp.transpose(w[:, 0:128].astype(F32)).astype(BF16)
    wqv[128:256, :] = jnp.transpose(w[:, 256:384].astype(F32)).astype(BF16)
    keys = w[:, 128:256].astype(F32)
    turned = pltpu.roll(keys, 64, 1)
    lane = iota((128, 128), 1)
    zero = jnp.zeros((128, 128), F32)
    wk[0:128, 0:128] = jnp.where(lane < 64, keys, zero).astype(BF16)
    wk[0:128, 128:256] = jnp.where(lane < 64, turned, zero).astype(BF16)
    wk[128:256, 0:128] = jnp.where(lane >= 64, turned, zero).astype(BF16)
    wk[128:256, 128:256] = jnp.where(lane >= 64, keys, zero).astype(BF16)


def mask(*conditions):
    lane = iota((64, 128), 1)
    sides = {"1": lane < 64, "2": lane >= 64, "up": (lane & 32) == 0, "down": (lane & 32) > 0}
    sides |= {"left": (lane & 4) == 0, "right": (lane & 4) > 0}
    keep = sides[conditions[0]]
    for name in conditions[1:]:
        keep = keep & sides[name]
    return jnp.where(keep, 1.0, 0.0).astype(BF16)


def side_by_side(tokens, wk):
    pairs = tokens.reshape(-1, 2, 64, 128)
    lanes = cat([cat([pairs[p, 0], pairs[p, 1]], 1) for p in range(pairs.shape[0])])
    return dot(lanes, wk).astype(BF16)


def attention(queries, keys, values, units):
    zero = jnp.zeros((32, 128), BF16)
    scores = []
    for u, (pairs, masks, bias) in enumerate(units):
        q = queries[:, 128 * u : 128 * u + 128]
        for half in range(2):
            r = 64 * half
            rows = []
            for m in masks:
                rows.append(cat([q[r : r + 32] * m[0:32], zero], 1))
                rows.append(cat([zero, q[r + 32 : r + 64] * m[0:32]], 1))
            k = cat([keys[64 * p : 64 * p + 64, 128 * half : 128 * half + 128] for p in pairs], 1)
            scores.append(dot(k, cat(rows)))
    for u, (pairs, masks, bias) in enumerate(units):
        for half in range(2):
            s = scores[2 * u + half] * SCALE + bias[:, 256 * half : 256 * half + 256]
            p = jnp.exp2(s - jnp.max(s, axis=0, keepdims=True))
            part = 1.0 / jnp.sum(p, axis=0, keepdims=True)
            scores[2 * u + half] = (p * part).astype(BF16)
    context = []
    for u, (pairs, masks, bias) in enumerate(units):
        out = []
        for half in range(2):
            r = 64 * half
            p = scores[2 * u + half]
            seen = cat([cat([p[:, 0:128] * m, p[:, 128:256] * m], 1) for m in masks])
            v = cat([values[r : r + 64, 128 * j : 128 * j + 128] for j in pairs], 1)
            ct = dot(v, seen)
            out += [ct[0:32, 0:128], ct[32:64, 128:256]]
        context.append(cat(out).astype(BF16))
    return cat(context, 1)


def finish(z, context, wo, gain, we, ws):
    middle = z + dot(context, wo, TN).astype(BF16).astype(F32)
    normed = layer_norm(middle, gain).astype(BF16)
    size = min(CHUNK, z.shape[0])
    hidden = [dot(normed[i : i + size], we) for i in range(0, z.shape[0], size)]
    hidden = [twice_gelu(h).astype(BF16) for h in hidden]
    return middle + 0.5 * cat([dot(h, ws) for h in hidden])


def half_turn(x):
    return pltpu.roll(x.reshape(-1, 8, 128), 4, 1)


def low_half(shape):
    return iota(shape, 1) < 4


def windows_of(block):
    parts = block.astype(F32).reshape(8, 2, 8, 128)
    return [parts[:, 0].reshape(64, 128), parts[:, 1].reshape(64, 128)]


def shifted_columns(tokens):
    pairs = tokens.reshape(-1, 2, 64, 128)
    a, b = half_turn(pairs[:, 0]), half_turn(pairs[:, 1])
    low = low_half(a.shape)
    return jnp.where(low, a, b).reshape(-1, 128), jnp.where(low, b, a).reshape(-1, 128)


def edges(outer):
    pairs = outer.reshape(-1, 2, 8, 128)
    even, odd = pairs[:, 0], pairs[:, 1]
    low = low_half(even.shape)
    right = jnp.where(low, even, pltpu.roll(odd, 4, 1)).reshape(-1, 128)
    left = jnp.where(low, pltpu.roll(even, 4, 1), odd).reshape(-1, 128)
    return right.astype(BF16), left.astype(BF16)


def edge_rows_kernel(x_ref, odd_ref, even_ref, sems):
    bottom = x_ref.shape[0] - WIN
    is_odd = lax.rem(lax.axis_index("gy"), 2)
    copies = [
        pltpu.make_async_copy(x_ref.at[pl.ds(is_odd * bottom, WIN)], odd_ref, sems.at[0]),
        pltpu.make_async_copy(x_ref.at[pl.ds((1 - is_odd) * bottom, WIN)], even_ref, sems.at[1]),
    ]
    for copy in copies:
        copy.start()
    for copy in copies:
        copy.wait()


def own_kernel(
    x_hbm, w_hbm, wo_hbm, we_hbm, ws_hbm, ag_ref, pb_ref, hg_ref,
    fa_ref, fb_ref, na_ref, nb_ref, right_ref, left_ref, bias_ref, wqv_ref, wk_ref, w_ref, wo_ref, we_ref, ws_ref,
    x_ref, sems,
):
    copies = [
        pltpu.make_async_copy(a, b, sems.at[i])
        for i, (a, b) in enumerate(
            [(w_hbm, w_ref), (x_hbm, x_ref), (wo_hbm, wo_ref), (we_hbm, we_ref), (ws_hbm, ws_ref)]
        )
    ]
    for copy in copies:
        copy.start()
    for head, yj, values in bias_rows(pb_ref, 0):
        bias_ref[yj * 8 : yj * 8 + 8, head * 128 : head * 128 + 128] = values
    copies[0].wait()
    fill_weights(w_ref[0], wqv_ref, wk_ref)
    copies[1].wait()
    bands = x_ref.shape[0] // WIN
    z = cat([t for b in range(bands) for t in windows_of(x_ref[WIN * b : WIN * b + WIN])])
    normed = layer_norm(z, ag_ref[0:1, :]).astype(BF16)
    qv = dot(wqv_ref[...], normed, NT).astype(BF16)
    keys = side_by_side(normed, wk_ref[...])
    masks = [mask("1"), mask("2")]
    units = [([b], masks, bias_ref[...]) for b in range(bands)]
    context = attention(qv[0:128], keys, qv[128:256], units)
    for copy in copies[2:]:
        copy.wait()
    out = finish(z, context, wo_ref[0], hg_ref[0:1, :], we_ref[0], ws_ref[0])
    fa_ref[...], fb_ref[...] = shifted_columns(out)
    na, nb = shifted_columns(layer_norm(out, ag_ref[1:2, :]))
    na_ref[...] = na.astype(BF16)
    nb_ref[...] = nb.astype(BF16)
    right_ref[...], left_ref[...] = edges(nb)


def halo_kernel(
    rows_odd_ref, rows_even_ref, own_right_ref, own_left_ref, bias_ref, wqv_ref, wk_ref, wo_ref, we_ref, ws_ref, ag_ref, hg_ref,
    na_ref, nb_ref, cols_odd_ref, cols_even_ref,
):
    row_odd = lax.rem(lax.axis_index("gy"), 2) == 1
    rows_odd, rows_even = rows_odd_ref[...].astype(F32), rows_even_ref[...].astype(F32)
    down = jnp.where(row_odd, rows_odd, rows_even)
    up = jnp.where(row_odd, rows_even, rows_odd)
    z = cat(windows_of(down) + windows_of(up))
    normed = layer_norm(z, ag_ref[0:1, :]).astype(BF16)
    keys = side_by_side(normed, wk_ref[...])
    values = dot(wqv_ref[128:256, :], normed, NT).astype(BF16)

    def wanted(t):
        return cat([t[0:32], t[160:192], t[64:96], t[224:256]])

    queries = dot(wqv_ref[0:128, :], wanted(normed), NT).astype(BF16)
    masks = [mask("1", "up"), mask("2", "up"), mask("1", "down"), mask("2", "down")]
    context = attention(queries, keys, values, [([0, 1], masks, bias_ref[...])])
    out = finish(wanted(z), context, wo_ref[0], hg_ref[0:1, :], we_ref[0], ws_ref[0])
    na, nb = shifted_columns(layer_norm(out, ag_ref[1:2, :]))
    na_ref[...] = na.astype(BF16)
    nb_ref[...] = nb.astype(BF16)
    right, left = edges(nb)
    n = own_right_ref.shape[0]
    col_odd = lax.rem(lax.axis_index("gx"), 2) == 1
    for at, size, a, b in [(0, n, own_right_ref[...], own_left_ref[...]), (n, 32, right, left)]:
        a, b = a.astype(F32), b.astype(F32)
        cols_odd_ref[at : at + size, :] = jnp.where(col_odd, a, b).astype(BF16)
        cols_even_ref[at : at + size, :] = jnp.where(col_odd, b, a).astype(BF16)


def middle_kernel(
    fa_ref, na_ref, va_ref, pb_ref, w_ref, wo_ref, we_ref, ws_ref, hg_ref,
    out_ref, bias_b, bias_bv, wqv_ref, wk_ref,
    bias_a, bias_av,
):
    sub = iota((8, 128), 0)
    lane = iota((8, 128), 1)
    query_left = (lane & 4) == 0
    query_up = (lane & 32) == 0
    row, col = lax.axis_index("gy"), lax.axis_index("gx")
    last_col = jnp.where(query_left, lax.axis_size("gx") - 1, 0) == col
    last_row = jnp.where(query_up, lax.axis_size("gy") - 1, 0) == row
    cut_col = last_col & (query_left != (sub < 4))
    for head, yj, values in bias_rows(pb_ref, 1):
        at = (slice(yj * 8, yj * 8 + 8), slice(head * 128, head * 128 + 128))
        cut = values - 100.0 * LOG2E
        cut_row = (lane >= 64) & last_row & (jnp.logical_not(query_up) if yj < 4 else query_up)
        bias_a[at] = values
        bias_av[at] = jnp.where(cut_row, cut, values)
        bias_b[at] = jnp.where(cut_col, cut, values)
        bias_bv[at] = jnp.where(cut_row | cut_col, cut, values)
    fill_weights(w_ref[1], wqv_ref, wk_ref)
    n = na_ref.shape[0]
    inner = na_ref[32 : n - 32, :]
    first = cat([va_ref[32:64, :], na_ref[0:32, :]])
    last = cat([na_ref[n - 32 : n, :], va_ref[0:32, :]])
    looked_at = cat([inner, last, first, first])
    keys = side_by_side(looked_at, wk_ref[...])
    values = dot(wqv_ref[128:256, :], looked_at, NT).astype(BF16)
    wanted = cat([na_ref[32:n, :], na_ref[0:32, :]])
    queries = dot(wqv_ref[0:128, :], wanted, NT).astype(BF16)
    last_unit = n // 128 - 1
    masks = [mask("1"), mask("2")]
    units = [([u], masks, bias_a[...]) for u in range(last_unit)]
    masks = [mask("1"), mask("2", "up"), mask("2", "down"), jnp.zeros((64, 128), BF16)]
    units.append(([last_unit, last_unit + 1], masks, bias_av[...]))
    context = attention(queries, keys, values, units)
    z = cat([fa_ref[32:n, :], fa_ref[0:32, :]])
    out = finish(z, context, wo_ref[1], hg_ref[1:2, :], we_ref[1], ws_ref[1])
    out = half_turn(out).reshape(n, 128)
    out_ref[32:n, :] = out[0 : n - 32]
    out_ref[0:32, :] = out[n - 32 : n]


def outer_kernel(
    fb_ref, nb_ref, vb_ref, cols_odd_ref, cols_even_ref, oa_ref, bias_b, bias_bv, wqv_ref, wk_ref, wo_ref, we_ref, ws_ref, hg_ref,
    out_ref,
):
    n = nb_ref.shape[0]
    h = n // 2

    def in_order(ref, end, size):
        rows = cat([ref[end + size : end + 2 * size, :], ref[0:end, :], ref[end : end + size, :]])
        return rows.astype(F32).reshape(-1, 8, 128)

    own = cat([vb_ref[32:64, :], nb_ref[...], vb_ref[0:32, :]]).astype(F32).reshape(-1, 8, 128)
    odd, even = in_order(cols_odd_ref, h, 16), in_order(cols_even_ref, h, 16)
    col_odd = lax.rem(lax.axis_index("gx"), 2) == 1
    hl, hr = jnp.where(col_odd, even, odd), jnp.where(col_odd, odd, even)
    low = low_half(hl.shape)
    even = jnp.where(low, hl, pltpu.roll(hr, 4, 1))
    odd = jnp.where(low, pltpu.roll(hl, 4, 1), hr)
    halo = jnp.stack([even, odd], axis=1).reshape(own.shape)
    low = low_half(own.shape)
    right = jnp.where(low, own, halo).reshape(-1, 64, 128).astype(BF16)
    left = jnp.where(low, halo, own).reshape(-1, 64, 128).astype(BF16)
    count = right.shape[0]
    looked_at = cat([t for w in range(count) for t in (right[w], left[w])])
    keys = side_by_side(looked_at, wk_ref[...])
    values = dot(wqv_ref[128:256, :], looked_at, NT).astype(BF16)
    wanted = cat([nb_ref[32:n, :], nb_ref[0:32, :]])
    queries = dot(wqv_ref[0:128, :], wanted, NT).astype(BF16)
    masks = [mask(w, s) for w in "12" for s in ("left", "right")]
    units = [([w, w + 1], masks, bias_b[...]) for w in range(1, count - 2, 2)]
    masks = masks[0:2] + [mask("2", v, s) for v in ("up", "down") for s in ("left", "right")]
    units.append(([count - 2, count - 1, 0], masks, bias_bv[...]))
    context = attention(queries, keys, values, units)
    z = cat([fb_ref[32:n, :], fb_ref[0:32, :]])
    out = finish(z, context, wo_ref[1], hg_ref[1:2, :], we_ref[1], ws_ref[1])
    out = half_turn(out)
    rows = n // 8
    out = cat([out[rows - 4 :], out[: rows - 4]])
    inner = oa_ref[...].reshape(rows, 8, 128)
    low = low_half(out.shape)
    out_ref[:, 0:8, :] = jnp.where(low, out, inner)
    out_ref[:, 8:16, :] = jnp.where(low, inner, out)


def vmem(count):
    return [pl.BlockSpec(memory_space=pltpu.VMEM)] * count


def call(kernel, name, operands, specs, outs, scratch=(), flops=0):
    shapes = [jax.ShapeDtypeStruct(shape, dtype) for shape, dtype in outs]
    return pl.pallas_call(
        kernel,
        out_shape=shapes,
        in_specs=specs,
        out_specs=vmem(len(outs)),
        scratch_shapes=list(scratch),
        compiler_params=pltpu.CompilerParams(vmem_limit_bytes=32 * 1024 * 1024),
        cost_estimate=pl.CostEstimate(flops=flops, bytes_accessed=1 << 20, transcendentals=0),
        name=name,
    )(*operands)


def on_device(x, ag, tw, ow, pb, hg, ew, sw):
    height, breadth = x.shape[0], x.shape[1]
    n = height * WIN
    hbm = [pl.BlockSpec(memory_space=pltpu.HBM)]
    odd, even = call(
        edge_rows_kernel, "edge_rows", (x,), hbm,
        [((WIN, breadth, C), BF16)] * 2, [pltpu.SemaphoreType.DMA((2,))], 4 * 10**10,
    )
    odd, even = swap(odd, "gy", 1), swap(even, "gy", 0)
    table = ((64, HEADS * 128), F32)
    prepared = [((256, 128), BF16), ((256, 256), BF16)]
    fa, fb, na, nb, right, left, bias, wqv, wk, w, wo, we, ws = call(
        own_kernel, "own", (x, tw, ow, ew, sw, ag, pb, hg), hbm * 5 + vmem(3),
        [((n, C), F32)] * 2 + [((n, C), BF16)] * 2 + [((n // 2, C), BF16)] * 2 + [table] + prepared
        + [(tw.shape, BF16), (ow.shape, BF16), (ew.shape, BF16), (sw.shape, BF16)],
        [pltpu.VMEM(x.shape, BF16), pltpu.SemaphoreType.DMA((5,))], 4 * 10**9,
    )
    va, vb, odd, even = call(
        halo_kernel, "halo", (odd, even, right, left, bias, wqv, wk, wo, we, ws, ag, hg), vmem(12),
        [((64, C), BF16)] * 2 + [((n // 2 + 32, C), BF16)] * 2, (), 10**9,
    )
    odd, even = swap(odd, "gx", 1), swap(even, "gx", 0)
    oa, bias_b, bias_bv, wqv, wk = call(
        middle_kernel, "middle", (fa, na, va, pb, w, wo, we, ws, hg),
        vmem(9),
        [((n, C), F32), table, table] + prepared,
        [pltpu.VMEM(*table)] * 2, 2 * 10**9,
    )
    return call(
        outer_kernel, "outer", (fb, nb, vb, odd, even, oa, bias_b, bias_bv, wqv, wk, wo, we, ws, hg), vmem(14),
        [((height, breadth, C), F32)], (), 2 * 10**9,
    )[0]


def solution(mesh):
    return jax.shard_map(
        on_device,
        mesh=mesh,
        in_specs=(P("gy", "gx", None), P(), P(), P(), P(), P(), P(), P()),
        out_specs=P("gy", "gx", None),
        check_vma=False,
    )
```

```python
import math

import jax
import jax.numpy as jnp
from jax import lax
from jax.experimental import pallas as pl
from jax.experimental.pallas import tpu as pltpu
from jax.sharding import PartitionSpec as P

C = 128
HEADS = 4
HID = 512
WIN = 8
HD = 32
EPSILON = 1e-05
LOG2E = math.log2(math.e)
SCALE = HD ** (-0.5) * LOG2E
F32 = jnp.float32
BF16 = jnp.bfloat16
NT = (((1,), (1,)), ((), ()))
TN = (((0,), (0,)), ((), ()))
CHUNK = 256


def swap(x, axis, first):
    length = lax.axis_size(axis)
    there = [(i, (i + 1) % length) for i in range(first, length, 2)]
    return lax.ppermute(x, axis, there + [(b, a) for a, b in there])


def iota(shape, dim):
    return lax.broadcasted_iota(jnp.int32, shape, dim)


def dot(a, b, dims=None):
    if dims is None:
        return jnp.dot(a, b, preferred_element_type=F32)
    return lax.dot_general(a, b, dims, preferred_element_type=F32)


def cat(parts, axis=0):
    return jnp.concatenate(parts, axis=axis)


def layer_norm(x, gain):
    center = x - jnp.mean(x, axis=-1, keepdims=True)
    spread = jnp.sum(center * center, axis=-1, keepdims=True)
    return center * lax.rsqrt(spread + C * EPSILON) * (gain * C**0.5)


def twice_gelu(x):
    return x + x * lax.erf(x * (0.5**0.5))


def bias_rows(pb_ref, block):
    sub = iota((8, 128), 0)
    lane = iota((8, 128), 1)
    place = lax.min((lane >> 3) * 15 + 7 + (lane & 7) - sub, 224)
    for head in range(HEADS):
        low = jnp.broadcast_to(pb_ref[block, head : head + 1, 0:128], (8, 128))
        high = jnp.broadcast_to(pb_ref[block, head : head + 1, 97:225], (8, 128))
        strip = jnp.where(
            place < 128,
            jnp.take_along_axis(low, lax.min(place, 127), axis=1),
            jnp.take_along_axis(high, lax.max(place - 97, 0), axis=1),
        )
        strip = strip * LOG2E
        for yj in range(8):
            turn = (128 - (7 - yj) * 8) % 128
            first = pltpu.roll(strip, turn, 1) if turn else strip
            second = pltpu.roll(strip, (turn + 64) % 128, 1)
            yield head, yj, jnp.where(lane < 64, first, second)


def fill_weights(w, wqv, wk):
    wqv[0:128, :] = jnp.transpose(w[:, 0:128].astype(F32)).astype(BF16)
    wqv[128:256, :] = jnp.transpose(w[:, 256:384].astype(F32)).astype(BF16)
    keys = w[:, 128:256].astype(F32)
    turned = pltpu.roll(keys, 64, 1)
    lane = iota((128, 128), 1)
    zero = jnp.zeros((128, 128), F32)
    wk[0:128, 0:128] = jnp.where(lane < 64, keys, zero).astype(BF16)
    wk[0:128, 128:256] = jnp.where(lane < 64, turned, zero).astype(BF16)
    wk[128:256, 0:128] = jnp.where(lane >= 64, turned, zero).astype(BF16)
    wk[128:256, 128:256] = jnp.where(lane >= 64, keys, zero).astype(BF16)


def mask(*conditions):
    lane = iota((64, 128), 1)
    sides = {"1": lane < 64, "2": lane >= 64, "up": (lane & 32) == 0, "down": (lane & 32) > 0}
    sides |= {"left": (lane & 4) == 0, "right": (lane & 4) > 0}
    keep = sides[conditions[0]]
    for name in conditions[1:]:
        keep = keep & sides[name]
    return jnp.where(keep, 1.0, 0.0).astype(BF16)


def side_by_side(tokens, wk):
    pairs = tokens.reshape(-1, 2, 64, 128)
    lanes = cat([cat([pairs[p, 0], pairs[p, 1]], 1) for p in range(pairs.shape[0])])
    return dot(lanes, wk).astype(BF16)


def attention(queries, keys, values, units):
    zero = jnp.zeros((32, 128), BF16)
    scores = []
    for u, (pairs, masks, bias) in enumerate(units):
        q = queries[:, 128 * u : 128 * u + 128]
        for half in range(2):
            r = 64 * half
            rows = []
            for m in masks:
                rows.append(cat([q[r : r + 32] * m[0:32], zero], 1))
                rows.append(cat([zero, q[r + 32 : r + 64] * m[0:32]], 1))
            k = cat([keys[64 * p : 64 * p + 64, 128 * half : 128 * half + 128] for p in pairs], 1)
            scores.append(dot(k, cat(rows)))
    for u, (pairs, masks, bias) in enumerate(units):
        for half in range(2):
            s = scores[2 * u + half] * SCALE + bias[:, 256 * half : 256 * half + 256]
            p = jnp.exp2(s - jnp.max(s, axis=0, keepdims=True))
            part = 1.0 / jnp.sum(p, axis=0, keepdims=True)
            scores[2 * u + half] = (p * part).astype(BF16)
    context = []
    for u, (pairs, masks, bias) in enumerate(units):
        out = []
        for half in range(2):
            r = 64 * half
            p = scores[2 * u + half]
            seen = cat([cat([p[:, 0:128] * m, p[:, 128:256] * m], 1) for m in masks])
            v = cat([values[r : r + 64, 128 * j : 128 * j + 128] for j in pairs], 1)
            ct = dot(v, seen)
            out += [ct[0:32, 0:128], ct[32:64, 128:256]]
        context.append(cat(out).astype(BF16))
    return cat(context, 1)


def finish(z, context, wo, gain, we, ws):
    middle = z + dot(context, wo, TN).astype(BF16).astype(F32)
    normed = layer_norm(middle, gain).astype(BF16)
    size = min(CHUNK, z.shape[0])
    hidden = [dot(normed[i : i + size], we) for i in range(0, z.shape[0], size)]
    hidden = [twice_gelu(h).astype(BF16) for h in hidden]
    return middle + 0.5 * cat([dot(h, ws) for h in hidden])


def half_turn(x):
    return pltpu.roll(x.reshape(-1, 8, 128), 4, 1)


def low_half(shape):
    return iota(shape, 1) < 4


def windows_of(block):
    parts = block.astype(F32).reshape(8, 2, 8, 128)
    return [parts[:, 0].reshape(64, 128), parts[:, 1].reshape(64, 128)]


def shifted_columns(tokens):
    pairs = tokens.reshape(-1, 2, 64, 128)
    a, b = half_turn(pairs[:, 0]), half_turn(pairs[:, 1])
    low = low_half(a.shape)
    return jnp.where(low, a, b).reshape(-1, 128), jnp.where(low, b, a).reshape(-1, 128)


def edges(outer):
    pairs = outer.reshape(-1, 2, 8, 128)
    even, odd = pairs[:, 0], pairs[:, 1]
    low = low_half(even.shape)
    right = jnp.where(low, even, pltpu.roll(odd, 4, 1)).reshape(-1, 128)
    left = jnp.where(low, pltpu.roll(even, 4, 1), odd).reshape(-1, 128)
    return right.astype(BF16), left.astype(BF16)


def goes_first():
    row, rows = lax.axis_index("gy"), lax.axis_size("gy")
    return lax.rem(row, rows // 2) < rows // 4


def own_block(
    x_ref, w_ref, wo_ref, we_ref, ws_ref, ag_ref, pb_ref, hg_ref,
    fa_ref, fb_ref, na_ref, nb_ref, right_ref, left_ref, bias_ref, wqv_ref, wk_ref,
):
    for head, yj, values in bias_rows(pb_ref, 0):
        bias_ref[yj * 8 : yj * 8 + 8, head * 128 : head * 128 + 128] = values
    fill_weights(w_ref[0], wqv_ref, wk_ref)
    bands = x_ref.shape[0] // WIN
    z = cat([t for b in range(bands) for t in windows_of(x_ref[WIN * b : WIN * b + WIN])])
    normed = layer_norm(z, ag_ref[0:1, :]).astype(BF16)
    qv = dot(wqv_ref[...], normed, NT).astype(BF16)
    keys = side_by_side(normed, wk_ref[...])
    masks = [mask("1"), mask("2")]
    units = [([b], masks, bias_ref[...]) for b in range(bands)]
    context = attention(qv[0:128], keys, qv[128:256], units)
    out = finish(z, context, wo_ref[0], hg_ref[0:1, :], we_ref[0], ws_ref[0])
    fa_ref[...], fb_ref[...] = shifted_columns(out)
    na, nb = shifted_columns(layer_norm(out, ag_ref[1:2, :]))
    na_ref[...] = na.astype(BF16)
    nb_ref[...] = nb.astype(BF16)
    right_ref[...], left_ref[...] = edges(nb)


def parity_kernel(out_ref):
    out_ref[...] = jnp.full(out_ref.shape, lax.rem(lax.axis_index("gy"), 2), jnp.int32)


def edge_rows_kernel(x_ref, parity_ref, odd_ref, even_ref, sems):
    bottom = x_ref.shape[0] - WIN
    is_odd = parity_ref[0, 0]
    copies = [
        pltpu.make_async_copy(x_ref.at[pl.ds(is_odd * bottom, WIN)], odd_ref, sems.at[0]),
        pltpu.make_async_copy(x_ref.at[pl.ds((1 - is_odd) * bottom, WIN)], even_ref, sems.at[1]),
    ]
    for copy in copies:
        copy.start()
    for copy in copies:
        copy.wait()


def first_kernel(*refs):
    @pl.when(goes_first())
    def _():
        own_block(*refs[0:8], *refs[12:])


def second_kernel(*refs):
    @pl.when(jnp.logical_not(goes_first()))
    def _():
        own_block(*refs[0:8], *refs[17:])


def halo_kernel(
    rows_odd_ref, rows_even_ref, own_right_ref, own_left_ref, bias_ref, wqv_ref, wk_ref, wo_ref, we_ref, ws_ref, ag_ref, hg_ref,
    na_ref, nb_ref, cols_odd_ref, cols_even_ref,
):
    row_odd = lax.rem(lax.axis_index("gy"), 2) == 1
    rows_odd, rows_even = rows_odd_ref[...].astype(F32), rows_even_ref[...].astype(F32)
    down = jnp.where(row_odd, rows_odd, rows_even)
    up = jnp.where(row_odd, rows_even, rows_odd)
    z = cat(windows_of(down) + windows_of(up))
    normed = layer_norm(z, ag_ref[0:1, :]).astype(BF16)
    keys = side_by_side(normed, wk_ref[...])
    values = dot(wqv_ref[128:256, :], normed, NT).astype(BF16)

    def wanted(t):
        return cat([t[0:32], t[160:192], t[64:96], t[224:256]])

    queries = dot(wqv_ref[0:128, :], wanted(normed), NT).astype(BF16)
    masks = [mask("1", "up"), mask("2", "up"), mask("1", "down"), mask("2", "down")]
    context = attention(queries, keys, values, [([0, 1], masks, bias_ref[...])])
    out = finish(wanted(z), context, wo_ref[0], hg_ref[0:1, :], we_ref[0], ws_ref[0])
    na, nb = shifted_columns(layer_norm(out, ag_ref[1:2, :]))
    na_ref[...] = na.astype(BF16)
    nb_ref[...] = nb.astype(BF16)
    right, left = edges(nb)
    n = own_right_ref.shape[0]
    col_odd = lax.rem(lax.axis_index("gx"), 2) == 1
    for at, size, a, b in [(0, n, own_right_ref[...], own_left_ref[...]), (n, 32, right, left)]:
        a, b = a.astype(F32), b.astype(F32)
        cols_odd_ref[at : at + size, :] = jnp.where(col_odd, a, b).astype(BF16)
        cols_even_ref[at : at + size, :] = jnp.where(col_odd, b, a).astype(BF16)


def middle_kernel(
    fa_ref, na_ref, va_ref, pb_ref, w_ref, wo_ref, we_ref, ws_ref, hg_ref,
    out_ref, bias_b, bias_bv, wqv_ref, wk_ref,
    bias_a, bias_av,
):
    sub = iota((8, 128), 0)
    lane = iota((8, 128), 1)
    query_left = (lane & 4) == 0
    query_up = (lane & 32) == 0
    row, col = lax.axis_index("gy"), lax.axis_index("gx")
    last_col = jnp.where(query_left, lax.axis_size("gx") - 1, 0) == col
    last_row = jnp.where(query_up, lax.axis_size("gy") - 1, 0) == row
    cut_col = last_col & (query_left != (sub < 4))
    for head, yj, values in bias_rows(pb_ref, 1):
        at = (slice(yj * 8, yj * 8 + 8), slice(head * 128, head * 128 + 128))
        cut = values - 100.0 * LOG2E
        cut_row = (lane >= 64) & last_row & (jnp.logical_not(query_up) if yj < 4 else query_up)
        bias_a[at] = values
        bias_av[at] = jnp.where(cut_row, cut, values)
        bias_b[at] = jnp.where(cut_col, cut, values)
        bias_bv[at] = jnp.where(cut_row | cut_col, cut, values)
    fill_weights(w_ref[1], wqv_ref, wk_ref)
    n = na_ref.shape[0]
    inner = na_ref[32 : n - 32, :]
    first = cat([va_ref[32:64, :], na_ref[0:32, :]])
    last = cat([na_ref[n - 32 : n, :], va_ref[0:32, :]])
    looked_at = cat([inner, last, first, first])
    keys = side_by_side(looked_at, wk_ref[...])
    values = dot(wqv_ref[128:256, :], looked_at, NT).astype(BF16)
    wanted = cat([na_ref[32:n, :], na_ref[0:32, :]])
    queries = dot(wqv_ref[0:128, :], wanted, NT).astype(BF16)
    last_unit = n // 128 - 1
    masks = [mask("1"), mask("2")]
    units = [([u], masks, bias_a[...]) for u in range(last_unit)]
    masks = [mask("1"), mask("2", "up"), mask("2", "down"), jnp.zeros((64, 128), BF16)]
    units.append(([last_unit, last_unit + 1], masks, bias_av[...]))
    context = attention(queries, keys, values, units)
    z = cat([fa_ref[32:n, :], fa_ref[0:32, :]])
    out = finish(z, context, wo_ref[1], hg_ref[1:2, :], we_ref[1], ws_ref[1])
    out = half_turn(out).reshape(n, 128)
    out_ref[32:n, :] = out[0 : n - 32]
    out_ref[0:32, :] = out[n - 32 : n]


def outer_kernel(
    fb_ref, nb_ref, vb_ref, cols_odd_ref, cols_even_ref, oa_ref, bias_b, bias_bv, wqv_ref, wk_ref, wo_ref, we_ref, ws_ref, hg_ref,
    out_ref,
):
    n = nb_ref.shape[0]
    h = n // 2

    def in_order(ref, end, size):
        rows = cat([ref[end + size : end + 2 * size, :], ref[0:end, :], ref[end : end + size, :]])
        return rows.astype(F32).reshape(-1, 8, 128)

    own = cat([vb_ref[32:64, :], nb_ref[...], vb_ref[0:32, :]]).astype(F32).reshape(-1, 8, 128)
    odd, even = in_order(cols_odd_ref, h, 16), in_order(cols_even_ref, h, 16)
    col_odd = lax.rem(lax.axis_index("gx"), 2) == 1
    hl, hr = jnp.where(col_odd, even, odd), jnp.where(col_odd, odd, even)
    low = low_half(hl.shape)
    even = jnp.where(low, hl, pltpu.roll(hr, 4, 1))
    odd = jnp.where(low, pltpu.roll(hl, 4, 1), hr)
    halo = jnp.stack([even, odd], axis=1).reshape(own.shape)
    low = low_half(own.shape)
    right = jnp.where(low, own, halo).reshape(-1, 64, 128).astype(BF16)
    left = jnp.where(low, halo, own).reshape(-1, 64, 128).astype(BF16)
    count = right.shape[0]
    looked_at = cat([t for w in range(count) for t in (right[w], left[w])])
    keys = side_by_side(looked_at, wk_ref[...])
    values = dot(wqv_ref[128:256, :], looked_at, NT).astype(BF16)
    wanted = cat([nb_ref[32:n, :], nb_ref[0:32, :]])
    queries = dot(wqv_ref[0:128, :], wanted, NT).astype(BF16)
    masks = [mask(w, s) for w in "12" for s in ("left", "right")]
    units = [([w, w + 1], masks, bias_b[...]) for w in range(1, count - 2, 2)]
    masks = masks[0:2] + [mask("2", v, s) for v in ("up", "down") for s in ("left", "right")]
    units.append(([count - 2, count - 1, 0], masks, bias_bv[...]))
    context = attention(queries, keys, values, units)
    z = cat([fb_ref[32:n, :], fb_ref[0:32, :]])
    out = finish(z, context, wo_ref[1], hg_ref[1:2, :], we_ref[1], ws_ref[1])
    out = half_turn(out)
    rows = n // 8
    out = cat([out[rows - 4 :], out[: rows - 4]])
    inner = oa_ref[...].reshape(rows, 8, 128)
    low = low_half(out.shape)
    out_ref[:, 0:8, :] = jnp.where(low, out, inner)
    out_ref[:, 8:16, :] = jnp.where(low, inner, out)


def vmem(count):
    return [pl.BlockSpec(memory_space=pltpu.VMEM)] * count


def call(kernel, name, operands, outs, scratch=(), flops=0, aliases=None):
    shapes = [jax.ShapeDtypeStruct(shape, dtype) for shape, dtype in outs]
    return pl.pallas_call(
        kernel,
        out_shape=shapes,
        in_specs=vmem(len(operands)),
        out_specs=vmem(len(outs)),
        scratch_shapes=list(scratch),
        input_output_aliases=aliases or {},
        compiler_params=pltpu.CompilerParams(vmem_limit_bytes=32 * 1024 * 1024),
        cost_estimate=pl.CostEstimate(flops=flops, bytes_accessed=1 << 20, transcendentals=0),
        name=name,
    )(*operands)


def on_device(x, ag, tw, ow, pb, hg, ew, sw):
    height, breadth = x.shape[0], x.shape[1]
    n = height * WIN
    table = ((64, HEADS * 128), F32)
    prepared = [((256, 128), BF16), ((256, 256), BF16)]
    weights = (x, tw, ow, ew, sw, ag, pb, hg)
    kept = [((n, C), F32)] * 2 + [((n, C), BF16)] * 2 + [((n // 2, C), BF16)] * 2 + [table] + prepared
    rows = [((WIN, breadth, C), BF16)] * 2
    (parity,) = call(parity_kernel, "parity", (), [((8, 128), jnp.int32)], (), 4 * 10**10)
    odd, even = call(
        edge_rows_kernel, "edge_rows", (x, parity), rows, [pltpu.SemaphoreType.DMA((2,))]
    )
    odd, even, *state = call(
        first_kernel, "first", (*weights, odd, even), rows + kept, (), 4 * 10**9, {8: 0, 9: 1}
    )
    odd, even = swap(odd, "gy", 1), swap(even, "gy", 0)
    state = call(
        second_kernel, "second", (*weights, *state), kept, (), 4 * 10**9, {8 + i: i for i in range(9)}
    )
    fa, fb, na, nb, right, left, bias, wqv, wk = state
    va, vb, odd, even = call(
        halo_kernel, "halo", (odd, even, right, left, bias, wqv, wk, ow, ew, sw, ag, hg),
        [((64, C), BF16)] * 2 + [((n // 2 + 32, C), BF16)] * 2, (), 10**9,
    )
    odd, even = swap(odd, "gx", 1), swap(even, "gx", 0)
    oa, bias_b, bias_bv, wqv, wk = call(
        middle_kernel, "middle", (fa, na, va, pb, tw, ow, ew, sw, hg),
        [((n, C), F32), table, table] + prepared, [pltpu.VMEM(*table)] * 2, 2 * 10**9,
    )
    return call(
        outer_kernel, "outer", (fb, nb, vb, odd, even, oa, bias_b, bias_bv, wqv, wk, ow, ew, sw, hg),
        [((height, breadth, C), F32)], (), 2 * 10**9,
    )[0]


def solution(mesh):
    return jax.shard_map(
        on_device,
        mesh=mesh,
        in_specs=(P("gy", "gx", None), P(), P(), P(), P(), P(), P(), P()),
        out_specs=P("gy", "gx", None),
        check_vma=False,
    )
```

```python
import math

import jax
import jax.numpy as jnp
from jax import lax
from jax.experimental import pallas as pl
from jax.experimental.pallas import tpu as pltpu
from jax.sharding import PartitionSpec as P

C = 128
HEADS = 4
HID = 512
WIN = 8
HD = 32
EPSILON = 1e-05
LOG2E = math.log2(math.e)
SCALE = HD ** (-0.5) * LOG2E
F32 = jnp.float32
BF16 = jnp.bfloat16
NT = (((1,), (1,)), ((), ()))
TN = (((0,), (0,)), ((), ()))
CHUNK = 256


def swap(x, axis, first):
    length = lax.axis_size(axis)
    there = [(i, (i + 1) % length) for i in range(first, length, 2)]
    return lax.ppermute(x, axis, there + [(b, a) for a, b in there])


def iota(shape, dim):
    return lax.broadcasted_iota(jnp.int32, shape, dim)


def dot(a, b, dims=None):
    if dims is None:
        return jnp.dot(a, b, preferred_element_type=F32)
    return lax.dot_general(a, b, dims, preferred_element_type=F32)


def cat(parts, axis=0):
    return jnp.concatenate(parts, axis=axis)


def layer_norm(x, gain):
    center = x - jnp.mean(x, axis=-1, keepdims=True)
    spread = jnp.sum(center * center, axis=-1, keepdims=True)
    return center * lax.rsqrt(spread + C * EPSILON) * (gain * C**0.5)


def twice_gelu(x):
    return x + x * lax.erf(x * (0.5**0.5))


def bias_rows(pb_ref, block):
    sub = iota((8, 128), 0)
    lane = iota((8, 128), 1)
    place = lax.min((lane >> 3) * 15 + 7 + (lane & 7) - sub, 224)
    for head in range(HEADS):
        low = jnp.broadcast_to(pb_ref[block, head : head + 1, 0:128], (8, 128))
        high = jnp.broadcast_to(pb_ref[block, head : head + 1, 97:225], (8, 128))
        strip = jnp.where(
            place < 128,
            jnp.take_along_axis(low, lax.min(place, 127), axis=1),
            jnp.take_along_axis(high, lax.max(place - 97, 0), axis=1),
        )
        strip = strip * LOG2E
        for yj in range(8):
            turn = (128 - (7 - yj) * 8) % 128
            first = pltpu.roll(strip, turn, 1) if turn else strip
            second = pltpu.roll(strip, (turn + 64) % 128, 1)
            yield head, yj, jnp.where(lane < 64, first, second)


def fill_weights(w, wqv, wk):
    wqv[0:128, :] = jnp.transpose(w[:, 0:128].astype(F32)).astype(BF16)
    wqv[128:256, :] = jnp.transpose(w[:, 256:384].astype(F32)).astype(BF16)
    keys = w[:, 128:256].astype(F32)
    turned = pltpu.roll(keys, 64, 1)
    lane = iota((128, 128), 1)
    zero = jnp.zeros((128, 128), F32)
    wk[0:128, 0:128] = jnp.where(lane < 64, keys, zero).astype(BF16)
    wk[0:128, 128:256] = jnp.where(lane < 64, turned, zero).astype(BF16)
    wk[128:256, 0:128] = jnp.where(lane >= 64, turned, zero).astype(BF16)
    wk[128:256, 128:256] = jnp.where(lane >= 64, keys, zero).astype(BF16)


def mask(*conditions):
    lane = iota((64, 128), 1)
    sides = {"1": lane < 64, "2": lane >= 64, "up": (lane & 32) == 0, "down": (lane & 32) > 0}
    sides |= {"left": (lane & 4) == 0, "right": (lane & 4) > 0}
    keep = sides[conditions[0]]
    for name in conditions[1:]:
        keep = keep & sides[name]
    return jnp.where(keep, 1.0, 0.0).astype(BF16)


def side_by_side(tokens, wk):
    pairs = tokens.reshape(-1, 2, 64, 128)
    lanes = cat([cat([pairs[p, 0], pairs[p, 1]], 1) for p in range(pairs.shape[0])])
    return dot(lanes, wk).astype(BF16)


def attention(queries, keys, values, units):
    zero = jnp.zeros((32, 128), BF16)
    scores = []
    for u, (pairs, masks, bias) in enumerate(units):
        q = queries[:, 128 * u : 128 * u + 128]
        for half in range(2):
            r = 64 * half
            rows = []
            for m in masks:
                rows.append(cat([q[r : r + 32] * m[0:32], zero], 1))
                rows.append(cat([zero, q[r + 32 : r + 64] * m[0:32]], 1))
            k = cat([keys[64 * p : 64 * p + 64, 128 * half : 128 * half + 128] for p in pairs], 1)
            scores.append(dot(k, cat(rows)))
    for u, (pairs, masks, bias) in enumerate(units):
        for half in range(2):
            s = scores[2 * u + half] * SCALE + bias[:, 256 * half : 256 * half + 256]
            p = jnp.exp2(s - jnp.max(s, axis=0, keepdims=True))
            part = 1.0 / jnp.sum(p, axis=0, keepdims=True)
            scores[2 * u + half] = (p * part).astype(BF16)
    context = []
    for u, (pairs, masks, bias) in enumerate(units):
        out = []
        for half in range(2):
            r = 64 * half
            p = scores[2 * u + half]
            seen = cat([cat([p[:, 0:128] * m, p[:, 128:256] * m], 1) for m in masks])
            v = cat([values[r : r + 64, 128 * j : 128 * j + 128] for j in pairs], 1)
            ct = dot(v, seen)
            out += [ct[0:32, 0:128], ct[32:64, 128:256]]
        context.append(cat(out).astype(BF16))
    return cat(context, 1)


def finish(z, context, wo, gain, we, ws):
    middle = z + dot(context, wo, TN).astype(BF16).astype(F32)
    normed = layer_norm(middle, gain).astype(BF16)
    size = min(CHUNK, z.shape[0])
    hidden = [dot(normed[i : i + size], we) for i in range(0, z.shape[0], size)]
    hidden = [twice_gelu(h).astype(BF16) for h in hidden]
    return middle + 0.5 * cat([dot(h, ws) for h in hidden])


def half_turn(x):
    return pltpu.roll(x.reshape(-1, 8, 128), 4, 1)


def low_half(shape):
    return iota(shape, 1) < 4


def windows_of(block):
    parts = block.astype(F32).reshape(8, 2, 8, 128)
    return [parts[:, 0].reshape(64, 128), parts[:, 1].reshape(64, 128)]


def shifted_columns(tokens):
    pairs = tokens.reshape(-1, 2, 64, 128)
    a, b = half_turn(pairs[:, 0]), half_turn(pairs[:, 1])
    low = low_half(a.shape)
    return jnp.where(low, a, b).reshape(-1, 128), jnp.where(low, b, a).reshape(-1, 128)


def edges(outer):
    pairs = outer.reshape(-1, 2, 8, 128)
    even, odd = pairs[:, 0], pairs[:, 1]
    low = low_half(even.shape)
    right = jnp.where(low, even, pltpu.roll(odd, 4, 1)).reshape(-1, 128)
    left = jnp.where(low, pltpu.roll(even, 4, 1), odd).reshape(-1, 128)
    return right.astype(BF16), left.astype(BF16)


def goes_first():
    row, rows = lax.axis_index("gy"), lax.axis_size("gy")
    return lax.rem(row, rows // 2) < rows // 4


def own_block(
    x_ref, w_ref, wo_ref, we_ref, ws_ref, ag_ref, pb_ref, hg_ref,
    fa_ref, fb_ref, na_ref, nb_ref, right_ref, left_ref, bias_ref, wqv_ref, wk_ref,
):
    for head, yj, values in bias_rows(pb_ref, 0):
        bias_ref[yj * 8 : yj * 8 + 8, head * 128 : head * 128 + 128] = values
    fill_weights(w_ref[0], wqv_ref, wk_ref)
    bands = x_ref.shape[0] // WIN
    z = cat([t for b in range(bands) for t in windows_of(x_ref[WIN * b : WIN * b + WIN])])
    normed = layer_norm(z, ag_ref[0:1, :]).astype(BF16)
    qv = dot(wqv_ref[...], normed, NT).astype(BF16)
    keys = side_by_side(normed, wk_ref[...])
    masks = [mask("1"), mask("2")]
    units = [([b], masks, bias_ref[...]) for b in range(bands)]
    context = attention(qv[0:128], keys, qv[128:256], units)
    out = finish(z, context, wo_ref[0], hg_ref[0:1, :], we_ref[0], ws_ref[0])
    fa_ref[...], fb_ref[...] = shifted_columns(out)
    na, nb = shifted_columns(layer_norm(out, ag_ref[1:2, :]))
    na_ref[...] = na.astype(BF16)
    nb_ref[...] = nb.astype(BF16)
    right_ref[...], left_ref[...] = edges(nb)


def parity_kernel(out_ref):
    out_ref[...] = jnp.full(out_ref.shape, lax.rem(lax.axis_index("gy"), 2), jnp.int32)


def edge_rows_kernel(x_ref, parity_ref, ag_ref, pb_ref, hg_ref, odd_ref, even_ref, sems):
    bottom = x_ref.shape[0] - WIN
    is_odd = parity_ref[0, 0]
    copies = [
        pltpu.make_async_copy(x_ref.at[pl.ds(is_odd * bottom, WIN)], odd_ref, sems.at[0]),
        pltpu.make_async_copy(x_ref.at[pl.ds((1 - is_odd) * bottom, WIN)], even_ref, sems.at[1]),
    ]
    for copy in copies:
        copy.start()
    for copy in copies:
        copy.wait()


def first_kernel(*refs):
    own_block(*refs[0:8], *refs[12:])


def nothing_kernel(*refs):
    pass


def second_kernel(*refs):
    @pl.when(jnp.logical_not(goes_first()))
    def _():
        own_block(*refs[0:8], *refs[17:])


def halo_kernel(
    rows_odd_ref, rows_even_ref, own_right_ref, own_left_ref, bias_ref, wqv_ref, wk_ref, wo_ref, we_ref, ws_ref, ag_ref, hg_ref,
    na_ref, nb_ref, cols_odd_ref, cols_even_ref,
):
    row_odd = lax.rem(lax.axis_index("gy"), 2) == 1
    rows_odd, rows_even = rows_odd_ref[...].astype(F32), rows_even_ref[...].astype(F32)
    down = jnp.where(row_odd, rows_odd, rows_even)
    up = jnp.where(row_odd, rows_even, rows_odd)
    z = cat(windows_of(down) + windows_of(up))
    normed = layer_norm(z, ag_ref[0:1, :]).astype(BF16)
    keys = side_by_side(normed, wk_ref[...])
    values = dot(wqv_ref[128:256, :], normed, NT).astype(BF16)

    def wanted(t):
        return cat([t[0:32], t[160:192], t[64:96], t[224:256]])

    queries = dot(wqv_ref[0:128, :], wanted(normed), NT).astype(BF16)
    masks = [mask("1", "up"), mask("2", "up"), mask("1", "down"), mask("2", "down")]
    context = attention(queries, keys, values, [([0, 1], masks, bias_ref[...])])
    out = finish(wanted(z), context, wo_ref[0], hg_ref[0:1, :], we_ref[0], ws_ref[0])
    na, nb = shifted_columns(layer_norm(out, ag_ref[1:2, :]))
    na_ref[...] = na.astype(BF16)
    nb_ref[...] = nb.astype(BF16)
    right, left = edges(nb)
    n = own_right_ref.shape[0]
    col_odd = lax.rem(lax.axis_index("gx"), 2) == 1
    for at, size, a, b in [(0, n, own_right_ref[...], own_left_ref[...]), (n, 32, right, left)]:
        a, b = a.astype(F32), b.astype(F32)
        cols_odd_ref[at : at + size, :] = jnp.where(col_odd, a, b).astype(BF16)
        cols_even_ref[at : at + size, :] = jnp.where(col_odd, b, a).astype(BF16)


def middle_kernel(
    fa_ref, na_ref, va_ref, pb_ref, w_ref, wo_ref, we_ref, ws_ref, hg_ref,
    out_ref, bias_b, bias_bv, wqv_ref, wk_ref,
    bias_a, bias_av,
):
    sub = iota((8, 128), 0)
    lane = iota((8, 128), 1)
    query_left = (lane & 4) == 0
    query_up = (lane & 32) == 0
    row, col = lax.axis_index("gy"), lax.axis_index("gx")
    last_col = jnp.where(query_left, lax.axis_size("gx") - 1, 0) == col
    last_row = jnp.where(query_up, lax.axis_size("gy") - 1, 0) == row
    cut_col = last_col & (query_left != (sub < 4))
    for head, yj, values in bias_rows(pb_ref, 1):
        at = (slice(yj * 8, yj * 8 + 8), slice(head * 128, head * 128 + 128))
        cut = values - 100.0 * LOG2E
        cut_row = (lane >= 64) & last_row & (jnp.logical_not(query_up) if yj < 4 else query_up)
        bias_a[at] = values
        bias_av[at] = jnp.where(cut_row, cut, values)
        bias_b[at] = jnp.where(cut_col, cut, values)
        bias_bv[at] = jnp.where(cut_row | cut_col, cut, values)
    fill_weights(w_ref[1], wqv_ref, wk_ref)
    n = na_ref.shape[0]
    inner = na_ref[32 : n - 32, :]
    first = cat([va_ref[32:64, :], na_ref[0:32, :]])
    last = cat([na_ref[n - 32 : n, :], va_ref[0:32, :]])
    looked_at = cat([inner, last, first, first])
    keys = side_by_side(looked_at, wk_ref[...])
    values = dot(wqv_ref[128:256, :], looked_at, NT).astype(BF16)
    wanted = cat([na_ref[32:n, :], na_ref[0:32, :]])
    queries = dot(wqv_ref[0:128, :], wanted, NT).astype(BF16)
    last_unit = n // 128 - 1
    masks = [mask("1"), mask("2")]
    units = [([u], masks, bias_a[...]) for u in range(last_unit)]
    masks = [mask("1"), mask("2", "up"), mask("2", "down"), jnp.zeros((64, 128), BF16)]
    units.append(([last_unit, last_unit + 1], masks, bias_av[...]))
    context = attention(queries, keys, values, units)
    z = cat([fa_ref[32:n, :], fa_ref[0:32, :]])
    out = finish(z, context, wo_ref[1], hg_ref[1:2, :], we_ref[1], ws_ref[1])
    out = half_turn(out).reshape(n, 128)
    out_ref[32:n, :] = out[0 : n - 32]
    out_ref[0:32, :] = out[n - 32 : n]


def outer_kernel(
    fb_ref, nb_ref, vb_ref, cols_odd_ref, cols_even_ref, oa_ref, bias_b, bias_bv, wqv_ref, wk_ref, wo_ref, we_ref, ws_ref, hg_ref,
    out_ref,
):
    n = nb_ref.shape[0]
    h = n // 2

    def in_order(ref, end, size):
        rows = cat([ref[end + size : end + 2 * size, :], ref[0:end, :], ref[end : end + size, :]])
        return rows.astype(F32).reshape(-1, 8, 128)

    own = cat([vb_ref[32:64, :], nb_ref[...], vb_ref[0:32, :]]).astype(F32).reshape(-1, 8, 128)
    odd, even = in_order(cols_odd_ref, h, 16), in_order(cols_even_ref, h, 16)
    col_odd = lax.rem(lax.axis_index("gx"), 2) == 1
    hl, hr = jnp.where(col_odd, even, odd), jnp.where(col_odd, odd, even)
    low = low_half(hl.shape)
    even = jnp.where(low, hl, pltpu.roll(hr, 4, 1))
    odd = jnp.where(low, pltpu.roll(hl, 4, 1), hr)
    halo = jnp.stack([even, odd], axis=1).reshape(own.shape)
    low = low_half(own.shape)
    right = jnp.where(low, own, halo).reshape(-1, 64, 128).astype(BF16)
    left = jnp.where(low, halo, own).reshape(-1, 64, 128).astype(BF16)
    count = right.shape[0]
    looked_at = cat([t for w in range(count) for t in (right[w], left[w])])
    keys = side_by_side(looked_at, wk_ref[...])
    values = dot(wqv_ref[128:256, :], looked_at, NT).astype(BF16)
    wanted = cat([nb_ref[32:n, :], nb_ref[0:32, :]])
    queries = dot(wqv_ref[0:128, :], wanted, NT).astype(BF16)
    masks = [mask(w, s) for w in "12" for s in ("left", "right")]
    units = [([w, w + 1], masks, bias_b[...]) for w in range(1, count - 2, 2)]
    masks = masks[0:2] + [mask("2", v, s) for v in ("up", "down") for s in ("left", "right")]
    units.append(([count - 2, count - 1, 0], masks, bias_bv[...]))
    context = attention(queries, keys, values, units)
    z = cat([fb_ref[32:n, :], fb_ref[0:32, :]])
    out = finish(z, context, wo_ref[1], hg_ref[1:2, :], we_ref[1], ws_ref[1])
    out = half_turn(out)
    rows = n // 8
    out = cat([out[rows - 4 :], out[: rows - 4]])
    inner = oa_ref[...].reshape(rows, 8, 128)
    low = low_half(out.shape)
    out_ref[:, 0:8, :] = jnp.where(low, out, inner)
    out_ref[:, 8:16, :] = jnp.where(low, inner, out)


def vmem(count):
    return [pl.BlockSpec(memory_space=pltpu.VMEM)] * count


def call(kernel, name, operands, outs, scratch=(), flops=0, aliases=None):
    shapes = [jax.ShapeDtypeStruct(shape, dtype) for shape, dtype in outs]
    return pl.pallas_call(
        kernel,
        out_shape=shapes,
        in_specs=vmem(len(operands)),
        out_specs=vmem(len(outs)),
        scratch_shapes=list(scratch),
        input_output_aliases=aliases or {},
        compiler_params=pltpu.CompilerParams(vmem_limit_bytes=32 * 1024 * 1024),
        cost_estimate=pl.CostEstimate(flops=flops, bytes_accessed=1 << 20, transcendentals=0),
        name=name,
    )(*operands)


def on_device(x, ag, tw, ow, pb, hg, ew, sw):
    height, breadth = x.shape[0], x.shape[1]
    n = height * WIN
    table = ((64, HEADS * 128), F32)
    prepared = [((256, 128), BF16), ((256, 256), BF16)]
    weights = (x, tw, ow, ew, sw, ag, pb, hg)
    kept = [((n, C), F32)] * 2 + [((n, C), BF16)] * 2 + [((n // 2, C), BF16)] * 2 + [table] + prepared
    rows = [((WIN, breadth, C), BF16)] * 2
    (parity,) = call(parity_kernel, "parity", (), [((8, 128), jnp.int32)], (), 4 * 10**10)
    odd, even = call(
        edge_rows_kernel, "edge_rows", (x, parity, ag, pb, hg), rows, [pltpu.SemaphoreType.DMA((2,))]
    )

    def run(*operands):
        return call(first_kernel, "first", operands, rows + kept, (), 4 * 10**9, {8: 0, 9: 1})

    def skip(*operands):
        return call(nothing_kernel, "nothing", operands[8:10], rows + kept, (), 0, {0: 0, 1: 1})

    odd, even, *state = lax.cond(goes_first(), run, skip, *weights, odd, even)
    even, odd = swap(even, "gy", 0), swap(odd, "gy", 1)
    state = call(
        second_kernel, "second", (*weights, *state), kept, (), 4 * 10**9, {8 + i: i for i in range(9)}
    )
    fa, fb, na, nb, right, left, bias, wqv, wk = state
    va, vb, odd, even = call(
        halo_kernel, "halo", (odd, even, right, left, bias, wqv, wk, ow, ew, sw, ag, hg),
        [((64, C), BF16)] * 2 + [((n // 2 + 32, C), BF16)] * 2, (), 10**9,
    )
    odd, even = swap(odd, "gx", 1), swap(even, "gx", 0)
    oa, bias_b, bias_bv, wqv, wk = call(
        middle_kernel, "middle", (fa, na, va, pb, tw, ow, ew, sw, hg),
        [((n, C), F32), table, table] + prepared, [pltpu.VMEM(*table)] * 2, 2 * 10**9,
    )
    return call(
        outer_kernel, "outer", (fb, nb, vb, odd, even, oa, bias_b, bias_bv, wqv, wk, ow, ew, sw, hg),
        [((height, breadth, C), F32)], (), 2 * 10**9,
    )[0]


def solution(mesh):
    return jax.shard_map(
        on_device,
        mesh=mesh,
        in_specs=(P("gy", "gx", None), P(), P(), P(), P(), P(), P(), P()),
        out_specs=P("gy", "gx", None),
        check_vma=False,
    )
```

```python
import math

import jax
import jax.numpy as jnp
from jax import lax
from jax.experimental import pallas as pl
from jax.experimental.pallas import tpu as pltpu
from jax.sharding import PartitionSpec as P

C = 128
HEADS = 4
HID = 512
WIN = 8
HD = 32
EPSILON = 1e-05
LOG2E = math.log2(math.e)
SCALE = HD ** (-0.5) * LOG2E
F32 = jnp.float32
BF16 = jnp.bfloat16
NT = (((1,), (1,)), ((), ()))
TN = (((0,), (0,)), ((), ()))
CHUNK = 256


def swap(x, axis, first):
    length = lax.axis_size(axis)
    there = [(i, (i + 1) % length) for i in range(first, length, 2)]
    return lax.ppermute(x, axis, there + [(b, a) for a, b in there])


def iota(shape, dim):
    return lax.broadcasted_iota(jnp.int32, shape, dim)


def dot(a, b, dims=None):
    if dims is None:
        return jnp.dot(a, b, preferred_element_type=F32)
    return lax.dot_general(a, b, dims, preferred_element_type=F32)


def cat(parts, axis=0):
    return jnp.concatenate(parts, axis=axis)


def layer_norm(x, gain):
    center = x - jnp.mean(x, axis=-1, keepdims=True)
    spread = jnp.sum(center * center, axis=-1, keepdims=True)
    return center * lax.rsqrt(spread + C * EPSILON) * (gain * C**0.5)


def twice_gelu(x):
    return x + x * lax.erf(x * (0.5**0.5))


def bias_rows(pb_ref, block):
    sub = iota((8, 128), 0)
    lane = iota((8, 128), 1)
    place = lax.min((lane >> 3) * 15 + 7 + (lane & 7) - sub, 224)
    for head in range(HEADS):
        low = jnp.broadcast_to(pb_ref[block, head : head + 1, 0:128], (8, 128))
        high = jnp.broadcast_to(pb_ref[block, head : head + 1, 97:225], (8, 128))
        strip = jnp.where(
            place < 128,
            jnp.take_along_axis(low, lax.min(place, 127), axis=1),
            jnp.take_along_axis(high, lax.max(place - 97, 0), axis=1),
        )
        strip = strip * LOG2E
        for yj in range(8):
            turn = (128 - (7 - yj) * 8) % 128
            first = pltpu.roll(strip, turn, 1) if turn else strip
            second = pltpu.roll(strip, (turn + 64) % 128, 1)
            yield head, yj, jnp.where(lane < 64, first, second)


def fill_weights(w, wqv, wk):
    wqv[0:128, :] = jnp.transpose(w[:, 0:128].astype(F32)).astype(BF16)
    wqv[128:256, :] = jnp.transpose(w[:, 256:384].astype(F32)).astype(BF16)
    keys = w[:, 128:256].astype(F32)
    turned = pltpu.roll(keys, 64, 1)
    lane = iota((128, 128), 1)
    zero = jnp.zeros((128, 128), F32)
    wk[0:128, 0:128] = jnp.where(lane < 64, keys, zero).astype(BF16)
    wk[0:128, 128:256] = jnp.where(lane < 64, turned, zero).astype(BF16)
    wk[128:256, 0:128] = jnp.where(lane >= 64, turned, zero).astype(BF16)
    wk[128:256, 128:256] = jnp.where(lane >= 64, keys, zero).astype(BF16)


def mask(*conditions):
    lane = iota((64, 128), 1)
    sides = {"1": lane < 64, "2": lane >= 64, "up": (lane & 32) == 0, "down": (lane & 32) > 0}
    sides |= {"left": (lane & 4) == 0, "right": (lane & 4) > 0}
    keep = sides[conditions[0]]
    for name in conditions[1:]:
        keep = keep & sides[name]
    return jnp.where(keep, 1.0, 0.0).astype(BF16)


def side_by_side(tokens, wk):
    pairs = tokens.reshape(-1, 2, 64, 128)
    lanes = cat([cat([pairs[p, 0], pairs[p, 1]], 1) for p in range(pairs.shape[0])])
    return dot(lanes, wk).astype(BF16)


def attention(queries, keys, values, units):
    zero = jnp.zeros((32, 128), BF16)
    scores = []
    for u, (pairs, masks, bias) in enumerate(units):
        q = queries[:, 128 * u : 128 * u + 128]
        for half in range(2):
            r = 64 * half
            rows = []
            for m in masks:
                rows.append(cat([q[r : r + 32] * m[0:32], zero], 1))
                rows.append(cat([zero, q[r + 32 : r + 64] * m[0:32]], 1))
            k = cat([keys[64 * p : 64 * p + 64, 128 * half : 128 * half + 128] for p in pairs], 1)
            scores.append(dot(k, cat(rows)))
    for u, (pairs, masks, bias) in enumerate(units):
        for half in range(2):
            s = scores[2 * u + half] * SCALE + bias[:, 256 * half : 256 * half + 256]
            p = jnp.exp2(s - jnp.max(s, axis=0, keepdims=True))
            part = 1.0 / jnp.sum(p, axis=0, keepdims=True)
            scores[2 * u + half] = (p * part).astype(BF16)
    context = []
    for u, (pairs, masks, bias) in enumerate(units):
        out = []
        for half in range(2):
            r = 64 * half
            p = scores[2 * u + half]
            seen = cat([cat([p[:, 0:128] * m, p[:, 128:256] * m], 1) for m in masks])
            v = cat([values[r : r + 64, 128 * j : 128 * j + 128] for j in pairs], 1)
            ct = dot(v, seen)
            out += [ct[0:32, 0:128], ct[32:64, 128:256]]
        context.append(cat(out).astype(BF16))
    return cat(context, 1)


def finish(z, context, wo, gain, we, ws):
    middle = z + dot(context, wo, TN).astype(BF16).astype(F32)
    normed = layer_norm(middle, gain).astype(BF16)
    size = min(CHUNK, z.shape[0])
    hidden = [dot(normed[i : i + size], we) for i in range(0, z.shape[0], size)]
    hidden = [twice_gelu(h).astype(BF16) for h in hidden]
    return middle + 0.5 * cat([dot(h, ws) for h in hidden])


def half_turn(x):
    return pltpu.roll(x.reshape(-1, 8, 128), 4, 1)


def low_half(shape):
    return iota(shape, 1) < 4


def windows_of(block):
    parts = block.astype(F32).reshape(8, 2, 8, 128)
    return [parts[:, 0].reshape(64, 128), parts[:, 1].reshape(64, 128)]


def shifted_columns(tokens):
    pairs = tokens.reshape(-1, 2, 64, 128)
    a, b = half_turn(pairs[:, 0]), half_turn(pairs[:, 1])
    low = low_half(a.shape)
    return jnp.where(low, a, b).reshape(-1, 128), jnp.where(low, b, a).reshape(-1, 128)


def edges(outer):
    pairs = outer.reshape(-1, 2, 8, 128)
    even, odd = pairs[:, 0], pairs[:, 1]
    low = low_half(even.shape)
    right = jnp.where(low, even, pltpu.roll(odd, 4, 1)).reshape(-1, 128)
    left = jnp.where(low, pltpu.roll(even, 4, 1), odd).reshape(-1, 128)
    return right.astype(BF16), left.astype(BF16)


def goes_first():
    row, rows = lax.axis_index("gy"), lax.axis_size("gy")
    return lax.rem(row, rows // 2) < rows // 4


def own_block(
    x_ref, w_ref, wo_ref, we_ref, ws_ref, ag_ref, pb_ref, hg_ref,
    fa_ref, fb_ref, na_ref, nb_ref, right_ref, left_ref, bias_ref, wqv_ref, wk_ref,
):
    for head, yj, values in bias_rows(pb_ref, 0):
        bias_ref[yj * 8 : yj * 8 + 8, head * 128 : head * 128 + 128] = values
    fill_weights(w_ref[0], wqv_ref, wk_ref)
    bands = x_ref.shape[0] // WIN
    z = cat([t for b in range(bands) for t in windows_of(x_ref[WIN * b : WIN * b + WIN])])
    normed = layer_norm(z, ag_ref[0:1, :]).astype(BF16)
    qv = dot(wqv_ref[...], normed, NT).astype(BF16)
    keys = side_by_side(normed, wk_ref[...])
    masks = [mask("1"), mask("2")]
    units = [([b], masks, bias_ref[...]) for b in range(bands)]
    context = attention(qv[0:128], keys, qv[128:256], units)
    out = finish(z, context, wo_ref[0], hg_ref[0:1, :], we_ref[0], ws_ref[0])
    fa_ref[...], fb_ref[...] = shifted_columns(out)
    na, nb = shifted_columns(layer_norm(out, ag_ref[1:2, :]))
    na_ref[...] = na.astype(BF16)
    nb_ref[...] = nb.astype(BF16)
    right_ref[...], left_ref[...] = edges(nb)


def parity_kernel(out_ref):
    out_ref[...] = jnp.full(out_ref.shape, lax.rem(lax.axis_index("gy"), 2), jnp.int32)


def edge_rows_kernel(x_ref, parity_ref, ag_ref, pb_ref, hg_ref, odd_ref, even_ref, sems):
    bottom = x_ref.shape[0] - WIN
    is_odd = parity_ref[0, 0]
    copies = [
        pltpu.make_async_copy(x_ref.at[pl.ds(is_odd * bottom, WIN)], odd_ref, sems.at[0]),
        pltpu.make_async_copy(x_ref.at[pl.ds((1 - is_odd) * bottom, WIN)], even_ref, sems.at[1]),
    ]
    for copy in copies:
        copy.start()
    for copy in copies:
        copy.wait()


def first_kernel(*refs):
    own_block(*refs[0:8], *refs[10:])


def nothing_kernel(*refs):
    pass


def second_kernel(*refs):
    @pl.when(jnp.logical_not(goes_first()))
    def _():
        own_block(*refs[0:8], *refs[17:])


def halo_kernel(
    rows_even_ref, rows_odd_ref, own_right_ref, own_left_ref, bias_ref, wqv_ref, wk_ref, wo_ref, we_ref, ws_ref, ag_ref, hg_ref,
    na_ref, nb_ref, cols_odd_ref, cols_even_ref,
):
    row_odd = lax.rem(lax.axis_index("gy"), 2) == 1
    rows_odd, rows_even = rows_odd_ref[...].astype(F32), rows_even_ref[...].astype(F32)
    down = jnp.where(row_odd, rows_odd, rows_even)
    up = jnp.where(row_odd, rows_even, rows_odd)
    z = cat(windows_of(down) + windows_of(up))
    normed = layer_norm(z, ag_ref[0:1, :]).astype(BF16)
    keys = side_by_side(normed, wk_ref[...])
    values = dot(wqv_ref[128:256, :], normed, NT).astype(BF16)

    def wanted(t):
        return cat([t[0:32], t[160:192], t[64:96], t[224:256]])

    queries = dot(wqv_ref[0:128, :], wanted(normed), NT).astype(BF16)
    masks = [mask("1", "up"), mask("2", "up"), mask("1", "down"), mask("2", "down")]
    context = attention(queries, keys, values, [([0, 1], masks, bias_ref[...])])
    out = finish(wanted(z), context, wo_ref[0], hg_ref[0:1, :], we_ref[0], ws_ref[0])
    na, nb = shifted_columns(layer_norm(out, ag_ref[1:2, :]))
    na_ref[...] = na.astype(BF16)
    nb_ref[...] = nb.astype(BF16)
    right, left = edges(nb)
    n = own_right_ref.shape[0]
    col_odd = lax.rem(lax.axis_index("gx"), 2) == 1
    for at, size, a, b in [(0, n, own_right_ref[...], own_left_ref[...]), (n, 32, right, left)]:
        a, b = a.astype(F32), b.astype(F32)
        cols_odd_ref[at : at + size, :] = jnp.where(col_odd, a, b).astype(BF16)
        cols_even_ref[at : at + size, :] = jnp.where(col_odd, b, a).astype(BF16)


def middle_kernel(
    fa_ref, na_ref, va_ref, pb_ref, w_ref, wo_ref, we_ref, ws_ref, hg_ref,
    out_ref, bias_b, bias_bv, wqv_ref, wk_ref,
    bias_a, bias_av,
):
    sub = iota((8, 128), 0)
    lane = iota((8, 128), 1)
    query_left = (lane & 4) == 0
    query_up = (lane & 32) == 0
    row, col = lax.axis_index("gy"), lax.axis_index("gx")
    last_col = jnp.where(query_left, lax.axis_size("gx") - 1, 0) == col
    last_row = jnp.where(query_up, lax.axis_size("gy") - 1, 0) == row
    cut_col = last_col & (query_left != (sub < 4))
    for head, yj, values in bias_rows(pb_ref, 1):
        at = (slice(yj * 8, yj * 8 + 8), slice(head * 128, head * 128 + 128))
        cut = values - 100.0 * LOG2E
        cut_row = (lane >= 64) & last_row & (jnp.logical_not(query_up) if yj < 4 else query_up)
        bias_a[at] = values
        bias_av[at] = jnp.where(cut_row, cut, values)
        bias_b[at] = jnp.where(cut_col, cut, values)
        bias_bv[at] = jnp.where(cut_row | cut_col, cut, values)
    fill_weights(w_ref[1], wqv_ref, wk_ref)
    n = na_ref.shape[0]
    inner = na_ref[32 : n - 32, :]
    first = cat([va_ref[32:64, :], na_ref[0:32, :]])
    last = cat([na_ref[n - 32 : n, :], va_ref[0:32, :]])
    looked_at = cat([inner, last, first, first])
    keys = side_by_side(looked_at, wk_ref[...])
    values = dot(wqv_ref[128:256, :], looked_at, NT).astype(BF16)
    wanted = cat([na_ref[32:n, :], na_ref[0:32, :]])
    queries = dot(wqv_ref[0:128, :], wanted, NT).astype(BF16)
    last_unit = n // 128 - 1
    masks = [mask("1"), mask("2")]
    units = [([u], masks, bias_a[...]) for u in range(last_unit)]
    masks = [mask("1"), mask("2", "up"), mask("2", "down"), jnp.zeros((64, 128), BF16)]
    units.append(([last_unit, last_unit + 1], masks, bias_av[...]))
    context = attention(queries, keys, values, units)
    z = cat([fa_ref[32:n, :], fa_ref[0:32, :]])
    out = finish(z, context, wo_ref[1], hg_ref[1:2, :], we_ref[1], ws_ref[1])
    out = half_turn(out).reshape(n, 128)
    out_ref[32:n, :] = out[0 : n - 32]
    out_ref[0:32, :] = out[n - 32 : n]


def outer_kernel(
    fb_ref, nb_ref, vb_ref, cols_odd_ref, cols_even_ref, oa_ref, bias_b, bias_bv, wqv_ref, wk_ref, wo_ref, we_ref, ws_ref, hg_ref,
    out_ref,
):
    n = nb_ref.shape[0]
    h = n // 2

    def in_order(ref, end, size):
        rows = cat([ref[end + size : end + 2 * size, :], ref[0:end, :], ref[end : end + size, :]])
        return rows.astype(F32).reshape(-1, 8, 128)

    own = cat([vb_ref[32:64, :], nb_ref[...], vb_ref[0:32, :]]).astype(F32).reshape(-1, 8, 128)
    odd, even = in_order(cols_odd_ref, h, 16), in_order(cols_even_ref, h, 16)
    col_odd = lax.rem(lax.axis_index("gx"), 2) == 1
    hl, hr = jnp.where(col_odd, even, odd), jnp.where(col_odd, odd, even)
    low = low_half(hl.shape)
    even = jnp.where(low, hl, pltpu.roll(hr, 4, 1))
    odd = jnp.where(low, pltpu.roll(hl, 4, 1), hr)
    halo = jnp.stack([even, odd], axis=1).reshape(own.shape)
    low = low_half(own.shape)
    right = jnp.where(low, own, halo).reshape(-1, 64, 128).astype(BF16)
    left = jnp.where(low, halo, own).reshape(-1, 64, 128).astype(BF16)
    count = right.shape[0]
    looked_at = cat([t for w in range(count) for t in (right[w], left[w])])
    keys = side_by_side(looked_at, wk_ref[...])
    values = dot(wqv_ref[128:256, :], looked_at, NT).astype(BF16)
    wanted = cat([nb_ref[32:n, :], nb_ref[0:32, :]])
    queries = dot(wqv_ref[0:128, :], wanted, NT).astype(BF16)
    masks = [mask(w, s) for w in "12" for s in ("left", "right")]
    units = [([w, w + 1], masks, bias_b[...]) for w in range(1, count - 2, 2)]
    masks = masks[0:2] + [mask("2", v, s) for v in ("up", "down") for s in ("left", "right")]
    units.append(([count - 2, count - 1, 0], masks, bias_bv[...]))
    context = attention(queries, keys, values, units)
    z = cat([fb_ref[32:n, :], fb_ref[0:32, :]])
    out = finish(z, context, wo_ref[1], hg_ref[1:2, :], we_ref[1], ws_ref[1])
    out = half_turn(out)
    rows = n // 8
    out = cat([out[rows - 4 :], out[: rows - 4]])
    inner = oa_ref[...].reshape(rows, 8, 128)
    low = low_half(out.shape)
    out_ref[:, 0:8, :] = jnp.where(low, out, inner)
    out_ref[:, 8:16, :] = jnp.where(low, inner, out)


def vmem(count):
    return [pl.BlockSpec(memory_space=pltpu.VMEM)] * count


def call(kernel, name, operands, outs, scratch=(), flops=0, aliases=None):
    shapes = [jax.ShapeDtypeStruct(shape, dtype) for shape, dtype in outs]
    return pl.pallas_call(
        kernel,
        out_shape=shapes,
        in_specs=vmem(len(operands)),
        out_specs=vmem(len(outs)),
        scratch_shapes=list(scratch),
        input_output_aliases=aliases or {},
        compiler_params=pltpu.CompilerParams(vmem_limit_bytes=32 * 1024 * 1024),
        cost_estimate=pl.CostEstimate(flops=flops, bytes_accessed=1 << 20, transcendentals=0),
        name=name,
    )(*operands)


def on_device(x, ag, tw, ow, pb, hg, ew, sw):
    height, breadth = x.shape[0], x.shape[1]
    n = height * WIN
    table = ((64, HEADS * 128), F32)
    prepared = [((256, 128), BF16), ((256, 256), BF16)]
    weights = (x, tw, ow, ew, sw, ag, pb, hg)
    kept = [((n, C), F32)] * 2 + [((n, C), BF16)] * 2 + [((n // 2, C), BF16)] * 2 + [table] + prepared
    rows = [((WIN, breadth, C), BF16)] * 2
    (parity,) = call(parity_kernel, "parity", (), [((8, 128), jnp.int32)], (), 4 * 10**10)
    odd, even = call(
        edge_rows_kernel, "edge_rows", (x, parity, ag, pb, hg), rows, [pltpu.SemaphoreType.DMA((2,))]
    )

    def run(*operands):
        return call(first_kernel, "first", operands, rows[0:1] + kept, (), 4 * 10**9, {8: 0})

    def skip(*operands):
        return call(nothing_kernel, "nothing", operands[8:9], rows[0:1] + kept, (), 0, {0: 0})

    even = swap(even, "gy", 0)
    odd, *state = lax.cond(goes_first(), run, skip, *weights, odd)
    odd = swap(odd, "gy", 1)
    state = call(
        second_kernel, "second", (*weights, *state), kept, (), 4 * 10**9, {8 + i: i for i in range(9)}
    )
    fa, fb, na, nb, right, left, bias, wqv, wk = state
    va, vb, odd, even = call(
        halo_kernel, "halo", (even, odd, right, left, bias, wqv, wk, ow, ew, sw, ag, hg),
        [((64, C), BF16)] * 2 + [((n // 2 + 32, C), BF16)] * 2, (), 10**9,
    )
    odd, even = swap(odd, "gx", 1), swap(even, "gx", 0)
    oa, bias_b, bias_bv, wqv, wk = call(
        middle_kernel, "middle", (fa, na, va, pb, tw, ow, ew, sw, hg),
        [((n, C), F32), table, table] + prepared, [pltpu.VMEM(*table)] * 2, 2 * 10**9,
    )
    return call(
        outer_kernel, "outer", (fb, nb, vb, odd, even, oa, bias_b, bias_bv, wqv, wk, ow, ew, sw, hg),
        [((height, breadth, C), F32)], (), 2 * 10**9,
    )[0]


def solution(mesh):
    return jax.shard_map(
        on_device,
        mesh=mesh,
        in_specs=(P("gy", "gx", None), P(), P(), P(), P(), P(), P(), P()),
        out_specs=P("gy", "gx", None),
        check_vma=False,
    )
```

```python
import math

import jax
import jax.numpy as jnp
from jax import lax
from jax.experimental import pallas as pl
from jax.experimental.pallas import tpu as pltpu
from jax.sharding import PartitionSpec as P

C = 128
HEADS = 4
HID = 512
WIN = 8
HD = 32
EPSILON = 1e-05
LOG2E = math.log2(math.e)
SCALE = HD ** (-0.5) * LOG2E
F32 = jnp.float32
BF16 = jnp.bfloat16
NT = (((1,), (1,)), ((), ()))
TN = (((0,), (0,)), ((), ()))
CHUNK = 256


def shift(x, axis, by):
    length = lax.axis_size(axis)
    return lax.ppermute(x, axis, [(i, (i + by) % length) for i in range(length)])


def swap(x, axis, first):
    length = lax.axis_size(axis)
    there = [(i, (i + 1) % length) for i in range(first, length, 2)]
    return lax.ppermute(x, axis, there + [(b, a) for a, b in there])


def iota(shape, dim):
    return lax.broadcasted_iota(jnp.int32, shape, dim)


def dot(a, b, dims=None):
    if dims is None:
        return jnp.dot(a, b, preferred_element_type=F32)
    return lax.dot_general(a, b, dims, preferred_element_type=F32)


def cat(parts, axis=0):
    return jnp.concatenate(parts, axis=axis)


def layer_norm(x, gain):
    center = x - jnp.mean(x, axis=-1, keepdims=True)
    spread = jnp.sum(center * center, axis=-1, keepdims=True)
    return center * lax.rsqrt(spread + C * EPSILON) * (gain * C**0.5)


def twice_gelu(x):
    return x + x * lax.erf(x * (0.5**0.5))


def bias_rows(pb_ref, block):
    sub = iota((8, 128), 0)
    lane = iota((8, 128), 1)
    place = lax.min((lane >> 3) * 15 + 7 + (lane & 7) - sub, 224)
    for head in range(HEADS):
        low = jnp.broadcast_to(pb_ref[block, head : head + 1, 0:128], (8, 128))
        high = jnp.broadcast_to(pb_ref[block, head : head + 1, 97:225], (8, 128))
        strip = jnp.where(
            place < 128,
            jnp.take_along_axis(low, lax.min(place, 127), axis=1),
            jnp.take_along_axis(high, lax.max(place - 97, 0), axis=1),
        )
        strip = strip * LOG2E
        for yj in range(8):
            turn = (128 - (7 - yj) * 8) % 128
            first = pltpu.roll(strip, turn, 1) if turn else strip
            second = pltpu.roll(strip, (turn + 64) % 128, 1)
            yield head, yj, jnp.where(lane < 64, first, second)


def fill_weights(w, wqv, wk):
    wqv[0:128, :] = jnp.transpose(w[:, 0:128].astype(F32)).astype(BF16)
    wqv[128:256, :] = jnp.transpose(w[:, 256:384].astype(F32)).astype(BF16)
    keys = w[:, 128:256].astype(F32)
    turned = pltpu.roll(keys, 64, 1)
    lane = iota((128, 128), 1)
    zero = jnp.zeros((128, 128), F32)
    wk[0:128, 0:128] = jnp.where(lane < 64, keys, zero).astype(BF16)
    wk[0:128, 128:256] = jnp.where(lane < 64, turned, zero).astype(BF16)
    wk[128:256, 0:128] = jnp.where(lane >= 64, turned, zero).astype(BF16)
    wk[128:256, 128:256] = jnp.where(lane >= 64, keys, zero).astype(BF16)


def mask(*conditions):
    lane = iota((64, 128), 1)
    sides = {"1": lane < 64, "2": lane >= 64, "up": (lane & 32) == 0, "down": (lane & 32) > 0}
    sides |= {"left": (lane & 4) == 0, "right": (lane & 4) > 0}
    keep = sides[conditions[0]]
    for name in conditions[1:]:
        keep = keep & sides[name]
    return jnp.where(keep, 1.0, 0.0).astype(BF16)


def side_by_side(tokens, wk):
    pairs = tokens.reshape(-1, 2, 64, 128)
    lanes = cat([cat([pairs[p, 0], pairs[p, 1]], 1) for p in range(pairs.shape[0])])
    return dot(lanes, wk).astype(BF16)


def attention(queries, keys, values, units):
    zero = jnp.zeros((32, 128), BF16)
    scores = []
    for u, (pairs, masks, bias) in enumerate(units):
        q = queries[:, 128 * u : 128 * u + 128]
        for half in range(2):
            r = 64 * half
            rows = []
            for m in masks:
                rows.append(cat([q[r : r + 32] * m[0:32], zero], 1))
                rows.append(cat([zero, q[r + 32 : r + 64] * m[0:32]], 1))
            k = cat([keys[64 * p : 64 * p + 64, 128 * half : 128 * half + 128] for p in pairs], 1)
            scores.append(dot(k, cat(rows)))
    for u, (pairs, masks, bias) in enumerate(units):
        for half in range(2):
            s = scores[2 * u + half] * SCALE + bias[:, 256 * half : 256 * half + 256]
            p = jnp.exp2(s - jnp.max(s, axis=0, keepdims=True))
            part = 1.0 / jnp.sum(p, axis=0, keepdims=True)
            scores[2 * u + half] = (p * part).astype(BF16)
    context = []
    for u, (pairs, masks, bias) in enumerate(units):
        out = []
        for half in range(2):
            r = 64 * half
            p = scores[2 * u + half]
            seen = cat([cat([p[:, 0:128] * m, p[:, 128:256] * m], 1) for m in masks])
            v = cat([values[r : r + 64, 128 * j : 128 * j + 128] for j in pairs], 1)
            ct = dot(v, seen)
            out += [ct[0:32, 0:128], ct[32:64, 128:256]]
        context.append(cat(out).astype(BF16))
    return cat(context, 1)


def finish(z, context, wo, gain, we, ws):
    middle = z + dot(context, wo, TN).astype(BF16).astype(F32)
    normed = layer_norm(middle, gain).astype(BF16)
    size = min(CHUNK, z.shape[0])
    hidden = [dot(normed[i : i + size], we) for i in range(0, z.shape[0], size)]
    hidden = [twice_gelu(h).astype(BF16) for h in hidden]
    return middle + 0.5 * cat([dot(h, ws) for h in hidden])


def half_turn(x):
    return pltpu.roll(x.reshape(-1, 8, 128), 4, 1)


def low_half(shape):
    return iota(shape, 1) < 4


def windows_of(block):
    parts = block.astype(F32).reshape(8, 2, 8, 128)
    return [parts[:, 0].reshape(64, 128), parts[:, 1].reshape(64, 128)]


def shifted_columns(tokens):
    pairs = tokens.reshape(-1, 2, 64, 128)
    a, b = half_turn(pairs[:, 0]), half_turn(pairs[:, 1])
    low = low_half(a.shape)
    return jnp.where(low, a, b).reshape(-1, 128), jnp.where(low, b, a).reshape(-1, 128)


def edges(outer):
    pairs = outer.reshape(-1, 2, 8, 128)
    even, odd = pairs[:, 0], pairs[:, 1]
    low = low_half(even.shape)
    right = jnp.where(low, even, pltpu.roll(odd, 4, 1)).reshape(-1, 128)
    left = jnp.where(low, pltpu.roll(even, 4, 1), odd).reshape(-1, 128)
    return right.astype(BF16), left.astype(BF16)


def goes_first():
    row, rows = lax.axis_index("gy"), lax.axis_size("gy")
    return lax.rem(row, rows // 2) < rows // 8


def own_block(
    x_ref, w_ref, wo_ref, we_ref, ws_ref, ag_ref, pb_ref, hg_ref,
    fa_ref, fb_ref, na_ref, nb_ref, right_ref, left_ref, bias_ref, wqv_ref, wk_ref,
):
    for head, yj, values in bias_rows(pb_ref, 0):
        bias_ref[yj * 8 : yj * 8 + 8, head * 128 : head * 128 + 128] = values
    fill_weights(w_ref[0], wqv_ref, wk_ref)
    bands = x_ref.shape[0] // WIN
    z = cat([t for b in range(bands) for t in windows_of(x_ref[WIN * b : WIN * b + WIN])])
    normed = layer_norm(z, ag_ref[0:1, :]).astype(BF16)
    qv = dot(wqv_ref[...], normed, NT).astype(BF16)
    keys = side_by_side(normed, wk_ref[...])
    masks = [mask("1"), mask("2")]
    units = [([b], masks, bias_ref[...]) for b in range(bands)]
    context = attention(qv[0:128], keys, qv[128:256], units)
    out = finish(z, context, wo_ref[0], hg_ref[0:1, :], we_ref[0], ws_ref[0])
    fa_ref[...], fb_ref[...] = shifted_columns(out)
    na, nb = shifted_columns(layer_norm(out, ag_ref[1:2, :]))
    na_ref[...] = na.astype(BF16)
    nb_ref[...] = nb.astype(BF16)
    right_ref[...], left_ref[...] = edges(nb)


def start_kernel(out_ref):
    out_ref[...] = jnp.zeros(out_ref.shape, jnp.int32)


def edge_rows_kernel(x_ref, start_ref, ag_ref, pb_ref, hg_ref, last_ref, first_ref, sems):
    bottom = x_ref.shape[0] - WIN
    copies = [
        pltpu.make_async_copy(x_ref.at[pl.ds(bottom, WIN)], last_ref, sems.at[0]),
        pltpu.make_async_copy(x_ref.at[pl.ds(0, WIN)], first_ref, sems.at[1]),
    ]
    for copy in copies:
        copy.start()
    for copy in copies:
        copy.wait()


def first_kernel(*refs):
    own_block(*refs[0:8], *refs[10:])


def nothing_kernel(*refs):
    pass


def second_kernel(*refs):
    @pl.when(jnp.logical_not(goes_first()))
    def _():
        own_block(*refs[0:8], *refs[17:])


def halo_kernel(
    up_ref, down_ref, own_right_ref, own_left_ref, bias_ref, wqv_ref, wk_ref, wo_ref, we_ref, ws_ref, ag_ref, hg_ref,
    na_ref, nb_ref, cols_odd_ref, cols_even_ref,
):
    z = cat(windows_of(down_ref[...]) + windows_of(up_ref[...]))
    normed = layer_norm(z, ag_ref[0:1, :]).astype(BF16)
    keys = side_by_side(normed, wk_ref[...])
    values = dot(wqv_ref[128:256, :], normed, NT).astype(BF16)

    def wanted(t):
        return cat([t[0:32], t[160:192], t[64:96], t[224:256]])

    queries = dot(wqv_ref[0:128, :], wanted(normed), NT).astype(BF16)
    masks = [mask("1", "up"), mask("2", "up"), mask("1", "down"), mask("2", "down")]
    context = attention(queries, keys, values, [([0, 1], masks, bias_ref[...])])
    out = finish(wanted(z), context, wo_ref[0], hg_ref[0:1, :], we_ref[0], ws_ref[0])
    na, nb = shifted_columns(layer_norm(out, ag_ref[1:2, :]))
    na_ref[...] = na.astype(BF16)
    nb_ref[...] = nb.astype(BF16)
    right, left = edges(nb)
    n = own_right_ref.shape[0]
    col_odd = lax.rem(lax.axis_index("gx"), 2) == 1
    for at, size, a, b in [(0, n, own_right_ref[...], own_left_ref[...]), (n, 32, right, left)]:
        a, b = a.astype(F32), b.astype(F32)
        cols_odd_ref[at : at + size, :] = jnp.where(col_odd, a, b).astype(BF16)
        cols_even_ref[at : at + size, :] = jnp.where(col_odd, b, a).astype(BF16)


def middle_kernel(
    fa_ref, na_ref, va_ref, pb_ref, w_ref, wo_ref, we_ref, ws_ref, hg_ref,
    out_ref, bias_b, bias_bv, wqv_ref, wk_ref,
    bias_a, bias_av,
):
    sub = iota((8, 128), 0)
    lane = iota((8, 128), 1)
    query_left = (lane & 4) == 0
    query_up = (lane & 32) == 0
    row, col = lax.axis_index("gy"), lax.axis_index("gx")
    last_col = jnp.where(query_left, lax.axis_size("gx") - 1, 0) == col
    last_row = jnp.where(query_up, lax.axis_size("gy") - 1, 0) == row
    cut_col = last_col & (query_left != (sub < 4))
    for head, yj, values in bias_rows(pb_ref, 1):
        at = (slice(yj * 8, yj * 8 + 8), slice(head * 128, head * 128 + 128))
        cut = values - 100.0 * LOG2E
        cut_row = (lane >= 64) & last_row & (jnp.logical_not(query_up) if yj < 4 else query_up)
        bias_a[at] = values
        bias_av[at] = jnp.where(cut_row, cut, values)
        bias_b[at] = jnp.where(cut_col, cut, values)
        bias_bv[at] = jnp.where(cut_row | cut_col, cut, values)
    fill_weights(w_ref[1], wqv_ref, wk_ref)
    n = na_ref.shape[0]
    inner = na_ref[32 : n - 32, :]
    first = cat([va_ref[32:64, :], na_ref[0:32, :]])
    last = cat([na_ref[n - 32 : n, :], va_ref[0:32, :]])
    looked_at = cat([inner, last, first, first])
    keys = side_by_side(looked_at, wk_ref[...])
    values = dot(wqv_ref[128:256, :], looked_at, NT).astype(BF16)
    wanted = cat([na_ref[32:n, :], na_ref[0:32, :]])
    queries = dot(wqv_ref[0:128, :], wanted, NT).astype(BF16)
    last_unit = n // 128 - 1
    masks = [mask("1"), mask("2")]
    units = [([u], masks, bias_a[...]) for u in range(last_unit)]
    masks = [mask("1"), mask("2", "up"), mask("2", "down"), jnp.zeros((64, 128), BF16)]
    units.append(([last_unit, last_unit + 1], masks, bias_av[...]))
    context = attention(queries, keys, values, units)
    z = cat([fa_ref[32:n, :], fa_ref[0:32, :]])
    out = finish(z, context, wo_ref[1], hg_ref[1:2, :], we_ref[1], ws_ref[1])
    out = half_turn(out).reshape(n, 128)
    out_ref[32:n, :] = out[0 : n - 32]
    out_ref[0:32, :] = out[n - 32 : n]


def outer_kernel(
    fb_ref, nb_ref, vb_ref, cols_odd_ref, cols_even_ref, oa_ref, bias_b, bias_bv, wqv_ref, wk_ref, wo_ref, we_ref, ws_ref, hg_ref,
    out_ref,
):
    n = nb_ref.shape[0]
    h = n // 2

    def in_order(ref, end, size):
        rows = cat([ref[end + size : end + 2 * size, :], ref[0:end, :], ref[end : end + size, :]])
        return rows.astype(F32).reshape(-1, 8, 128)

    own = cat([vb_ref[32:64, :], nb_ref[...], vb_ref[0:32, :]]).astype(F32).reshape(-1, 8, 128)
    odd, even = in_order(cols_odd_ref, h, 16), in_order(cols_even_ref, h, 16)
    col_odd = lax.rem(lax.axis_index("gx"), 2) == 1
    hl, hr = jnp.where(col_odd, even, odd), jnp.where(col_odd, odd, even)
    low = low_half(hl.shape)
    even = jnp.where(low, hl, pltpu.roll(hr, 4, 1))
    odd = jnp.where(low, pltpu.roll(hl, 4, 1), hr)
    halo = jnp.stack([even, odd], axis=1).reshape(own.shape)
    low = low_half(own.shape)
    right = jnp.where(low, own, halo).reshape(-1, 64, 128).astype(BF16)
    left = jnp.where(low, halo, own).reshape(-1, 64, 128).astype(BF16)
    count = right.shape[0]
    looked_at = cat([t for w in range(count) for t in (right[w], left[w])])
    keys = side_by_side(looked_at, wk_ref[...])
    values = dot(wqv_ref[128:256, :], looked_at, NT).astype(BF16)
    wanted = cat([nb_ref[32:n, :], nb_ref[0:32, :]])
    queries = dot(wqv_ref[0:128, :], wanted, NT).astype(BF16)
    masks = [mask(w, s) for w in "12" for s in ("left", "right")]
    units = [([w, w + 1], masks, bias_b[...]) for w in range(1, count - 2, 2)]
    masks = masks[0:2] + [mask("2", v, s) for v in ("up", "down") for s in ("left", "right")]
    units.append(([count - 2, count - 1, 0], masks, bias_bv[...]))
    context = attention(queries, keys, values, units)
    z = cat([fb_ref[32:n, :], fb_ref[0:32, :]])
    out = finish(z, context, wo_ref[1], hg_ref[1:2, :], we_ref[1], ws_ref[1])
    out = half_turn(out)
    rows = n // 8
    out = cat([out[rows - 4 :], out[: rows - 4]])
    inner = oa_ref[...].reshape(rows, 8, 128)
    low = low_half(out.shape)
    out_ref[:, 0:8, :] = jnp.where(low, out, inner)
    out_ref[:, 8:16, :] = jnp.where(low, inner, out)


def vmem(count):
    return [pl.BlockSpec(memory_space=pltpu.VMEM)] * count


def call(kernel, name, operands, outs, scratch=(), flops=0, aliases=None):
    shapes = [jax.ShapeDtypeStruct(shape, dtype) for shape, dtype in outs]
    return pl.pallas_call(
        kernel,
        out_shape=shapes,
        in_specs=vmem(len(operands)),
        out_specs=vmem(len(outs)),
        scratch_shapes=list(scratch),
        input_output_aliases=aliases or {},
        compiler_params=pltpu.CompilerParams(vmem_limit_bytes=32 * 1024 * 1024),
        cost_estimate=pl.CostEstimate(flops=flops, bytes_accessed=1 << 20, transcendentals=0),
        name=name,
    )(*operands)


def on_device(x, ag, tw, ow, pb, hg, ew, sw):
    height, breadth = x.shape[0], x.shape[1]
    n = height * WIN
    table = ((64, HEADS * 128), F32)
    prepared = [((256, 128), BF16), ((256, 256), BF16)]
    weights = (x, tw, ow, ew, sw, ag, pb, hg)
    kept = [((n, C), F32)] * 2 + [((n, C), BF16)] * 2 + [((n // 2, C), BF16)] * 2 + [table] + prepared
    rows = [((WIN, breadth, C), BF16)] * 2
    (start,) = call(start_kernel, "start", (), [((8, 128), jnp.int32)], (), 4 * 10**10)
    last, first = call(
        edge_rows_kernel, "edge_rows", (x, start, ag, pb, hg), rows, [pltpu.SemaphoreType.DMA((2,))]
    )

    def run(*operands):
        return call(first_kernel, "first", operands, rows[0:1] + kept, (), 4 * 10**9, {8: 0})

    def skip(*operands):
        return call(nothing_kernel, "nothing", operands[8:9], rows[0:1] + kept, (), 0, {0: 0})

    up = shift(last, "gy", 1)
    first, *state = lax.cond(goes_first(), run, skip, *weights, first)
    down = shift(first, "gy", -1)
    state = call(
        second_kernel, "second", (*weights, *state), kept, (), 4 * 10**9, {8 + i: i for i in range(9)}
    )
    fa, fb, na, nb, right, left, bias, wqv, wk = state
    va, vb, odd, even = call(
        halo_kernel, "halo", (up, down, right, left, bias, wqv, wk, ow, ew, sw, ag, hg),
        [((64, C), BF16)] * 2 + [((n // 2 + 32, C), BF16)] * 2, (), 10**9,
    )
    odd, even = swap(odd, "gx", 1), swap(even, "gx", 0)
    oa, bias_b, bias_bv, wqv, wk = call(
        middle_kernel, "middle", (fa, na, va, pb, tw, ow, ew, sw, hg),
        [((n, C), F32), table, table] + prepared, [pltpu.VMEM(*table)] * 2, 2 * 10**9,
    )
    return call(
        outer_kernel, "outer", (fb, nb, vb, odd, even, oa, bias_b, bias_bv, wqv, wk, ow, ew, sw, hg),
        [((height, breadth, C), F32)], (), 2 * 10**9,
    )[0]


def solution(mesh):
    return jax.shard_map(
        on_device,
        mesh=mesh,
        in_specs=(P("gy", "gx", None), P(), P(), P(), P(), P(), P(), P()),
        out_specs=P("gy", "gx", None),
        check_vma=False,
    )
```

```python
import math

import jax
import jax.numpy as jnp
from jax import lax
from jax.experimental import pallas as pl
from jax.experimental.pallas import tpu as pltpu
from jax.sharding import PartitionSpec as P

C = 128
HEADS = 4
HID = 512
WIN = 8
HD = 32
EPSILON = 1e-05
LOG2E = math.log2(math.e)
SCALE = HD ** (-0.5) * LOG2E
F32 = jnp.float32
BF16 = jnp.bfloat16
NT = (((1,), (1,)), ((), ()))
TN = (((0,), (0,)), ((), ()))
CHUNK = 256


def shift(x, axis, by):
    length = lax.axis_size(axis)
    return lax.ppermute(x, axis, [(i, (i + by) % length) for i in range(length)])


def iota(shape, dim):
    return lax.broadcasted_iota(jnp.int32, shape, dim)


def dot(a, b, dims=None):
    if dims is None:
        return jnp.dot(a, b, preferred_element_type=F32)
    return lax.dot_general(a, b, dims, preferred_element_type=F32)


def cat(parts, axis=0):
    return jnp.concatenate(parts, axis=axis)


def layer_norm(x, gain):
    center = x - jnp.mean(x, axis=-1, keepdims=True)
    spread = jnp.sum(center * center, axis=-1, keepdims=True)
    return center * lax.rsqrt(spread + C * EPSILON) * (gain * C**0.5)


def twice_gelu(x):
    return x + x * lax.erf(x * (0.5**0.5))


def bias_rows(pb_ref, block):
    sub = iota((8, 128), 0)
    lane = iota((8, 128), 1)
    place = lax.min((lane >> 3) * 15 + 7 + (lane & 7) - sub, 224)
    for head in range(HEADS):
        low = jnp.broadcast_to(pb_ref[block, head : head + 1, 0:128], (8, 128))
        high = jnp.broadcast_to(pb_ref[block, head : head + 1, 97:225], (8, 128))
        strip = jnp.where(
            place < 128,
            jnp.take_along_axis(low, lax.min(place, 127), axis=1),
            jnp.take_along_axis(high, lax.max(place - 97, 0), axis=1),
        )
        strip = strip * LOG2E
        for yj in range(8):
            turn = (128 - (7 - yj) * 8) % 128
            first = pltpu.roll(strip, turn, 1) if turn else strip
            second = pltpu.roll(strip, (turn + 64) % 128, 1)
            yield head, yj, jnp.where(lane < 64, first, second)


def fill_weights(w, wqv, wk):
    wqv[0:128, :] = jnp.transpose(w[:, 0:128].astype(F32)).astype(BF16)
    wqv[128:256, :] = jnp.transpose(w[:, 256:384].astype(F32)).astype(BF16)
    keys = w[:, 128:256].astype(F32)
    turned = pltpu.roll(keys, 64, 1)
    lane = iota((128, 128), 1)
    zero = jnp.zeros((128, 128), F32)
    wk[0:128, 0:128] = jnp.where(lane < 64, keys, zero).astype(BF16)
    wk[0:128, 128:256] = jnp.where(lane < 64, turned, zero).astype(BF16)
    wk[128:256, 0:128] = jnp.where(lane >= 64, turned, zero).astype(BF16)
    wk[128:256, 128:256] = jnp.where(lane >= 64, keys, zero).astype(BF16)


def mask(*conditions):
    lane = iota((64, 128), 1)
    sides = {"1": lane < 64, "2": lane >= 64, "up": (lane & 32) == 0, "down": (lane & 32) > 0}
    sides |= {"left": (lane & 4) == 0, "right": (lane & 4) > 0}
    keep = sides[conditions[0]]
    for name in conditions[1:]:
        keep = keep & sides[name]
    return jnp.where(keep, 1.0, 0.0).astype(BF16)


def side_by_side(tokens, wk):
    pairs = tokens.reshape(-1, 2, 64, 128)
    lanes = cat([cat([pairs[p, 0], pairs[p, 1]], 1) for p in range(pairs.shape[0])])
    return dot(lanes, wk).astype(BF16)


def attention(queries, keys, values, units):
    zero = jnp.zeros((32, 128), BF16)
    scores = []
    for u, (pairs, masks, bias) in enumerate(units):
        q = queries[:, 128 * u : 128 * u + 128]
        for half in range(2):
            r = 64 * half
            rows = []
            for m in masks:
                rows.append(cat([q[r : r + 32] * m[0:32], zero], 1))
                rows.append(cat([zero, q[r + 32 : r + 64] * m[0:32]], 1))
            k = cat([keys[64 * p : 64 * p + 64, 128 * half : 128 * half + 128] for p in pairs], 1)
            scores.append(dot(k, cat(rows)))
    for u, (pairs, masks, bias) in enumerate(units):
        for half in range(2):
            s = scores[2 * u + half] * SCALE + bias[:, 256 * half : 256 * half + 256]
            p = jnp.exp2(s - jnp.max(s, axis=0, keepdims=True))
            part = 1.0 / jnp.sum(p, axis=0, keepdims=True)
            scores[2 * u + half] = (p * part).astype(BF16)
    context = []
    for u, (pairs, masks, bias) in enumerate(units):
        out = []
        for half in range(2):
            r = 64 * half
            p = scores[2 * u + half]
            seen = cat([cat([p[:, 0:128] * m, p[:, 128:256] * m], 1) for m in masks])
            v = cat([values[r : r + 64, 128 * j : 128 * j + 128] for j in pairs], 1)
            ct = dot(v, seen)
            out += [ct[0:32, 0:128], ct[32:64, 128:256]]
        context.append(cat(out).astype(BF16))
    return cat(context, 1)


def finish(z, context, wo, gain, we, ws):
    middle = z + dot(context, wo, TN).astype(BF16).astype(F32)
    normed = layer_norm(middle, gain).astype(BF16)
    size = min(CHUNK, z.shape[0])
    hidden = [dot(normed[i : i + size], we) for i in range(0, z.shape[0], size)]
    hidden = [twice_gelu(h).astype(BF16) for h in hidden]
    return middle + 0.5 * cat([dot(h, ws) for h in hidden])


def half_turn(x):
    return pltpu.roll(x.reshape(-1, 8, 128), 4, 1)


def low_half(shape):
    return iota(shape, 1) < 4


def windows_of(block):
    parts = block.astype(F32).reshape(8, 2, 8, 128)
    return [parts[:, 0].reshape(64, 128), parts[:, 1].reshape(64, 128)]


def shifted_columns(tokens):
    pairs = tokens.reshape(-1, 2, 64, 128)
    a, b = half_turn(pairs[:, 0]), half_turn(pairs[:, 1])
    low = low_half(a.shape)
    return jnp.where(low, a, b).reshape(-1, 128), jnp.where(low, b, a).reshape(-1, 128)


def edges(outer):
    pairs = outer.reshape(-1, 2, 8, 128)
    even, odd = pairs[:, 0], pairs[:, 1]
    low = low_half(even.shape)
    right = jnp.where(low, even, pltpu.roll(odd, 4, 1)).reshape(-1, 128)
    left = jnp.where(low, pltpu.roll(even, 4, 1), odd).reshape(-1, 128)
    return right.astype(BF16), left.astype(BF16)


def goes_first():
    row, rows = lax.axis_index("gy"), lax.axis_size("gy")
    return lax.rem(row, rows // 2) < rows // 8


def own_block(
    x_ref, w_ref, wo_ref, we_ref, ws_ref, ag_ref, pb_ref, hg_ref,
    fa_ref, fb_ref, na_ref, nb_ref, right_ref, left_ref, bias_ref, wqv_ref, wk_ref,
):
    for head, yj, values in bias_rows(pb_ref, 0):
        bias_ref[yj * 8 : yj * 8 + 8, head * 128 : head * 128 + 128] = values
    fill_weights(w_ref[0], wqv_ref, wk_ref)
    bands = x_ref.shape[0] // WIN
    z = cat([t for b in range(bands) for t in windows_of(x_ref[WIN * b : WIN * b + WIN])])
    normed = layer_norm(z, ag_ref[0:1, :]).astype(BF16)
    qv = dot(wqv_ref[...], normed, NT).astype(BF16)
    keys = side_by_side(normed, wk_ref[...])
    masks = [mask("1"), mask("2")]
    units = [([b], masks, bias_ref[...]) for b in range(bands)]
    context = attention(qv[0:128], keys, qv[128:256], units)
    out = finish(z, context, wo_ref[0], hg_ref[0:1, :], we_ref[0], ws_ref[0])
    fa_ref[...], fb_ref[...] = shifted_columns(out)
    na, nb = shifted_columns(layer_norm(out, ag_ref[1:2, :]))
    na_ref[...] = na.astype(BF16)
    nb_ref[...] = nb.astype(BF16)
    right_ref[...], left_ref[...] = edges(nb)


def start_kernel(out_ref):
    out_ref[...] = jnp.zeros(out_ref.shape, jnp.int32)


def edge_rows_kernel(x_ref, start_ref, ag_ref, pb_ref, hg_ref, last_ref, first_ref, sems):
    bottom = x_ref.shape[0] - WIN
    copies = [
        pltpu.make_async_copy(x_ref.at[pl.ds(bottom, WIN)], last_ref, sems.at[0]),
        pltpu.make_async_copy(x_ref.at[pl.ds(0, WIN)], first_ref, sems.at[1]),
    ]
    for copy in copies:
        copy.start()
    for copy in copies:
        copy.wait()


def first_kernel(*refs):
    own_block(*refs[0:8], *refs[10:])


def nothing_kernel(*refs):
    pass


def second_kernel(*refs):
    @pl.when(jnp.logical_not(goes_first()))
    def _():
        own_block(*refs[0:8], *refs[17:])


def halo_kernel(
    up_ref, down_ref, own_right_ref, own_left_ref, bias_ref, wqv_ref, wk_ref, wo_ref, we_ref, ws_ref, ag_ref, hg_ref,
    na_ref, nb_ref, right_ref, left_ref,
):
    z = cat(windows_of(down_ref[...]) + windows_of(up_ref[...]))
    normed = layer_norm(z, ag_ref[0:1, :]).astype(BF16)
    keys = side_by_side(normed, wk_ref[...])
    values = dot(wqv_ref[128:256, :], normed, NT).astype(BF16)

    def wanted(t):
        return cat([t[0:32], t[160:192], t[64:96], t[224:256]])

    queries = dot(wqv_ref[0:128, :], wanted(normed), NT).astype(BF16)
    masks = [mask("1", "up"), mask("2", "up"), mask("1", "down"), mask("2", "down")]
    context = attention(queries, keys, values, [([0, 1], masks, bias_ref[...])])
    out = finish(wanted(z), context, wo_ref[0], hg_ref[0:1, :], we_ref[0], ws_ref[0])
    na, nb = shifted_columns(layer_norm(out, ag_ref[1:2, :]))
    na_ref[...] = na.astype(BF16)
    nb_ref[...] = nb.astype(BF16)
    right, left = edges(nb)
    n = own_right_ref.shape[0]
    right_ref[0:n, :] = own_right_ref[...]
    left_ref[0:n, :] = own_left_ref[...]
    right_ref[n : n + 32, :] = right
    left_ref[n : n + 32, :] = left


def middle_kernel(
    fa_ref, na_ref, va_ref, pb_ref, w_ref, wo_ref, we_ref, ws_ref, hg_ref,
    out_ref, bias_b, bias_bv, wqv_ref, wk_ref,
    bias_a, bias_av,
):
    sub = iota((8, 128), 0)
    lane = iota((8, 128), 1)
    query_left = (lane & 4) == 0
    query_up = (lane & 32) == 0
    row, col = lax.axis_index("gy"), lax.axis_index("gx")
    last_col = jnp.where(query_left, lax.axis_size("gx") - 1, 0) == col
    last_row = jnp.where(query_up, lax.axis_size("gy") - 1, 0) == row
    cut_col = last_col & (query_left != (sub < 4))
    for head, yj, values in bias_rows(pb_ref, 1):
        at = (slice(yj * 8, yj * 8 + 8), slice(head * 128, head * 128 + 128))
        cut = values - 100.0 * LOG2E
        cut_row = (lane >= 64) & last_row & (jnp.logical_not(query_up) if yj < 4 else query_up)
        bias_a[at] = values
        bias_av[at] = jnp.where(cut_row, cut, values)
        bias_b[at] = jnp.where(cut_col, cut, values)
        bias_bv[at] = jnp.where(cut_row | cut_col, cut, values)
    fill_weights(w_ref[1], wqv_ref, wk_ref)
    n = na_ref.shape[0]
    inner = na_ref[32 : n - 32, :]
    first = cat([va_ref[32:64, :], na_ref[0:32, :]])
    last = cat([na_ref[n - 32 : n, :], va_ref[0:32, :]])
    looked_at = cat([inner, last, first, first])
    keys = side_by_side(looked_at, wk_ref[...])
    values = dot(wqv_ref[128:256, :], looked_at, NT).astype(BF16)
    wanted = cat([na_ref[32:n, :], na_ref[0:32, :]])
    queries = dot(wqv_ref[0:128, :], wanted, NT).astype(BF16)
    last_unit = n // 128 - 1
    masks = [mask("1"), mask("2")]
    units = [([u], masks, bias_a[...]) for u in range(last_unit)]
    masks = [mask("1"), mask("2", "up"), mask("2", "down"), jnp.zeros((64, 128), BF16)]
    units.append(([last_unit, last_unit + 1], masks, bias_av[...]))
    context = attention(queries, keys, values, units)
    z = cat([fa_ref[32:n, :], fa_ref[0:32, :]])
    out = finish(z, context, wo_ref[1], hg_ref[1:2, :], we_ref[1], ws_ref[1])
    out = half_turn(out).reshape(n, 128)
    out_ref[32:n, :] = out[0 : n - 32]
    out_ref[0:32, :] = out[n - 32 : n]


def outer_kernel(
    fb_ref, nb_ref, vb_ref, hl_ref, hr_ref, oa_ref, bias_b, bias_bv, wqv_ref, wk_ref, wo_ref, we_ref, ws_ref, hg_ref,
    out_ref,
):
    n = nb_ref.shape[0]
    h = n // 2

    def in_order(ref, end, size):
        rows = cat([ref[end + size : end + 2 * size, :], ref[0:end, :], ref[end : end + size, :]])
        return rows.astype(F32).reshape(-1, 8, 128)

    own = cat([vb_ref[32:64, :], nb_ref[...], vb_ref[0:32, :]]).astype(F32).reshape(-1, 8, 128)
    hl, hr = in_order(hl_ref, h, 16), in_order(hr_ref, h, 16)
    low = low_half(hl.shape)
    even = jnp.where(low, hl, pltpu.roll(hr, 4, 1))
    odd = jnp.where(low, pltpu.roll(hl, 4, 1), hr)
    halo = jnp.stack([even, odd], axis=1).reshape(own.shape)
    low = low_half(own.shape)
    right = jnp.where(low, own, halo).reshape(-1, 64, 128).astype(BF16)
    left = jnp.where(low, halo, own).reshape(-1, 64, 128).astype(BF16)
    count = right.shape[0]
    looked_at = cat([t for w in range(count) for t in (right[w], left[w])])
    keys = side_by_side(looked_at, wk_ref[...])
    values = dot(wqv_ref[128:256, :], looked_at, NT).astype(BF16)
    wanted = cat([nb_ref[32:n, :], nb_ref[0:32, :]])
    queries = dot(wqv_ref[0:128, :], wanted, NT).astype(BF16)
    masks = [mask(w, s) for w in "12" for s in ("left", "right")]
    units = [([w, w + 1], masks, bias_b[...]) for w in range(1, count - 2, 2)]
    masks = masks[0:2] + [mask("2", v, s) for v in ("up", "down") for s in ("left", "right")]
    units.append(([count - 2, count - 1, 0], masks, bias_bv[...]))
    context = attention(queries, keys, values, units)
    z = cat([fb_ref[32:n, :], fb_ref[0:32, :]])
    out = finish(z, context, wo_ref[1], hg_ref[1:2, :], we_ref[1], ws_ref[1])
    out = half_turn(out)
    rows = n // 8
    out = cat([out[rows - 4 :], out[: rows - 4]])
    inner = oa_ref[...].reshape(rows, 8, 128)
    low = low_half(out.shape)
    out_ref[:, 0:8, :] = jnp.where(low, out, inner)
    out_ref[:, 8:16, :] = jnp.where(low, inner, out)


def vmem(count):
    return [pl.BlockSpec(memory_space=pltpu.VMEM)] * count


def call(kernel, name, operands, outs, scratch=(), flops=0, aliases=None):
    shapes = [jax.ShapeDtypeStruct(shape, dtype) for shape, dtype in outs]
    return pl.pallas_call(
        kernel,
        out_shape=shapes,
        in_specs=vmem(len(operands)),
        out_specs=vmem(len(outs)),
        scratch_shapes=list(scratch),
        input_output_aliases=aliases or {},
        compiler_params=pltpu.CompilerParams(vmem_limit_bytes=32 * 1024 * 1024),
        cost_estimate=pl.CostEstimate(flops=flops, bytes_accessed=1 << 20, transcendentals=0),
        name=name,
    )(*operands)


def on_device(x, ag, tw, ow, pb, hg, ew, sw):
    height, breadth = x.shape[0], x.shape[1]
    n = height * WIN
    table = ((64, HEADS * 128), F32)
    prepared = [((256, 128), BF16), ((256, 256), BF16)]
    weights = (x, tw, ow, ew, sw, ag, pb, hg)
    kept = [((n, C), F32)] * 2 + [((n, C), BF16)] * 2 + [((n // 2, C), BF16)] * 2 + [table] + prepared
    rows = [((WIN, breadth, C), BF16)] * 2
    (start,) = call(start_kernel, "start", (), [((8, 128), jnp.int32)], (), 4 * 10**10)
    last, first = call(
        edge_rows_kernel, "edge_rows", (x, start, ag, pb, hg), rows, [pltpu.SemaphoreType.DMA((2,))]
    )

    def run(*operands):
        return call(first_kernel, "first", operands, rows[0:1] + kept, (), 4 * 10**9, {8: 0})

    def skip(*operands):
        return call(nothing_kernel, "nothing", operands[8:9], rows[0:1] + kept, (), 0, {0: 0})

    up = shift(last, "gy", 1)
    first, *state = lax.cond(goes_first(), run, skip, *weights, first)
    down = shift(first, "gy", -1)
    state = call(
        second_kernel, "second", (*weights, *state), kept, (), 4 * 10**9, {8 + i: i for i in range(9)}
    )
    fa, fb, na, nb, right, left, bias, wqv, wk = state
    va, vb, right, left = call(
        halo_kernel, "halo", (up, down, right, left, bias, wqv, wk, ow, ew, sw, ag, hg),
        [((64, C), BF16)] * 2 + [((n // 2 + 32, C), BF16)] * 2, (), 10**9,
    )
    hl = shift(right, "gx", 1)
    hr = shift(left, "gx", -1)
    oa, bias_b, bias_bv, wqv, wk = call(
        middle_kernel, "middle", (fa, na, va, pb, tw, ow, ew, sw, hg),
        [((n, C), F32), table, table] + prepared, [pltpu.VMEM(*table)] * 2, 2 * 10**9,
    )
    return call(
        outer_kernel, "outer", (fb, nb, vb, hl, hr, oa, bias_b, bias_bv, wqv, wk, ow, ew, sw, hg),
        [((height, breadth, C), F32)], (), 2 * 10**9,
    )[0]


def solution(mesh):
    return jax.shard_map(
        on_device,
        mesh=mesh,
        in_specs=(P("gy", "gx", None), P(), P(), P(), P(), P(), P(), P()),
        out_specs=P("gy", "gx", None),
        check_vma=False,
    )
```

```python
import math

import jax
import jax.numpy as jnp
from jax import lax
from jax.experimental import pallas as pl
from jax.experimental.pallas import tpu as pltpu
from jax.sharding import PartitionSpec as P

C = 128
HEADS = 4
HID = 512
WIN = 8
HD = 32
EPSILON = 1e-05
LOG2E = math.log2(math.e)
SCALE = HD ** (-0.5) * LOG2E
F32 = jnp.float32
BF16 = jnp.bfloat16
NT = (((1,), (1,)), ((), ()))
TN = (((0,), (0,)), ((), ()))
CHUNK = 256


def shift(x, axis, by):
    length = lax.axis_size(axis)
    return lax.ppermute(x, axis, [(i, (i + by) % length) for i in range(length)])


def far(index, length):
    place = index % (length // 2)
    return (place == 0) | (place == length // 2 - 1)


def near_first(x, axis):
    length = lax.axis_size(axis)
    return lax.ppermute(x, axis, [(i ^ 1, i) for i in range(length) if far(i, length)])


def near_last(x, axis):
    length = lax.axis_size(axis)
    return lax.ppermute(x, axis, [(i ^ 1, i) for i in range(length) if not far(i, length)])


def swap(x, axis, first):
    length = lax.axis_size(axis)
    there = [(i, (i + 1) % length) for i in range(first, length, 2)]
    return lax.ppermute(x, axis, there + [(b, a) for a, b in there])


def iota(shape, dim):
    return lax.broadcasted_iota(jnp.int32, shape, dim)


def dot(a, b, dims=None):
    if dims is None:
        return jnp.dot(a, b, preferred_element_type=F32)
    return lax.dot_general(a, b, dims, preferred_element_type=F32)


def cat(parts, axis=0):
    return jnp.concatenate(parts, axis=axis)


def layer_norm(x, gain):
    center = x - jnp.mean(x, axis=-1, keepdims=True)
    spread = jnp.sum(center * center, axis=-1, keepdims=True)
    return center * lax.rsqrt(spread + C * EPSILON) * (gain * C**0.5)


def twice_gelu(x):
    return x + x * lax.erf(x * (0.5**0.5))


def bias_rows(pb_ref, block):
    sub = iota((8, 128), 0)
    lane = iota((8, 128), 1)
    place = lax.min((lane >> 3) * 15 + 7 + (lane & 7) - sub, 224)
    for head in range(HEADS):
        low = jnp.broadcast_to(pb_ref[block, head : head + 1, 0:128], (8, 128))
        high = jnp.broadcast_to(pb_ref[block, head : head + 1, 97:225], (8, 128))
        strip = jnp.where(
            place < 128,
            jnp.take_along_axis(low, lax.min(place, 127), axis=1),
            jnp.take_along_axis(high, lax.max(place - 97, 0), axis=1),
        )
        strip = strip * LOG2E
        for yj in range(8):
            turn = (128 - (7 - yj) * 8) % 128
            first = pltpu.roll(strip, turn, 1) if turn else strip
            second = pltpu.roll(strip, (turn + 64) % 128, 1)
            yield head, yj, jnp.where(lane < 64, first, second)


def fill_weights(w, wqv, wk):
    wqv[0:128, :] = jnp.transpose(w[:, 0:128].astype(F32)).astype(BF16)
    wqv[128:256, :] = jnp.transpose(w[:, 256:384].astype(F32)).astype(BF16)
    keys = w[:, 128:256].astype(F32)
    turned = pltpu.roll(keys, 64, 1)
    lane = iota((128, 128), 1)
    zero = jnp.zeros((128, 128), F32)
    wk[0:128, 0:128] = jnp.where(lane < 64, keys, zero).astype(BF16)
    wk[0:128, 128:256] = jnp.where(lane < 64, turned, zero).astype(BF16)
    wk[128:256, 0:128] = jnp.where(lane >= 64, turned, zero).astype(BF16)
    wk[128:256, 128:256] = jnp.where(lane >= 64, keys, zero).astype(BF16)


def mask(*conditions):
    lane = iota((64, 128), 1)
    sides = {"1": lane < 64, "2": lane >= 64, "up": (lane & 32) == 0, "down": (lane & 32) > 0}
    sides |= {"left": (lane & 4) == 0, "right": (lane & 4) > 0}
    keep = sides[conditions[0]]
    for name in conditions[1:]:
        keep = keep & sides[name]
    return jnp.where(keep, 1.0, 0.0).astype(BF16)


def side_by_side(tokens, wk):
    pairs = tokens.reshape(-1, 2, 64, 128)
    lanes = cat([cat([pairs[p, 0], pairs[p, 1]], 1) for p in range(pairs.shape[0])])
    return dot(lanes, wk).astype(BF16)


def attention(queries, keys, values, units):
    zero = jnp.zeros((32, 128), BF16)
    scores = []
    for u, (pairs, masks, bias) in enumerate(units):
        q = queries[:, 128 * u : 128 * u + 128]
        for half in range(2):
            r = 64 * half
            rows = []
            for m in masks:
                rows.append(cat([q[r : r + 32] * m[0:32], zero], 1))
                rows.append(cat([zero, q[r + 32 : r + 64] * m[0:32]], 1))
            k = cat([keys[64 * p : 64 * p + 64, 128 * half : 128 * half + 128] for p in pairs], 1)
            scores.append(dot(k, cat(rows)))
    for u, (pairs, masks, bias) in enumerate(units):
        for half in range(2):
            s = scores[2 * u + half] * SCALE + bias[:, 256 * half : 256 * half + 256]
            p = jnp.exp2(s - jnp.max(s, axis=0, keepdims=True))
            part = 1.0 / jnp.sum(p, axis=0, keepdims=True)
            scores[2 * u + half] = (p * part).astype(BF16)
    context = []
    for u, (pairs, masks, bias) in enumerate(units):
        out = []
        for half in range(2):
            r = 64 * half
            p = scores[2 * u + half]
            seen = cat([cat([p[:, 0:128] * m, p[:, 128:256] * m], 1) for m in masks])
            v = cat([values[r : r + 64, 128 * j : 128 * j + 128] for j in pairs], 1)
            ct = dot(v, seen)
            out += [ct[0:32, 0:128], ct[32:64, 128:256]]
        context.append(cat(out).astype(BF16))
    return cat(context, 1)


def finish(z, context, wo, gain, we, ws):
    middle = z + dot(context, wo, TN).astype(BF16).astype(F32)
    normed = layer_norm(middle, gain).astype(BF16)
    size = min(CHUNK, z.shape[0])
    hidden = [dot(normed[i : i + size], we) for i in range(0, z.shape[0], size)]
    hidden = [twice_gelu(h).astype(BF16) for h in hidden]
    return middle + 0.5 * cat([dot(h, ws) for h in hidden])


def half_turn(x):
    return pltpu.roll(x.reshape(-1, 8, 128), 4, 1)


def low_half(shape):
    return iota(shape, 1) < 4


def windows_of(block):
    parts = block.astype(F32).reshape(8, 2, 8, 128)
    return [parts[:, 0].reshape(64, 128), parts[:, 1].reshape(64, 128)]


def shifted_columns(tokens):
    pairs = tokens.reshape(-1, 2, 64, 128)
    a, b = half_turn(pairs[:, 0]), half_turn(pairs[:, 1])
    low = low_half(a.shape)
    return jnp.where(low, a, b).reshape(-1, 128), jnp.where(low, b, a).reshape(-1, 128)


def edges(outer):
    pairs = outer.reshape(-1, 2, 8, 128)
    even, odd = pairs[:, 0], pairs[:, 1]
    low = low_half(even.shape)
    right = jnp.where(low, even, pltpu.roll(odd, 4, 1)).reshape(-1, 128)
    left = jnp.where(low, pltpu.roll(even, 4, 1), odd).reshape(-1, 128)
    return right.astype(BF16), left.astype(BF16)


def goes_first():
    row, rows = lax.axis_index("gy"), lax.axis_size("gy")
    return lax.rem(row, rows // 2) < rows // 8


def own_block(
    x_ref, w_ref, wo_ref, we_ref, ws_ref, ag_ref, pb_ref, hg_ref,
    fa_ref, fb_ref, na_ref, nb_ref, right_ref, left_ref, bias_ref, wqv_ref, wk_ref,
):
    for head, yj, values in bias_rows(pb_ref, 0):
        bias_ref[yj * 8 : yj * 8 + 8, head * 128 : head * 128 + 128] = values
    fill_weights(w_ref[0], wqv_ref, wk_ref)
    bands = x_ref.shape[0] // WIN
    z = cat([t for b in range(bands) for t in windows_of(x_ref[WIN * b : WIN * b + WIN])])
    normed = layer_norm(z, ag_ref[0:1, :]).astype(BF16)
    qv = dot(wqv_ref[...], normed, NT).astype(BF16)
    keys = side_by_side(normed, wk_ref[...])
    masks = [mask("1"), mask("2")]
    units = [([b], masks, bias_ref[...]) for b in range(bands)]
    context = attention(qv[0:128], keys, qv[128:256], units)
    out = finish(z, context, wo_ref[0], hg_ref[0:1, :], we_ref[0], ws_ref[0])
    fa_ref[...], fb_ref[...] = shifted_columns(out)
    na, nb = shifted_columns(layer_norm(out, ag_ref[1:2, :]))
    na_ref[...] = na.astype(BF16)
    nb_ref[...] = nb.astype(BF16)
    right_ref[...], left_ref[...] = edges(nb)


def start_kernel(out_ref):
    out_ref[...] = jnp.zeros(out_ref.shape, jnp.int32)


def edge_rows_kernel(x_ref, start_ref, ag_ref, pb_ref, hg_ref, last_ref, first_ref, sems):
    bottom = x_ref.shape[0] - WIN
    copies = [
        pltpu.make_async_copy(x_ref.at[pl.ds(bottom, WIN)], last_ref, sems.at[0]),
        pltpu.make_async_copy(x_ref.at[pl.ds(0, WIN)], first_ref, sems.at[1]),
    ]
    for copy in copies:
        copy.start()
    for copy in copies:
        copy.wait()


def first_kernel(*refs):
    own_block(*refs[0:8], *refs[10:])


def nothing_kernel(*refs):
    pass


def second_kernel(*refs):
    @pl.when(jnp.logical_not(goes_first()))
    def _():
        own_block(*refs[0:8], *refs[17:])


def halo_kernel(
    up_ref, down_ref, own_right_ref, own_left_ref, bias_ref, wqv_ref, wk_ref, wo_ref, we_ref, ws_ref, ag_ref, hg_ref,
    na_ref, nb_ref, cols_odd_ref, cols_even_ref, cols_early_ref,
):
    z = cat(windows_of(down_ref[...]) + windows_of(up_ref[...]))
    normed = layer_norm(z, ag_ref[0:1, :]).astype(BF16)
    keys = side_by_side(normed, wk_ref[...])
    values = dot(wqv_ref[128:256, :], normed, NT).astype(BF16)

    def wanted(t):
        return cat([t[0:32], t[160:192], t[64:96], t[224:256]])

    queries = dot(wqv_ref[0:128, :], wanted(normed), NT).astype(BF16)
    masks = [mask("1", "up"), mask("2", "up"), mask("1", "down"), mask("2", "down")]
    context = attention(queries, keys, values, [([0, 1], masks, bias_ref[...])])
    out = finish(wanted(z), context, wo_ref[0], hg_ref[0:1, :], we_ref[0], ws_ref[0])
    na, nb = shifted_columns(layer_norm(out, ag_ref[1:2, :]))
    na_ref[...] = na.astype(BF16)
    nb_ref[...] = nb.astype(BF16)
    right, left = edges(nb)
    n = own_right_ref.shape[0]
    col_odd = lax.rem(lax.axis_index("gx"), 2) == 1
    for at, size, a, b in [(0, n, own_right_ref[...], own_left_ref[...]), (n, 32, right, left)]:
        a, b = a.astype(F32), b.astype(F32)
        cols_odd_ref[at : at + size, :] = jnp.where(col_odd, a, b).astype(BF16)
        cols_even_ref[at : at + size, :] = jnp.where(col_odd, b, a).astype(BF16)
        cols_early_ref[at : at + size, :] = jnp.where(col_odd, b, a).astype(BF16)


def middle_kernel(
    fa_ref, na_ref, va_ref, pb_ref, w_ref, wo_ref, we_ref, ws_ref, hg_ref,
    out_ref, bias_b, bias_bv, wqv_ref, wk_ref,
    bias_a, bias_av,
):
    sub = iota((8, 128), 0)
    lane = iota((8, 128), 1)
    query_left = (lane & 4) == 0
    query_up = (lane & 32) == 0
    row, col = lax.axis_index("gy"), lax.axis_index("gx")
    last_col = jnp.where(query_left, lax.axis_size("gx") - 1, 0) == col
    last_row = jnp.where(query_up, lax.axis_size("gy") - 1, 0) == row
    cut_col = last_col & (query_left != (sub < 4))
    for head, yj, values in bias_rows(pb_ref, 1):
        at = (slice(yj * 8, yj * 8 + 8), slice(head * 128, head * 128 + 128))
        cut = values - 100.0 * LOG2E
        cut_row = (lane >= 64) & last_row & (jnp.logical_not(query_up) if yj < 4 else query_up)
        bias_a[at] = values
        bias_av[at] = jnp.where(cut_row, cut, values)
        bias_b[at] = jnp.where(cut_col, cut, values)
        bias_bv[at] = jnp.where(cut_row | cut_col, cut, values)
    fill_weights(w_ref[1], wqv_ref, wk_ref)
    n = na_ref.shape[0]
    inner = na_ref[32 : n - 32, :]
    first = cat([va_ref[32:64, :], na_ref[0:32, :]])
    last = cat([na_ref[n - 32 : n, :], va_ref[0:32, :]])
    looked_at = cat([inner, last, first, first])
    keys = side_by_side(looked_at, wk_ref[...])
    values = dot(wqv_ref[128:256, :], looked_at, NT).astype(BF16)
    wanted = cat([na_ref[32:n, :], na_ref[0:32, :]])
    queries = dot(wqv_ref[0:128, :], wanted, NT).astype(BF16)
    last_unit = n // 128 - 1
    masks = [mask("1"), mask("2")]
    units = [([u], masks, bias_a[...]) for u in range(last_unit)]
    masks = [mask("1"), mask("2", "up"), mask("2", "down"), jnp.zeros((64, 128), BF16)]
    units.append(([last_unit, last_unit + 1], masks, bias_av[...]))
    context = attention(queries, keys, values, units)
    z = cat([fa_ref[32:n, :], fa_ref[0:32, :]])
    out = finish(z, context, wo_ref[1], hg_ref[1:2, :], we_ref[1], ws_ref[1])
    out = half_turn(out).reshape(n, 128)
    out_ref[32:n, :] = out[0 : n - 32]
    out_ref[0:32, :] = out[n - 32 : n]


def outer_kernel(
    fb_ref, nb_ref, vb_ref, early_ref, odd_ref, even_ref, oa_ref, bias_b, bias_bv, wqv_ref, wk_ref, wo_ref, we_ref, ws_ref, hg_ref,
    out_ref,
):
    n = nb_ref.shape[0]
    h = n // 2

    def in_order(ref, end, size):
        rows = cat([ref[end + size : end + 2 * size, :], ref[0:end, :], ref[end : end + size, :]])
        return rows.astype(F32).reshape(-1, 8, 128)

    own = cat([vb_ref[32:64, :], nb_ref[...], vb_ref[0:32, :]]).astype(F32).reshape(-1, 8, 128)
    is_far = far(lax.axis_index("gx"), lax.axis_size("gx"))
    odd = in_order(odd_ref, h, 16)
    even = jnp.where(is_far, in_order(early_ref, h, 16), in_order(even_ref, h, 16))
    col_odd = lax.rem(lax.axis_index("gx"), 2) == 1
    hl, hr = jnp.where(col_odd, even, odd), jnp.where(col_odd, odd, even)
    low = low_half(hl.shape)
    even = jnp.where(low, hl, pltpu.roll(hr, 4, 1))
    odd = jnp.where(low, pltpu.roll(hl, 4, 1), hr)
    halo = jnp.stack([even, odd], axis=1).reshape(own.shape)
    low = low_half(own.shape)
    right = jnp.where(low, own, halo).reshape(-1, 64, 128).astype(BF16)
    left = jnp.where(low, halo, own).reshape(-1, 64, 128).astype(BF16)
    count = right.shape[0]
    looked_at = cat([t for w in range(count) for t in (right[w], left[w])])
    keys = side_by_side(looked_at, wk_ref[...])
    values = dot(wqv_ref[128:256, :], looked_at, NT).astype(BF16)
    wanted = cat([nb_ref[32:n, :], nb_ref[0:32, :]])
    queries = dot(wqv_ref[0:128, :], wanted, NT).astype(BF16)
    masks = [mask(w, s) for w in "12" for s in ("left", "right")]
    units = [([w, w + 1], masks, bias_b[...]) for w in range(1, count - 2, 2)]
    masks = masks[0:2] + [mask("2", v, s) for v in ("up", "down") for s in ("left", "right")]
    units.append(([count - 2, count - 1, 0], masks, bias_bv[...]))
    context = attention(queries, keys, values, units)
    z = cat([fb_ref[32:n, :], fb_ref[0:32, :]])
    out = finish(z, context, wo_ref[1], hg_ref[1:2, :], we_ref[1], ws_ref[1])
    out = half_turn(out)
    rows = n // 8
    out = cat([out[rows - 4 :], out[: rows - 4]])
    inner = oa_ref[...].reshape(rows, 8, 128)
    low = low_half(out.shape)
    out_ref[:, 0:8, :] = jnp.where(low, out, inner)
    out_ref[:, 8:16, :] = jnp.where(low, inner, out)


def vmem(count):
    return [pl.BlockSpec(memory_space=pltpu.VMEM)] * count


def call(kernel, name, operands, outs, scratch=(), flops=0, aliases=None):
    shapes = [jax.ShapeDtypeStruct(shape, dtype) for shape, dtype in outs]
    return pl.pallas_call(
        kernel,
        out_shape=shapes,
        in_specs=vmem(len(operands)),
        out_specs=vmem(len(outs)),
        scratch_shapes=list(scratch),
        input_output_aliases=aliases or {},
        compiler_params=pltpu.CompilerParams(vmem_limit_bytes=32 * 1024 * 1024),
        cost_estimate=pl.CostEstimate(flops=flops, bytes_accessed=1 << 20, transcendentals=0),
        name=name,
    )(*operands)


def on_device(x, ag, tw, ow, pb, hg, ew, sw):
    height, breadth = x.shape[0], x.shape[1]
    n = height * WIN
    table = ((64, HEADS * 128), F32)
    prepared = [((256, 128), BF16), ((256, 256), BF16)]
    weights = (x, tw, ow, ew, sw, ag, pb, hg)
    kept = [((n, C), F32)] * 2 + [((n, C), BF16)] * 2 + [((n // 2, C), BF16)] * 2 + [table] + prepared
    rows = [((WIN, breadth, C), BF16)] * 2
    (start,) = call(start_kernel, "start", (), [((8, 128), jnp.int32)], (), 4 * 10**10)
    last, first = call(
        edge_rows_kernel, "edge_rows", (x, start, ag, pb, hg), rows, [pltpu.SemaphoreType.DMA((2,))]
    )

    def run(*operands):
        return call(first_kernel, "first", operands, rows[0:1] + kept, (), 4 * 10**9, {8: 0})

    def skip(*operands):
        return call(nothing_kernel, "nothing", operands[8:9], rows[0:1] + kept, (), 0, {0: 0})

    up = shift(last, "gy", 1)
    first, *state = lax.cond(goes_first(), run, skip, *weights, first)
    down = shift(first, "gy", -1)
    state = call(
        second_kernel, "second", (*weights, *state), kept, (), 4 * 10**9, {8 + i: i for i in range(9)}
    )
    fa, fb, na, nb, right, left, bias, wqv, wk = state
    va, vb, odd, even, early = call(
        halo_kernel, "halo", (up, down, right, left, bias, wqv, wk, ow, ew, sw, ag, hg),
        [((64, C), BF16)] * 2 + [((n // 2 + 32, C), BF16)] * 3, (), 10**9,
    )
    early = near_first(early, "gx")
    odd = swap(odd, "gx", 1)
    even = near_last(even, "gx")
    oa, bias_b, bias_bv, wqv, wk = call(
        middle_kernel, "middle", (fa, na, va, pb, tw, ow, ew, sw, hg),
        [((n, C), F32), table, table] + prepared, [pltpu.VMEM(*table)] * 2, 2 * 10**9,
    )
    return call(
        outer_kernel, "outer", (fb, nb, vb, early, odd, even, oa, bias_b, bias_bv, wqv, wk, ow, ew, sw, hg),
        [((height, breadth, C), F32)], (), 2 * 10**9,
    )[0]


def solution(mesh):
    return jax.shard_map(
        on_device,
        mesh=mesh,
        in_specs=(P("gy", "gx", None), P(), P(), P(), P(), P(), P(), P()),
        out_specs=P("gy", "gx", None),
        check_vma=False,
    )
```

```python
import math

import jax
import jax.numpy as jnp
from jax import lax
from jax.experimental import pallas as pl
from jax.experimental.pallas import tpu as pltpu
from jax.sharding import PartitionSpec as P

C = 128
HEADS = 4
HID = 512
WIN = 8
HD = 32
EPSILON = 1e-05
LOG2E = math.log2(math.e)
SCALE = HD ** (-0.5) * LOG2E
F32 = jnp.float32
BF16 = jnp.bfloat16
NT = (((1,), (1,)), ((), ()))
TN = (((0,), (0,)), ((), ()))
CHUNK = 256


def shift(x, axis, by):
    length = lax.axis_size(axis)
    return lax.ppermute(x, axis, [(i, (i + by) % length) for i in range(length)])


def swap(x, axis, first):
    length = lax.axis_size(axis)
    there = [(i, (i + 1) % length) for i in range(first, length, 2)]
    return lax.ppermute(x, axis, there + [(b, a) for a, b in there])


def iota(shape, dim):
    return lax.broadcasted_iota(jnp.int32, shape, dim)


def dot(a, b, dims=None):
    if dims is None:
        return jnp.dot(a, b, preferred_element_type=F32)
    return lax.dot_general(a, b, dims, preferred_element_type=F32)


def cat(parts, axis=0):
    return jnp.concatenate(parts, axis=axis)


def layer_norm(x, gain):
    center = x - jnp.mean(x, axis=-1, keepdims=True)
    spread = jnp.sum(center * center, axis=-1, keepdims=True)
    return center * lax.rsqrt(spread + C * EPSILON) * (gain * C**0.5)


def twice_gelu(x):
    return x + x * lax.erf(x * (0.5**0.5))


def bias_rows(pb_ref, block):
    sub = iota((8, 128), 0)
    lane = iota((8, 128), 1)
    place = lax.min((lane >> 3) * 15 + 7 + (lane & 7) - sub, 224)
    for head in range(HEADS):
        low = jnp.broadcast_to(pb_ref[block, head : head + 1, 0:128], (8, 128))
        high = jnp.broadcast_to(pb_ref[block, head : head + 1, 97:225], (8, 128))
        strip = jnp.where(
            place < 128,
            jnp.take_along_axis(low, lax.min(place, 127), axis=1),
            jnp.take_along_axis(high, lax.max(place - 97, 0), axis=1),
        )
        strip = strip * LOG2E
        for yj in range(8):
            turn = (128 - (7 - yj) * 8) % 128
            first = pltpu.roll(strip, turn, 1) if turn else strip
            second = pltpu.roll(strip, (turn + 64) % 128, 1)
            yield head, yj, jnp.where(lane < 64, first, second)


def fill_weights(w, wqv, wk):
    wqv[0:128, :] = jnp.transpose(w[:, 0:128].astype(F32)).astype(BF16)
    wqv[128:256, :] = jnp.transpose(w[:, 256:384].astype(F32)).astype(BF16)
    keys = w[:, 128:256].astype(F32)
    turned = pltpu.roll(keys, 64, 1)
    lane = iota((128, 128), 1)
    zero = jnp.zeros((128, 128), F32)
    wk[0:128, 0:128] = jnp.where(lane < 64, keys, zero).astype(BF16)
    wk[0:128, 128:256] = jnp.where(lane < 64, turned, zero).astype(BF16)
    wk[128:256, 0:128] = jnp.where(lane >= 64, turned, zero).astype(BF16)
    wk[128:256, 128:256] = jnp.where(lane >= 64, keys, zero).astype(BF16)


def mask(*conditions):
    lane = iota((64, 128), 1)
    sides = {"1": lane < 64, "2": lane >= 64, "up": (lane & 32) == 0, "down": (lane & 32) > 0}
    sides |= {"left": (lane & 4) == 0, "right": (lane & 4) > 0}
    keep = sides[conditions[0]]
    for name in conditions[1:]:
        keep = keep & sides[name]
    return jnp.where(keep, 1.0, 0.0).astype(BF16)


def side_by_side(tokens, wk):
    pairs = tokens.reshape(-1, 2, 64, 128)
    lanes = cat([cat([pairs[p, 0], pairs[p, 1]], 1) for p in range(pairs.shape[0])])
    return dot(lanes, wk).astype(BF16)


def attention(queries, keys, values, units):
    zero = jnp.zeros((32, 128), BF16)
    scores = []
    for u, (pairs, masks, bias) in enumerate(units):
        q = queries[:, 128 * u : 128 * u + 128]
        for half in range(2):
            r = 64 * half
            rows = []
            for m in masks:
                rows.append(cat([q[r : r + 32] * m[0:32], zero], 1))
                rows.append(cat([zero, q[r + 32 : r + 64] * m[0:32]], 1))
            k = cat([keys[64 * p : 64 * p + 64, 128 * half : 128 * half + 128] for p in pairs], 1)
            scores.append(dot(k, cat(rows)))
    for u, (pairs, masks, bias) in enumerate(units):
        for half in range(2):
            s = scores[2 * u + half] * SCALE + bias[:, 256 * half : 256 * half + 256]
            p = jnp.exp2(s - jnp.max(s, axis=0, keepdims=True))
            part = 1.0 / jnp.sum(p, axis=0, keepdims=True)
            scores[2 * u + half] = (p * part).astype(BF16)
    context = []
    for u, (pairs, masks, bias) in enumerate(units):
        out = []
        for half in range(2):
            r = 64 * half
            p = scores[2 * u + half]
            seen = cat([cat([p[:, 0:128] * m, p[:, 128:256] * m], 1) for m in masks])
            v = cat([values[r : r + 64, 128 * j : 128 * j + 128] for j in pairs], 1)
            ct = dot(v, seen)
            out += [ct[0:32, 0:128], ct[32:64, 128:256]]
        context.append(cat(out).astype(BF16))
    return cat(context, 1)


def finish(z, context, wo, gain, we, ws):
    middle = z + dot(context, wo, TN).astype(BF16).astype(F32)
    normed = layer_norm(middle, gain).astype(BF16)
    size = min(CHUNK, z.shape[0])
    hidden = [dot(normed[i : i + size], we) for i in range(0, z.shape[0], size)]
    hidden = [twice_gelu(h).astype(BF16) for h in hidden]
    return middle + 0.5 * cat([dot(h, ws) for h in hidden])


def half_turn(x):
    return pltpu.roll(x.reshape(-1, 8, 128), 4, 1)


def low_half(shape):
    return iota(shape, 1) < 4


def windows_of(block):
    parts = block.astype(F32).reshape(8, 2, 8, 128)
    return [parts[:, 0].reshape(64, 128), parts[:, 1].reshape(64, 128)]


def shifted_columns(tokens):
    pairs = tokens.reshape(-1, 2, 64, 128)
    a, b = half_turn(pairs[:, 0]), half_turn(pairs[:, 1])
    low = low_half(a.shape)
    return jnp.where(low, a, b).reshape(-1, 128), jnp.where(low, b, a).reshape(-1, 128)


def edges(outer):
    pairs = outer.reshape(-1, 2, 8, 128)
    even, odd = pairs[:, 0], pairs[:, 1]
    low = low_half(even.shape)
    right = jnp.where(low, even, pltpu.roll(odd, 4, 1)).reshape(-1, 128)
    left = jnp.where(low, pltpu.roll(even, 4, 1), odd).reshape(-1, 128)
    return right.astype(BF16), left.astype(BF16)


def goes_first():
    row, rows = lax.axis_index("gy"), lax.axis_size("gy")
    return lax.rem(row, rows // 2) < rows // 8


def own_block(
    x_ref, w_ref, wo_ref, we_ref, ws_ref, ag_ref, pb_ref, hg_ref,
    fa_ref, fb_ref, na_ref, nb_ref, right_ref, left_ref, bias_ref, wqv_ref, wk_ref,
):
    for head, yj, values in bias_rows(pb_ref, 0):
        bias_ref[yj * 8 : yj * 8 + 8, head * 128 : head * 128 + 128] = values
    fill_weights(w_ref[0], wqv_ref, wk_ref)
    bands = x_ref.shape[0] // WIN
    z = cat([t for b in range(bands) for t in windows_of(x_ref[WIN * b : WIN * b + WIN])])
    normed = layer_norm(z, ag_ref[0:1, :]).astype(BF16)
    qv = dot(wqv_ref[...], normed, NT).astype(BF16)
    keys = side_by_side(normed, wk_ref[...])
    masks = [mask("1"), mask("2")]
    units = [([b], masks, bias_ref[...]) for b in range(bands)]
    context = attention(qv[0:128], keys, qv[128:256], units)
    out = finish(z, context, wo_ref[0], hg_ref[0:1, :], we_ref[0], ws_ref[0])
    fa_ref[...], fb_ref[...] = shifted_columns(out)
    na, nb = shifted_columns(layer_norm(out, ag_ref[1:2, :]))
    na_ref[...] = na.astype(BF16)
    nb_ref[...] = nb.astype(BF16)
    right_ref[...], left_ref[...] = edges(nb)


def start_kernel(out_ref):
    out_ref[...] = jnp.zeros(out_ref.shape, jnp.int32)


def edge_rows_kernel(x_ref, start_ref, ag_ref, pb_ref, hg_ref, last_ref, first_ref, sems):
    bottom = x_ref.shape[0] - WIN
    copies = [
        pltpu.make_async_copy(x_ref.at[pl.ds(bottom, WIN)], last_ref, sems.at[0]),
        pltpu.make_async_copy(x_ref.at[pl.ds(0, WIN)], first_ref, sems.at[1]),
    ]
    for copy in copies:
        copy.start()
    for copy in copies:
        copy.wait()


def first_kernel(*refs):
    own_block(*refs[0:8], *refs[10:])


def nothing_kernel(*refs):
    pass


def second_kernel(*refs):
    @pl.when(jnp.logical_not(goes_first()))
    def _():
        own_block(*refs[0:8], *refs[17:])


def halo_kernel(
    up_ref, down_ref, own_right_ref, own_left_ref, bias_ref, wqv_ref, wk_ref, wo_ref, we_ref, ws_ref, ag_ref, hg_ref,
    na_ref, nb_ref, cols_odd_ref, cols_even_ref,
):
    z = cat(windows_of(down_ref[...]) + windows_of(up_ref[...]))
    normed = layer_norm(z, ag_ref[0:1, :]).astype(BF16)
    keys = side_by_side(normed, wk_ref[...])
    values = dot(wqv_ref[128:256, :], normed, NT).astype(BF16)

    def wanted(t):
        return cat([t[0:32], t[160:192], t[64:96], t[224:256]])

    queries = dot(wqv_ref[0:128, :], wanted(normed), NT).astype(BF16)
    masks = [mask("1", "up"), mask("2", "up"), mask("1", "down"), mask("2", "down")]
    context = attention(queries, keys, values, [([0, 1], masks, bias_ref[...])])
    out = finish(wanted(z), context, wo_ref[0], hg_ref[0:1, :], we_ref[0], ws_ref[0])
    na, nb = shifted_columns(layer_norm(out, ag_ref[1:2, :]))
    na_ref[...] = na.astype(BF16)
    nb_ref[...] = nb.astype(BF16)
    right, left = edges(nb)
    n = own_right_ref.shape[0]
    col_odd = lax.rem(lax.axis_index("gx"), 2) == 1
    for at, size, a, b in [(0, n, own_right_ref[...], own_left_ref[...]), (n, 32, right, left)]:
        a, b = a.astype(F32), b.astype(F32)
        cols_odd_ref[at : at + size, :] = jnp.where(col_odd, a, b).astype(BF16)
        cols_even_ref[at : at + size, :] = jnp.where(col_odd, b, a).astype(BF16)


def middle_kernel(
    fa_ref, na_ref, va_ref, pb_ref, w_ref, wo_ref, we_ref, ws_ref, hg_ref,
    out_ref, bias_b, bias_bv, wqv_ref, wk_ref,
    bias_a, bias_av,
):
    sub = iota((8, 128), 0)
    lane = iota((8, 128), 1)
    query_left = (lane & 4) == 0
    query_up = (lane & 32) == 0
    row, col = lax.axis_index("gy"), lax.axis_index("gx")
    last_col = jnp.where(query_left, lax.axis_size("gx") - 1, 0) == col
    last_row = jnp.where(query_up, lax.axis_size("gy") - 1, 0) == row
    cut_col = last_col & (query_left != (sub < 4))
    for head, yj, values in bias_rows(pb_ref, 1):
        at = (slice(yj * 8, yj * 8 + 8), slice(head * 128, head * 128 + 128))
        cut = values - 100.0 * LOG2E
        cut_row = (lane >= 64) & last_row & (jnp.logical_not(query_up) if yj < 4 else query_up)
        bias_a[at] = values
        bias_av[at] = jnp.where(cut_row, cut, values)
        bias_b[at] = jnp.where(cut_col, cut, values)
        bias_bv[at] = jnp.where(cut_row | cut_col, cut, values)
    fill_weights(w_ref[1], wqv_ref, wk_ref)
    n = na_ref.shape[0]
    inner = na_ref[32 : n - 32, :]
    first = cat([va_ref[32:64, :], na_ref[0:32, :]])
    last = cat([na_ref[n - 32 : n, :], va_ref[0:32, :]])
    looked_at = cat([inner, last, first, first])
    keys = side_by_side(looked_at, wk_ref[...])
    values = dot(wqv_ref[128:256, :], looked_at, NT).astype(BF16)
    wanted = cat([na_ref[32:n, :], na_ref[0:32, :]])
    queries = dot(wqv_ref[0:128, :], wanted, NT).astype(BF16)
    last_unit = n // 128 - 1
    masks = [mask("1"), mask("2")]
    units = [([u], masks, bias_a[...]) for u in range(last_unit)]
    masks = [mask("1"), mask("2", "up"), mask("2", "down"), jnp.zeros((64, 128), BF16)]
    units.append(([last_unit, last_unit + 1], masks, bias_av[...]))
    context = attention(queries, keys, values, units)
    z = cat([fa_ref[32:n, :], fa_ref[0:32, :]])
    out = finish(z, context, wo_ref[1], hg_ref[1:2, :], we_ref[1], ws_ref[1])
    out = half_turn(out).reshape(n, 128)
    out_ref[32:n, :] = out[0 : n - 32]
    out_ref[0:32, :] = out[n - 32 : n]


def outer_kernel(
    fb_ref, nb_ref, vb_ref, cols_even_ref, cols_odd_ref, oa_ref, bias_b, bias_bv, wqv_ref, wk_ref, wo_ref, we_ref, ws_ref, hg_ref,
    out_ref,
):
    n = nb_ref.shape[0]
    h = n // 2

    def in_order(ref, end, size):
        rows = cat([ref[end + size : end + 2 * size, :], ref[0:end, :], ref[end : end + size, :]])
        return rows.astype(F32).reshape(-1, 8, 128)

    own = cat([vb_ref[32:64, :], nb_ref[...], vb_ref[0:32, :]]).astype(F32).reshape(-1, 8, 128)
    odd, even = in_order(cols_odd_ref, h, 16), in_order(cols_even_ref, h, 16)
    col_odd = lax.rem(lax.axis_index("gx"), 2) == 1
    hl, hr = jnp.where(col_odd, even, odd), jnp.where(col_odd, odd, even)
    low = low_half(hl.shape)
    even = jnp.where(low, hl, pltpu.roll(hr, 4, 1))
    odd = jnp.where(low, pltpu.roll(hl, 4, 1), hr)
    halo = jnp.stack([even, odd], axis=1).reshape(own.shape)
    low = low_half(own.shape)
    right = jnp.where(low, own, halo).reshape(-1, 64, 128).astype(BF16)
    left = jnp.where(low, halo, own).reshape(-1, 64, 128).astype(BF16)
    count = right.shape[0]
    looked_at = cat([t for w in range(count) for t in (right[w], left[w])])
    keys = side_by_side(looked_at, wk_ref[...])
    values = dot(wqv_ref[128:256, :], looked_at, NT).astype(BF16)
    wanted = cat([nb_ref[32:n, :], nb_ref[0:32, :]])
    queries = dot(wqv_ref[0:128, :], wanted, NT).astype(BF16)
    masks = [mask(w, s) for w in "12" for s in ("left", "right")]
    units = [([w, w + 1], masks, bias_b[...]) for w in range(1, count - 2, 2)]
    masks = masks[0:2] + [mask("2", v, s) for v in ("up", "down") for s in ("left", "right")]
    units.append(([count - 2, count - 1, 0], masks, bias_bv[...]))
    context = attention(queries, keys, values, units)
    z = cat([fb_ref[32:n, :], fb_ref[0:32, :]])
    out = finish(z, context, wo_ref[1], hg_ref[1:2, :], we_ref[1], ws_ref[1])
    out = half_turn(out)
    rows = n // 8
    out = cat([out[rows - 4 :], out[: rows - 4]])
    inner = oa_ref[...].reshape(rows, 8, 128)
    low = low_half(out.shape)
    out_ref[:, 0:8, :] = jnp.where(low, out, inner)
    out_ref[:, 8:16, :] = jnp.where(low, inner, out)


def vmem(count):
    return [pl.BlockSpec(memory_space=pltpu.VMEM)] * count


def call(kernel, name, operands, outs, scratch=(), flops=0, aliases=None):
    shapes = [jax.ShapeDtypeStruct(shape, dtype) for shape, dtype in outs]
    return pl.pallas_call(
        kernel,
        out_shape=shapes,
        in_specs=vmem(len(operands)),
        out_specs=vmem(len(outs)),
        scratch_shapes=list(scratch),
        input_output_aliases=aliases or {},
        compiler_params=pltpu.CompilerParams(vmem_limit_bytes=32 * 1024 * 1024),
        cost_estimate=pl.CostEstimate(flops=flops, bytes_accessed=1 << 20, transcendentals=0),
        name=name,
    )(*operands)


def on_device(x, ag, tw, ow, pb, hg, ew, sw):
    height, breadth = x.shape[0], x.shape[1]
    n = height * WIN
    table = ((64, HEADS * 128), F32)
    prepared = [((256, 128), BF16), ((256, 256), BF16)]
    weights = (x, tw, ow, ew, sw, ag, pb, hg)
    kept = [((n, C), F32)] * 2 + [((n, C), BF16)] * 2 + [((n // 2, C), BF16)] * 2 + [table] + prepared
    rows = [((WIN, breadth, C), BF16)] * 2
    (start,) = call(start_kernel, "start", (), [((8, 128), jnp.int32)], (), 4 * 10**10)
    last, first = call(
        edge_rows_kernel, "edge_rows", (x, start, ag, pb, hg), rows, [pltpu.SemaphoreType.DMA((2,))]
    )

    def run(*operands):
        return call(first_kernel, "first", operands, rows[0:1] + kept, (), 4 * 10**9, {8: 0})

    def skip(*operands):
        return call(nothing_kernel, "nothing", operands[8:9], rows[0:1] + kept, (), 0, {0: 0})

    up = shift(last, "gy", 1)
    first, *state = lax.cond(goes_first(), run, skip, *weights, first)
    down = shift(first, "gy", -1)
    state = call(
        second_kernel, "second", (*weights, *state), kept, (), 4 * 10**9, {8 + i: i for i in range(9)}
    )
    fa, fb, na, nb, right, left, bias, wqv, wk = state
    va, vb, odd, even = call(
        halo_kernel, "halo", (up, down, right, left, bias, wqv, wk, ow, ew, sw, ag, hg),
        [((64, C), BF16)] * 2 + [((n // 2 + 32, C), BF16)] * 2, (), 10**9,
    )
    even, odd = swap(even, "gx", 0), swap(odd, "gx", 1)
    oa, bias_b, bias_bv, wqv, wk = call(
        middle_kernel, "middle", (fa, na, va, pb, tw, ow, ew, sw, hg),
        [((n, C), F32), table, table] + prepared, [pltpu.VMEM(*table)] * 2, 2 * 10**9,
    )
    return call(
        outer_kernel, "outer", (fb, nb, vb, even, odd, oa, bias_b, bias_bv, wqv, wk, ow, ew, sw, hg),
        [((height, breadth, C), F32)], (), 2 * 10**9,
    )[0]


def solution(mesh):
    return jax.shard_map(
        on_device,
        mesh=mesh,
        in_specs=(P("gy", "gx", None), P(), P(), P(), P(), P(), P(), P()),
        out_specs=P("gy", "gx", None),
        check_vma=False,
    )
```

```python
import math

import jax
import jax.numpy as jnp
from jax import lax
from jax.experimental import pallas as pl
from jax.experimental.pallas import tpu as pltpu
from jax.sharding import PartitionSpec as P

C = 128
HEADS = 4
HID = 512
WIN = 8
HD = 32
EPSILON = 1e-05
LOG2E = math.log2(math.e)
SCALE = HD ** (-0.5) * LOG2E
F32 = jnp.float32
BF16 = jnp.bfloat16
NT = (((1,), (1,)), ((), ()))
TN = (((0,), (0,)), ((), ()))
CHUNK = 256


def shift(x, axis, by):
    length = lax.axis_size(axis)
    return lax.ppermute(x, axis, [(i, (i + by) % length) for i in range(length)])


def swaps_early(index, length):
    return index % (length // 2) < 2


def near_first(x, axis):
    length = lax.axis_size(axis)
    return lax.ppermute(x, axis, [(i ^ 1, i) for i in range(length) if swaps_early(i, length)])


def near_last(x, axis):
    length = lax.axis_size(axis)
    return lax.ppermute(x, axis, [(i ^ 1, i) for i in range(length) if not swaps_early(i, length)])


def swap(x, axis, first):
    length = lax.axis_size(axis)
    there = [(i, (i + 1) % length) for i in range(first, length, 2)]
    return lax.ppermute(x, axis, there + [(b, a) for a, b in there])


def iota(shape, dim):
    return lax.broadcasted_iota(jnp.int32, shape, dim)


def dot(a, b, dims=None):
    if dims is None:
        return jnp.dot(a, b, preferred_element_type=F32)
    return lax.dot_general(a, b, dims, preferred_element_type=F32)


def cat(parts, axis=0):
    return jnp.concatenate(parts, axis=axis)


def layer_norm(x, gain):
    center = x - jnp.mean(x, axis=-1, keepdims=True)
    spread = jnp.sum(center * center, axis=-1, keepdims=True)
    return center * lax.rsqrt(spread + C * EPSILON) * (gain * C**0.5)


def twice_gelu(x):
    return x + x * lax.erf(x * (0.5**0.5))


def bias_rows(pb_ref, block):
    sub = iota((8, 128), 0)
    lane = iota((8, 128), 1)
    place = lax.min((lane >> 3) * 15 + 7 + (lane & 7) - sub, 224)
    for head in range(HEADS):
        low = jnp.broadcast_to(pb_ref[block, head : head + 1, 0:128], (8, 128))
        high = jnp.broadcast_to(pb_ref[block, head : head + 1, 97:225], (8, 128))
        strip = jnp.where(
            place < 128,
            jnp.take_along_axis(low, lax.min(place, 127), axis=1),
            jnp.take_along_axis(high, lax.max(place - 97, 0), axis=1),
        )
        strip = strip * LOG2E
        for yj in range(8):
            turn = (128 - (7 - yj) * 8) % 128
            first = pltpu.roll(strip, turn, 1) if turn else strip
            second = pltpu.roll(strip, (turn + 64) % 128, 1)
            yield head, yj, jnp.where(lane < 64, first, second)


def fill_weights(w, wqv, wk):
    wqv[0:128, :] = jnp.transpose(w[:, 0:128].astype(F32)).astype(BF16)
    wqv[128:256, :] = jnp.transpose(w[:, 256:384].astype(F32)).astype(BF16)
    keys = w[:, 128:256].astype(F32)
    turned = pltpu.roll(keys, 64, 1)
    lane = iota((128, 128), 1)
    zero = jnp.zeros((128, 128), F32)
    wk[0:128, 0:128] = jnp.where(lane < 64, keys, zero).astype(BF16)
    wk[0:128, 128:256] = jnp.where(lane < 64, turned, zero).astype(BF16)
    wk[128:256, 0:128] = jnp.where(lane >= 64, turned, zero).astype(BF16)
    wk[128:256, 128:256] = jnp.where(lane >= 64, keys, zero).astype(BF16)


def mask(*conditions):
    lane = iota((64, 128), 1)
    sides = {"1": lane < 64, "2": lane >= 64, "up": (lane & 32) == 0, "down": (lane & 32) > 0}
    sides |= {"left": (lane & 4) == 0, "right": (lane & 4) > 0}
    keep = sides[conditions[0]]
    for name in conditions[1:]:
        keep = keep & sides[name]
    return jnp.where(keep, 1.0, 0.0).astype(BF16)


def side_by_side(tokens, wk):
    pairs = tokens.reshape(-1, 2, 64, 128)
    lanes = cat([cat([pairs[p, 0], pairs[p, 1]], 1) for p in range(pairs.shape[0])])
    return dot(lanes, wk).astype(BF16)


def attention(queries, keys, values, units):
    zero = jnp.zeros((32, 128), BF16)
    scores = []
    for u, (pairs, masks, bias) in enumerate(units):
        q = queries[:, 128 * u : 128 * u + 128]
        for half in range(2):
            r = 64 * half
            rows = []
            for m in masks:
                rows.append(cat([q[r : r + 32] * m[0:32], zero], 1))
                rows.append(cat([zero, q[r + 32 : r + 64] * m[0:32]], 1))
            k = cat([keys[64 * p : 64 * p + 64, 128 * half : 128 * half + 128] for p in pairs], 1)
            scores.append(dot(k, cat(rows)))
    for u, (pairs, masks, bias) in enumerate(units):
        for half in range(2):
            s = scores[2 * u + half] * SCALE + bias[:, 256 * half : 256 * half + 256]
            p = jnp.exp2(s - jnp.max(s, axis=0, keepdims=True))
            part = 1.0 / jnp.sum(p, axis=0, keepdims=True)
            scores[2 * u + half] = (p * part).astype(BF16)
    context = []
    for u, (pairs, masks, bias) in enumerate(units):
        out = []
        for half in range(2):
            r = 64 * half
            p = scores[2 * u + half]
            seen = cat([cat([p[:, 0:128] * m, p[:, 128:256] * m], 1) for m in masks])
            v = cat([values[r : r + 64, 128 * j : 128 * j + 128] for j in pairs], 1)
            ct = dot(v, seen)
            out += [ct[0:32, 0:128], ct[32:64, 128:256]]
        context.append(cat(out).astype(BF16))
    return cat(context, 1)


def finish(z, context, wo, gain, we, ws):
    middle = z + dot(context, wo, TN).astype(BF16).astype(F32)
    normed = layer_norm(middle, gain).astype(BF16)
    size = min(CHUNK, z.shape[0])
    hidden = [dot(normed[i : i + size], we) for i in range(0, z.shape[0], size)]
    hidden = [twice_gelu(h).astype(BF16) for h in hidden]
    return middle + 0.5 * cat([dot(h, ws) for h in hidden])


def half_turn(x):
    return pltpu.roll(x.reshape(-1, 8, 128), 4, 1)


def low_half(shape):
    return iota(shape, 1) < 4


def windows_of(block):
    parts = block.astype(F32).reshape(8, 2, 8, 128)
    return [parts[:, 0].reshape(64, 128), parts[:, 1].reshape(64, 128)]


def shifted_columns(tokens):
    pairs = tokens.reshape(-1, 2, 64, 128)
    a, b = half_turn(pairs[:, 0]), half_turn(pairs[:, 1])
    low = low_half(a.shape)
    return jnp.where(low, a, b).reshape(-1, 128), jnp.where(low, b, a).reshape(-1, 128)


def edges(outer):
    pairs = outer.reshape(-1, 2, 8, 128)
    even, odd = pairs[:, 0], pairs[:, 1]
    low = low_half(even.shape)
    right = jnp.where(low, even, pltpu.roll(odd, 4, 1)).reshape(-1, 128)
    left = jnp.where(low, pltpu.roll(even, 4, 1), odd).reshape(-1, 128)
    return right.astype(BF16), left.astype(BF16)


def goes_first():
    row, rows = lax.axis_index("gy"), lax.axis_size("gy")
    return lax.rem(row, rows // 2) < rows // 8


def own_block(
    x_ref, w_ref, wo_ref, we_ref, ws_ref, ag_ref, pb_ref, hg_ref,
    fa_ref, fb_ref, na_ref, nb_ref, right_ref, left_ref, bias_ref, wqv_ref, wk_ref,
):
    for head, yj, values in bias_rows(pb_ref, 0):
        bias_ref[yj * 8 : yj * 8 + 8, head * 128 : head * 128 + 128] = values
    fill_weights(w_ref[0], wqv_ref, wk_ref)
    bands = x_ref.shape[0] // WIN
    z = cat([t for b in range(bands) for t in windows_of(x_ref[WIN * b : WIN * b + WIN])])
    normed = layer_norm(z, ag_ref[0:1, :]).astype(BF16)
    qv = dot(wqv_ref[...], normed, NT).astype(BF16)
    keys = side_by_side(normed, wk_ref[...])
    masks = [mask("1"), mask("2")]
    units = [([b], masks, bias_ref[...]) for b in range(bands)]
    context = attention(qv[0:128], keys, qv[128:256], units)
    out = finish(z, context, wo_ref[0], hg_ref[0:1, :], we_ref[0], ws_ref[0])
    fa_ref[...], fb_ref[...] = shifted_columns(out)
    na, nb = shifted_columns(layer_norm(out, ag_ref[1:2, :]))
    na_ref[...] = na.astype(BF16)
    nb_ref[...] = nb.astype(BF16)
    right_ref[...], left_ref[...] = edges(nb)


def start_kernel(out_ref):
    out_ref[...] = jnp.zeros(out_ref.shape, jnp.int32)


def edge_rows_kernel(x_ref, start_ref, ag_ref, pb_ref, hg_ref, last_ref, first_ref, sems):
    bottom = x_ref.shape[0] - WIN
    copies = [
        pltpu.make_async_copy(x_ref.at[pl.ds(bottom, WIN)], last_ref, sems.at[0]),
        pltpu.make_async_copy(x_ref.at[pl.ds(0, WIN)], first_ref, sems.at[1]),
    ]
    for copy in copies:
        copy.start()
    for copy in copies:
        copy.wait()


def first_kernel(*refs):
    own_block(*refs[0:8], *refs[10:])


def nothing_kernel(*refs):
    pass


def second_kernel(*refs):
    @pl.when(jnp.logical_not(goes_first()))
    def _():
        own_block(*refs[0:8], *refs[17:])


def halo_kernel(
    up_ref, down_ref, own_right_ref, own_left_ref, bias_ref, wqv_ref, wk_ref, wo_ref, we_ref, ws_ref, ag_ref, hg_ref,
    na_ref, nb_ref, cols_odd_ref, cols_even_ref, cols_early_ref,
):
    z = cat(windows_of(down_ref[...]) + windows_of(up_ref[...]))
    normed = layer_norm(z, ag_ref[0:1, :]).astype(BF16)
    keys = side_by_side(normed, wk_ref[...])
    values = dot(wqv_ref[128:256, :], normed, NT).astype(BF16)

    def wanted(t):
        return cat([t[0:32], t[160:192], t[64:96], t[224:256]])

    queries = dot(wqv_ref[0:128, :], wanted(normed), NT).astype(BF16)
    masks = [mask("1", "up"), mask("2", "up"), mask("1", "down"), mask("2", "down")]
    context = attention(queries, keys, values, [([0, 1], masks, bias_ref[...])])
    out = finish(wanted(z), context, wo_ref[0], hg_ref[0:1, :], we_ref[0], ws_ref[0])
    na, nb = shifted_columns(layer_norm(out, ag_ref[1:2, :]))
    na_ref[...] = na.astype(BF16)
    nb_ref[...] = nb.astype(BF16)
    right, left = edges(nb)
    n = own_right_ref.shape[0]
    col_odd = lax.rem(lax.axis_index("gx"), 2) == 1
    for at, size, a, b in [(0, n, own_right_ref[...], own_left_ref[...]), (n, 32, right, left)]:
        a, b = a.astype(F32), b.astype(F32)
        cols_odd_ref[at : at + size, :] = jnp.where(col_odd, a, b).astype(BF16)
        cols_even_ref[at : at + size, :] = jnp.where(col_odd, b, a).astype(BF16)
        cols_early_ref[at : at + size, :] = jnp.where(col_odd, b, a).astype(BF16)


def middle_kernel(
    fa_ref, na_ref, va_ref, pb_ref, w_ref, wo_ref, we_ref, ws_ref, hg_ref,
    out_ref, bias_b, bias_bv, wqv_ref, wk_ref,
    bias_a, bias_av,
):
    sub = iota((8, 128), 0)
    lane = iota((8, 128), 1)
    query_left = (lane & 4) == 0
    query_up = (lane & 32) == 0
    row, col = lax.axis_index("gy"), lax.axis_index("gx")
    last_col = jnp.where(query_left, lax.axis_size("gx") - 1, 0) == col
    last_row = jnp.where(query_up, lax.axis_size("gy") - 1, 0) == row
    cut_col = last_col & (query_left != (sub < 4))
    for head, yj, values in bias_rows(pb_ref, 1):
        at = (slice(yj * 8, yj * 8 + 8), slice(head * 128, head * 128 + 128))
        cut = values - 100.0 * LOG2E
        cut_row = (lane >= 64) & last_row & (jnp.logical_not(query_up) if yj < 4 else query_up)
        bias_a[at] = values
        bias_av[at] = jnp.where(cut_row, cut, values)
        bias_b[at] = jnp.where(cut_col, cut, values)
        bias_bv[at] = jnp.where(cut_row | cut_col, cut, values)
    fill_weights(w_ref[1], wqv_ref, wk_ref)
    n = na_ref.shape[0]
    inner = na_ref[32 : n - 32, :]
    first = cat([va_ref[32:64, :], na_ref[0:32, :]])
    last = cat([na_ref[n - 32 : n, :], va_ref[0:32, :]])
    looked_at = cat([inner, last, first, first])
    keys = side_by_side(looked_at, wk_ref[...])
    values = dot(wqv_ref[128:256, :], looked_at, NT).astype(BF16)
    wanted = cat([na_ref[32:n, :], na_ref[0:32, :]])
    queries = dot(wqv_ref[0:128, :], wanted, NT).astype(BF16)
    last_unit = n // 128 - 1
    masks = [mask("1"), mask("2")]
    units = [([u], masks, bias_a[...]) for u in range(last_unit)]
    masks = [mask("1"), mask("2", "up"), mask("2", "down"), jnp.zeros((64, 128), BF16)]
    units.append(([last_unit, last_unit + 1], masks, bias_av[...]))
    context = attention(queries, keys, values, units)
    z = cat([fa_ref[32:n, :], fa_ref[0:32, :]])
    out = finish(z, context, wo_ref[1], hg_ref[1:2, :], we_ref[1], ws_ref[1])
    out = half_turn(out).reshape(n, 128)
    out_ref[32:n, :] = out[0 : n - 32]
    out_ref[0:32, :] = out[n - 32 : n]


def outer_kernel(
    fb_ref, nb_ref, vb_ref, early_ref, odd_ref, even_ref, oa_ref, bias_b, bias_bv, wqv_ref, wk_ref, wo_ref, we_ref, ws_ref, hg_ref,
    out_ref,
):
    n = nb_ref.shape[0]
    h = n // 2

    def in_order(ref, end, size):
        rows = cat([ref[end + size : end + 2 * size, :], ref[0:end, :], ref[end : end + size, :]])
        return rows.astype(F32).reshape(-1, 8, 128)

    own = cat([vb_ref[32:64, :], nb_ref[...], vb_ref[0:32, :]]).astype(F32).reshape(-1, 8, 128)
    is_early = swaps_early(lax.axis_index("gx"), lax.axis_size("gx"))
    odd = in_order(odd_ref, h, 16)
    even = jnp.where(is_early, in_order(early_ref, h, 16), in_order(even_ref, h, 16))
    col_odd = lax.rem(lax.axis_index("gx"), 2) == 1
    hl, hr = jnp.where(col_odd, even, odd), jnp.where(col_odd, odd, even)
    low = low_half(hl.shape)
    even = jnp.where(low, hl, pltpu.roll(hr, 4, 1))
    odd = jnp.where(low, pltpu.roll(hl, 4, 1), hr)
    halo = jnp.stack([even, odd], axis=1).reshape(own.shape)
    low = low_half(own.shape)
    right = jnp.where(low, own, halo).reshape(-1, 64, 128).astype(BF16)
    left = jnp.where(low, halo, own).reshape(-1, 64, 128).astype(BF16)
    count = right.shape[0]
    looked_at = cat([t for w in range(count) for t in (right[w], left[w])])
    keys = side_by_side(looked_at, wk_ref[...])
    values = dot(wqv_ref[128:256, :], looked_at, NT).astype(BF16)
    wanted = cat([nb_ref[32:n, :], nb_ref[0:32, :]])
    queries = dot(wqv_ref[0:128, :], wanted, NT).astype(BF16)
    masks = [mask(w, s) for w in "12" for s in ("left", "right")]
    units = [([w, w + 1], masks, bias_b[...]) for w in range(1, count - 2, 2)]
    masks = masks[0:2] + [mask("2", v, s) for v in ("up", "down") for s in ("left", "right")]
    units.append(([count - 2, count - 1, 0], masks, bias_bv[...]))
    context = attention(queries, keys, values, units)
    z = cat([fb_ref[32:n, :], fb_ref[0:32, :]])
    out = finish(z, context, wo_ref[1], hg_ref[1:2, :], we_ref[1], ws_ref[1])
    out = half_turn(out)
    rows = n // 8
    out = cat([out[rows - 4 :], out[: rows - 4]])
    inner = oa_ref[...].reshape(rows, 8, 128)
    low = low_half(out.shape)
    out_ref[:, 0:8, :] = jnp.where(low, out, inner)
    out_ref[:, 8:16, :] = jnp.where(low, inner, out)


def vmem(count):
    return [pl.BlockSpec(memory_space=pltpu.VMEM)] * count


def call(kernel, name, operands, outs, scratch=(), flops=0, aliases=None):
    shapes = [jax.ShapeDtypeStruct(shape, dtype) for shape, dtype in outs]
    return pl.pallas_call(
        kernel,
        out_shape=shapes,
        in_specs=vmem(len(operands)),
        out_specs=vmem(len(outs)),
        scratch_shapes=list(scratch),
        input_output_aliases=aliases or {},
        compiler_params=pltpu.CompilerParams(vmem_limit_bytes=32 * 1024 * 1024),
        cost_estimate=pl.CostEstimate(flops=flops, bytes_accessed=1 << 20, transcendentals=0),
        name=name,
    )(*operands)


def on_device(x, ag, tw, ow, pb, hg, ew, sw):
    height, breadth = x.shape[0], x.shape[1]
    n = height * WIN
    table = ((64, HEADS * 128), F32)
    prepared = [((256, 128), BF16), ((256, 256), BF16)]
    weights = (x, tw, ow, ew, sw, ag, pb, hg)
    kept = [((n, C), F32)] * 2 + [((n, C), BF16)] * 2 + [((n // 2, C), BF16)] * 2 + [table] + prepared
    rows = [((WIN, breadth, C), BF16)] * 2
    (start,) = call(start_kernel, "start", (), [((8, 128), jnp.int32)], (), 4 * 10**10)
    last, first = call(
        edge_rows_kernel, "edge_rows", (x, start, ag, pb, hg), rows, [pltpu.SemaphoreType.DMA((2,))]
    )

    def run(*operands):
        return call(first_kernel, "first", operands, rows[0:1] + kept, (), 4 * 10**9, {8: 0})

    def skip(*operands):
        return call(nothing_kernel, "nothing", operands[8:9], rows[0:1] + kept, (), 0, {0: 0})

    up = shift(last, "gy", 1)
    first, *state = lax.cond(goes_first(), run, skip, *weights, first)
    down = shift(first, "gy", -1)
    state = call(
        second_kernel, "second", (*weights, *state), kept, (), 4 * 10**9, {8 + i: i for i in range(9)}
    )
    fa, fb, na, nb, right, left, bias, wqv, wk = state
    va, vb, odd, even, early = call(
        halo_kernel, "halo", (up, down, right, left, bias, wqv, wk, ow, ew, sw, ag, hg),
        [((64, C), BF16)] * 2 + [((n // 2 + 32, C), BF16)] * 3, (), 10**9,
    )
    early = near_first(early, "gx")
    odd = swap(odd, "gx", 1)
    even = near_last(even, "gx")
    oa, bias_b, bias_bv, wqv, wk = call(
        middle_kernel, "middle", (fa, na, va, pb, tw, ow, ew, sw, hg),
        [((n, C), F32), table, table] + prepared, [pltpu.VMEM(*table)] * 2, 2 * 10**9,
    )
    return call(
        outer_kernel, "outer", (fb, nb, vb, early, odd, even, oa, bias_b, bias_bv, wqv, wk, ow, ew, sw, hg),
        [((height, breadth, C), F32)], (), 2 * 10**9,
    )[0]


def solution(mesh):
    return jax.shard_map(
        on_device,
        mesh=mesh,
        in_specs=(P("gy", "gx", None), P(), P(), P(), P(), P(), P(), P()),
        out_specs=P("gy", "gx", None),
        check_vma=False,
    )
```

```python
import math

import jax
import jax.numpy as jnp
from jax import lax
from jax.experimental import pallas as pl
from jax.experimental.pallas import tpu as pltpu
from jax.sharding import PartitionSpec as P

C = 128
HEADS = 4
HID = 512
WIN = 8
HD = 32
EPSILON = 1e-05
LOG2E = math.log2(math.e)
SCALE = HD ** (-0.5) * LOG2E
F32 = jnp.float32
BF16 = jnp.bfloat16
NT = (((1,), (1,)), ((), ()))
TN = (((0,), (0,)), ((), ()))
CHUNK = 256


def shift(x, axis, by):
    length = lax.axis_size(axis)
    return lax.ppermute(x, axis, [(i, (i + by) % length) for i in range(length)])


def swap(x, axis, first):
    length = lax.axis_size(axis)
    there = [(i, (i + 1) % length) for i in range(first, length, 2)]
    return lax.ppermute(x, axis, there + [(b, a) for a, b in there])


def iota(shape, dim):
    return lax.broadcasted_iota(jnp.int32, shape, dim)


def dot(a, b, dims=None):
    if dims is None:
        return jnp.dot(a, b, preferred_element_type=F32)
    return lax.dot_general(a, b, dims, preferred_element_type=F32)


def cat(parts, axis=0):
    return jnp.concatenate(parts, axis=axis)


def layer_norm(x, gain):
    center = x - jnp.mean(x, axis=-1, keepdims=True)
    spread = jnp.sum(center * center, axis=-1, keepdims=True)
    return center * lax.rsqrt(spread + C * EPSILON) * (gain * C**0.5)


def twice_gelu(x):
    return x + x * lax.erf(x * (0.5**0.5))


def bias_rows(pb_ref, block):
    sub = iota((8, 128), 0)
    lane = iota((8, 128), 1)
    place = lax.min((lane >> 3) * 15 + 7 + (lane & 7) - sub, 224)
    for head in range(HEADS):
        low = jnp.broadcast_to(pb_ref[block, head : head + 1, 0:128], (8, 128))
        high = jnp.broadcast_to(pb_ref[block, head : head + 1, 97:225], (8, 128))
        strip = jnp.where(
            place < 128,
            jnp.take_along_axis(low, lax.min(place, 127), axis=1),
            jnp.take_along_axis(high, lax.max(place - 97, 0), axis=1),
        )
        strip = strip * LOG2E
        for yj in range(8):
            turn = (128 - (7 - yj) * 8) % 128
            first = pltpu.roll(strip, turn, 1) if turn else strip
            second = pltpu.roll(strip, (turn + 64) % 128, 1)
            yield head, yj, jnp.where(lane < 64, first, second)


def fill_weights(w, wqv, wk):
    wqv[0:128, :] = jnp.transpose(w[:, 0:128].astype(F32)).astype(BF16)
    wqv[128:256, :] = jnp.transpose(w[:, 256:384].astype(F32)).astype(BF16)
    keys = w[:, 128:256].astype(F32)
    turned = pltpu.roll(keys, 64, 1)
    lane = iota((128, 128), 1)
    zero = jnp.zeros((128, 128), F32)
    wk[0:128, 0:128] = jnp.where(lane < 64, keys, zero).astype(BF16)
    wk[0:128, 128:256] = jnp.where(lane < 64, turned, zero).astype(BF16)
    wk[128:256, 0:128] = jnp.where(lane >= 64, turned, zero).astype(BF16)
    wk[128:256, 128:256] = jnp.where(lane >= 64, keys, zero).astype(BF16)


def mask(*conditions):
    lane = iota((64, 128), 1)
    sides = {"1": lane < 64, "2": lane >= 64, "up": (lane & 32) == 0, "down": (lane & 32) > 0}
    sides |= {"left": (lane & 4) == 0, "right": (lane & 4) > 0}
    keep = sides[conditions[0]]
    for name in conditions[1:]:
        keep = keep & sides[name]
    return jnp.where(keep, 1.0, 0.0).astype(BF16)


def side_by_side(tokens, wk):
    pairs = tokens.reshape(-1, 2, 64, 128)
    lanes = cat([cat([pairs[p, 0], pairs[p, 1]], 1) for p in range(pairs.shape[0])])
    return dot(lanes, wk).astype(BF16)


def attention(queries, keys, values, units):
    zero = jnp.zeros((32, 128), BF16)
    scores = []
    for u, (pairs, masks, bias) in enumerate(units):
        q = queries[:, 128 * u : 128 * u + 128]
        for half in range(2):
            r = 64 * half
            rows = []
            for m in masks:
                rows.append(cat([q[r : r + 32] * m[0:32], zero], 1))
                rows.append(cat([zero, q[r + 32 : r + 64] * m[0:32]], 1))
            k = cat([keys[64 * p : 64 * p + 64, 128 * half : 128 * half + 128] for p in pairs], 1)
            scores.append(dot(k, cat(rows)))
    for u, (pairs, masks, bias) in enumerate(units):
        for half in range(2):
            s = scores[2 * u + half] * SCALE + bias[:, 256 * half : 256 * half + 256]
            p = jnp.exp2(s - jnp.max(s, axis=0, keepdims=True))
            part = 1.0 / jnp.sum(p, axis=0, keepdims=True)
            scores[2 * u + half] = (p * part).astype(BF16)
    context = []
    for u, (pairs, masks, bias) in enumerate(units):
        out = []
        for half in range(2):
            r = 64 * half
            p = scores[2 * u + half]
            seen = cat([cat([p[:, 0:128] * m, p[:, 128:256] * m], 1) for m in masks])
            v = cat([values[r : r + 64, 128 * j : 128 * j + 128] for j in pairs], 1)
            ct = dot(v, seen)
            out += [ct[0:32, 0:128], ct[32:64, 128:256]]
        context.append(cat(out).astype(BF16))
    return cat(context, 1)


def finish(z, context, wo, gain, we, ws):
    middle = z + dot(context, wo, TN).astype(BF16).astype(F32)
    normed = layer_norm(middle, gain).astype(BF16)
    size = min(CHUNK, z.shape[0])
    hidden = [dot(normed[i : i + size], we) for i in range(0, z.shape[0], size)]
    hidden = [twice_gelu(h).astype(BF16) for h in hidden]
    return middle + 0.5 * cat([dot(h, ws) for h in hidden])


def half_turn(x):
    return pltpu.roll(x.reshape(-1, 8, 128), 4, 1)


def low_half(shape):
    return iota(shape, 1) < 4


def windows_of(block):
    parts = block.astype(F32).reshape(8, 2, 8, 128)
    return [parts[:, 0].reshape(64, 128), parts[:, 1].reshape(64, 128)]


def shifted_columns(tokens):
    pairs = tokens.reshape(-1, 2, 64, 128)
    a, b = half_turn(pairs[:, 0]), half_turn(pairs[:, 1])
    low = low_half(a.shape)
    return jnp.where(low, a, b).reshape(-1, 128), jnp.where(low, b, a).reshape(-1, 128)


def edges(outer):
    pairs = outer.reshape(-1, 2, 8, 128)
    even, odd = pairs[:, 0], pairs[:, 1]
    low = low_half(even.shape)
    right = jnp.where(low, even, pltpu.roll(odd, 4, 1)).reshape(-1, 128)
    left = jnp.where(low, pltpu.roll(even, 4, 1), odd).reshape(-1, 128)
    return right, left


def goes_first():
    row, rows = lax.axis_index("gy"), lax.axis_size("gy")
    return lax.rem(row, rows // 2) < rows // 8


def own_block(
    x_ref, w_ref, wo_ref, we_ref, ws_ref, ag_ref, pb_ref, hg_ref,
    fa_ref, fright_ref, fleft_ref, na_ref, right_ref, left_ref, bias_ref, wqv_ref, wk_ref,
):
    for head, yj, values in bias_rows(pb_ref, 0):
        bias_ref[yj * 8 : yj * 8 + 8, head * 128 : head * 128 + 128] = values
    fill_weights(w_ref[0], wqv_ref, wk_ref)
    bands = x_ref.shape[0] // WIN
    z = cat([t for b in range(bands) for t in windows_of(x_ref[WIN * b : WIN * b + WIN])])
    normed = layer_norm(z, ag_ref[0:1, :]).astype(BF16)
    qv = dot(wqv_ref[...], normed, NT).astype(BF16)
    keys = side_by_side(normed, wk_ref[...])
    masks = [mask("1"), mask("2")]
    units = [([b], masks, bias_ref[...]) for b in range(bands)]
    context = attention(qv[0:128], keys, qv[128:256], units)
    out = finish(z, context, wo_ref[0], hg_ref[0:1, :], we_ref[0], ws_ref[0])
    fa_ref[...], fb = shifted_columns(out)
    fright_ref[...], fleft_ref[...] = edges(fb)
    na, nb = shifted_columns(layer_norm(out, ag_ref[1:2, :]))
    na_ref[...] = na.astype(BF16)
    right, left = edges(nb)
    right_ref[...] = right.astype(BF16)
    left_ref[...] = left.astype(BF16)


def start_kernel(out_ref):
    out_ref[...] = jnp.zeros(out_ref.shape, jnp.int32)


def edge_rows_kernel(x_ref, start_ref, ag_ref, pb_ref, hg_ref, last_ref, first_ref, sems):
    bottom = x_ref.shape[0] - WIN
    copies = [
        pltpu.make_async_copy(x_ref.at[pl.ds(bottom, WIN)], last_ref, sems.at[0]),
        pltpu.make_async_copy(x_ref.at[pl.ds(0, WIN)], first_ref, sems.at[1]),
    ]
    for copy in copies:
        copy.start()
    for copy in copies:
        copy.wait()


def first_kernel(*refs):
    own_block(*refs[0:8], *refs[10:])


def nothing_kernel(*refs):
    pass


def second_kernel(*refs):
    @pl.when(jnp.logical_not(goes_first()))
    def _():
        own_block(*refs[0:8], *refs[17:])


def halo_kernel(
    up_ref, down_ref, own_right_ref, own_left_ref, bias_ref, wqv_ref, wk_ref, wo_ref, we_ref, ws_ref, ag_ref, hg_ref,
    na_ref, cols_odd_ref, cols_even_ref,
):
    z = cat(windows_of(down_ref[...]) + windows_of(up_ref[...]))
    normed = layer_norm(z, ag_ref[0:1, :]).astype(BF16)
    keys = side_by_side(normed, wk_ref[...])
    values = dot(wqv_ref[128:256, :], normed, NT).astype(BF16)

    def wanted(t):
        return cat([t[0:32], t[160:192], t[64:96], t[224:256]])

    queries = dot(wqv_ref[0:128, :], wanted(normed), NT).astype(BF16)
    masks = [mask("1", "up"), mask("2", "up"), mask("1", "down"), mask("2", "down")]
    context = attention(queries, keys, values, [([0, 1], masks, bias_ref[...])])
    out = finish(wanted(z), context, wo_ref[0], hg_ref[0:1, :], we_ref[0], ws_ref[0])
    na, nb = shifted_columns(layer_norm(out, ag_ref[1:2, :]))
    na_ref[...] = na.astype(BF16)
    right, left = edges(nb)
    n = own_right_ref.shape[0]
    col_odd = lax.rem(lax.axis_index("gx"), 2) == 1
    for at, size, a, b in [(0, n, own_right_ref[...], own_left_ref[...]), (n, 32, right, left)]:
        a, b = a.astype(F32), b.astype(F32)
        cols_odd_ref[at : at + size, :] = jnp.where(col_odd, a, b).astype(BF16)
        cols_even_ref[at : at + size, :] = jnp.where(col_odd, b, a).astype(BF16)


def border_bias(pb_ref, block, tables):
    sub = iota((8, 128), 0)
    lane = iota((8, 128), 1)
    yi = (lane >> 2) & 7
    row, rows = lax.axis_index("gy"), lax.axis_size("gy")
    col, cols = lax.axis_index("gx"), lax.axis_size("gx")
    is_odd = lax.rem(col, 2) == 1
    last_row = (lane >= 96) & (jnp.where(yi < 4, rows - 1, 0) == row)
    for head in range(HEADS):
        low = jnp.broadcast_to(pb_ref[block, head : head + 1, 0:128], (8, 128))
        high = jnp.broadcast_to(pb_ref[block, head : head + 1, 97:225], (8, 128))
        for group in range(8):
            yj = 2 * (group % 4) + (sub >> 2)
            cut_row = last_row & ((yi < 4) != (yj < 4))
            plain = (7 + yi - yj) * 15 + 7 + (lane & 3) - (sub & 3)
            for number, (table, table_v) in enumerate(tables):
                if group < 4 and number == 1:
                    values = kept
                    cut = values
                else:
                    is_right = is_odd if number == 0 else jnp.logical_not(is_odd)
                    place = plain if group < 4 else plain + jnp.where(is_right, -4, 4)
                    values = LOG2E * jnp.where(
                        place < 128,
                        jnp.take_along_axis(low, lax.clamp(0, place, 127), axis=1),
                        jnp.take_along_axis(high, lax.clamp(0, place - 97, 127), axis=1),
                    )
                    if group >= 4:
                        outside = jnp.where(is_right, cols - 1, 0) == col
                        values = values - jnp.where(outside, 100.0 * LOG2E, 0.0)
                    kept = values
                at = (slice(group * 8, group * 8 + 8), slice(head * 128, head * 128 + 128))
                table[at] = values
                if group < 4:
                    cut = values - 100.0 * LOG2E
                else:
                    outside = jnp.where(is_right, cols - 1, 0) == col
                    cut = values - jnp.where(outside, 0.0, 100.0 * LOG2E)
                table_v[at] = jnp.where(cut_row, cut, values)


def middle_kernel(
    fa_ref, na_ref, va_ref, pb_ref, w_ref, wo_ref, we_ref, ws_ref, hg_ref,
    out_ref, bias_odd, bias_oddv, bias_even, bias_evenv, wqv_ref, wk_ref,
    bias_a, bias_av,
):
    sub = iota((8, 128), 0)
    lane = iota((8, 128), 1)
    query_up = (lane & 32) == 0
    row = lax.axis_index("gy")
    last_row = jnp.where(query_up, lax.axis_size("gy") - 1, 0) == row
    for head, yj, values in bias_rows(pb_ref, 1):
        at = (slice(yj * 8, yj * 8 + 8), slice(head * 128, head * 128 + 128))
        cut_row = (lane >= 64) & last_row & (jnp.logical_not(query_up) if yj < 4 else query_up)
        bias_a[at] = values
        bias_av[at] = jnp.where(cut_row, values - 100.0 * LOG2E, values)
    border_bias(pb_ref, 1, ((bias_odd, bias_oddv), (bias_even, bias_evenv)))
    fill_weights(w_ref[1], wqv_ref, wk_ref)
    n = na_ref.shape[0]
    inner = na_ref[32 : n - 32, :]
    first = cat([va_ref[32:64, :], na_ref[0:32, :]])
    last = cat([na_ref[n - 32 : n, :], va_ref[0:32, :]])
    looked_at = cat([inner, last, first, first])
    keys = side_by_side(looked_at, wk_ref[...])
    values = dot(wqv_ref[128:256, :], looked_at, NT).astype(BF16)
    wanted = cat([na_ref[32:n, :], na_ref[0:32, :]])
    queries = dot(wqv_ref[0:128, :], wanted, NT).astype(BF16)
    last_unit = n // 128 - 1
    masks = [mask("1"), mask("2")]
    units = [([u], masks, bias_a[...]) for u in range(last_unit)]
    masks = [mask("1"), mask("2", "up"), mask("2", "down"), jnp.zeros((64, 128), BF16)]
    units.append(([last_unit, last_unit + 1], masks, bias_av[...]))
    context = attention(queries, keys, values, units)
    z = cat([fa_ref[32:n, :], fa_ref[0:32, :]])
    out = finish(z, context, wo_ref[1], hg_ref[1:2, :], we_ref[1], ws_ref[1])
    out = half_turn(out).reshape(n, 128)
    out_ref[32:n, :] = out[0 : n - 32]
    out_ref[0:32, :] = out[n - 32 : n]


def border_block(z_ref, own_ref, other_ref, bias_ref, bias_v_ref, wqv_ref, wk_ref, wo_ref, we_ref, ws_ref, hg_ref):
    n = z_ref[0].shape[0]

    def in_order(ref):
        return cat([ref[n + 16 : n + 32, :], ref[0:n, :], ref[n : n + 16, :]])

    own, other = in_order(own_ref), in_order(other_ref)
    count = own.shape[0] // 32
    order = [*range(1, count), 0, 0]
    looked_at = cat([t[32 * w : 32 * w + 32] for w in order for t in (own, other)])
    keys = side_by_side(looked_at, wk_ref[...])
    values = dot(wqv_ref[128:256, :], looked_at, NT).astype(BF16)
    wanted = cat([own_ref[16:n, :], own_ref[0:16, :]])
    queries = dot(wqv_ref[0:128, :], wanted, NT).astype(BF16)
    lane = iota((64, 128), 1)

    def keep(condition):
        return jnp.where(condition, 1.0, 0.0).astype(BF16)

    masks = [keep((lane >> 5) == k) for k in range(4)]
    up = (lane & 16) == 0
    last = [keep((lane >= 96) & up), keep((lane >= 96) & jnp.logical_not(up)), keep(lane < 0)]
    units = [([2 * u, 2 * u + 1], masks, bias_ref[...]) for u in range(n // 128 - 1)]
    first = 2 * len(units)
    units.append(([first, first + 1, first + 2], masks[0:3] + last, bias_v_ref[...]))
    context = attention(queries, keys, values, units)
    is_odd = lax.rem(lax.axis_index("gx"), 2) == 1
    z = jnp.where(is_odd, z_ref[0][...], z_ref[1][...])
    z = cat([z[16:n], z[0:16]])
    out = finish(z, context, wo_ref[1], hg_ref[1:2, :], we_ref[1], ws_ref[1])
    return cat([out[n - 16 : n], out[0 : n - 16]])


def odd_border_kernel(fright_ref, fleft_ref, *refs):
    refs[-1][...] = border_block((fright_ref, fleft_ref), *refs[:-2])


def even_border_kernel(fright_ref, fleft_ref, *refs):
    inner_ref, odd_ref, out_ref = refs[-3:]
    even = border_block((fleft_ref, fright_ref), *refs[:-3])
    odd = odd_ref[...]
    is_odd = lax.rem(lax.axis_index("gx"), 2) == 1
    right = jnp.where(is_odd, odd, even).reshape(-1, 8, 128)
    left = jnp.where(is_odd, even, odd).reshape(-1, 8, 128)
    inner = inner_ref[...].reshape(-1, 8, 128)
    right = jnp.stack([pltpu.roll(right, 4, 1), right], axis=1).reshape(inner.shape)
    left = jnp.stack([left, pltpu.roll(left, 4, 1)], axis=1).reshape(inner.shape)
    low = low_half(inner.shape)
    out_ref[:, 0:8, :] = jnp.where(low, left, inner)
    out_ref[:, 8:16, :] = jnp.where(low, inner, right)


def vmem(count):
    return [pl.BlockSpec(memory_space=pltpu.VMEM)] * count


def call(kernel, name, operands, outs, scratch=(), flops=0, aliases=None):
    shapes = [jax.ShapeDtypeStruct(shape, dtype) for shape, dtype in outs]
    return pl.pallas_call(
        kernel,
        out_shape=shapes,
        in_specs=vmem(len(operands)),
        out_specs=vmem(len(outs)),
        scratch_shapes=list(scratch),
        input_output_aliases=aliases or {},
        compiler_params=pltpu.CompilerParams(vmem_limit_bytes=32 * 1024 * 1024),
        cost_estimate=pl.CostEstimate(flops=flops, bytes_accessed=1 << 20, transcendentals=0),
        name=name,
    )(*operands)


def on_device(x, ag, tw, ow, pb, hg, ew, sw):
    height, breadth = x.shape[0], x.shape[1]
    n = height * WIN
    table = ((64, HEADS * 128), F32)
    prepared = [((256, 128), BF16), ((256, 256), BF16)]
    weights = (x, tw, ow, ew, sw, ag, pb, hg)
    kept = [((n, C), F32)] + [((n // 2, C), F32)] * 2 + [((n, C), BF16)] + [((n // 2, C), BF16)] * 2
    kept += [table] + prepared
    rows = [((WIN, breadth, C), BF16)] * 2
    (start,) = call(start_kernel, "start", (), [((8, 128), jnp.int32)], (), 4 * 10**10)
    last, first = call(
        edge_rows_kernel, "edge_rows", (x, start, ag, pb, hg), rows, [pltpu.SemaphoreType.DMA((2,))]
    )

    def run(*operands):
        return call(first_kernel, "first", operands, rows[0:1] + kept, (), 4 * 10**9, {8: 0})

    def skip(*operands):
        return call(nothing_kernel, "nothing", operands[8:9], rows[0:1] + kept, (), 0, {0: 0})

    up = shift(last, "gy", 1)
    first, *state = lax.cond(goes_first(), run, skip, *weights, first)
    down = shift(first, "gy", -1)
    state = call(
        second_kernel, "second", (*weights, *state), kept, (), 4 * 10**9, {8 + i: i for i in range(9)}
    )
    fa, fright, fleft, na, right, left, bias, wqv, wk = state
    va, odd, even = call(
        halo_kernel, "halo", (up, down, right, left, bias, wqv, wk, ow, ew, sw, ag, hg),
        [((64, C), BF16)] + [((n // 2 + 32, C), BF16)] * 2, (), 10**9,
    )
    from_odd, from_even = swap(odd, "gx", 1), swap(even, "gx", 0)
    oa, *tables, wqv, wk = call(
        middle_kernel, "middle", (fa, na, va, pb, tw, ow, ew, sw, hg),
        [((n, C), F32)] + [table] * 4 + prepared, [pltpu.VMEM(*table)] * 2, 2 * 10**9,
    )
    rest = (wqv, wk, ow, ew, sw, hg)
    (ob,) = call(
        odd_border_kernel, "odd_border", (fright, fleft, odd, from_odd, *tables[0:2], *rest, even),
        [((n // 2, C), F32)], (), 10**9,
    )
    return call(
        even_border_kernel, "even_border", (fright, fleft, even, from_even, *tables[2:4], *rest, oa, ob),
        [((height, breadth, C), F32)], (), 10**9,
    )[0]


def solution(mesh):
    return jax.shard_map(
        on_device,
        mesh=mesh,
        in_specs=(P("gy", "gx", None), P(), P(), P(), P(), P(), P(), P()),
        out_specs=P("gy", "gx", None),
        check_vma=False,
    )
```

```python
import math

import jax
import jax.numpy as jnp
from jax import lax
from jax.experimental import pallas as pl
from jax.experimental.pallas import tpu as pltpu
from jax.sharding import PartitionSpec as P

C = 128
HEADS = 4
HID = 512
WIN = 8
HD = 32
EPSILON = 1e-05
LOG2E = math.log2(math.e)
SCALE = HD ** (-0.5) * LOG2E
F32 = jnp.float32
BF16 = jnp.bfloat16
NT = (((1,), (1,)), ((), ()))
TN = (((0,), (0,)), ((), ()))
CHUNK = 256


def shift(x, axis, by):
    length = lax.axis_size(axis)
    return lax.ppermute(x, axis, [(i, (i + by) % length) for i in range(length)])


def swap(x, axis, first):
    length = lax.axis_size(axis)
    there = [(i, (i + 1) % length) for i in range(first, length, 2)]
    return lax.ppermute(x, axis, there + [(b, a) for a, b in there])


def iota(shape, dim):
    return lax.broadcasted_iota(jnp.int32, shape, dim)


def dot(a, b, dims=None):
    if dims is None:
        return jnp.dot(a, b, preferred_element_type=F32)
    return lax.dot_general(a, b, dims, preferred_element_type=F32)


def cat(parts, axis=0):
    return jnp.concatenate(parts, axis=axis)


def layer_norm(x, gain):
    center = x - jnp.mean(x, axis=-1, keepdims=True)
    spread = jnp.sum(center * center, axis=-1, keepdims=True)
    return center * lax.rsqrt(spread + C * EPSILON) * (gain * C**0.5)


def twice_gelu(x):
    return x + x * lax.erf(x * (0.5**0.5))


def bias_rows(pb_ref, block):
    sub = iota((8, 128), 0)
    lane = iota((8, 128), 1)
    place = lax.min((lane >> 3) * 15 + 7 + (lane & 7) - sub, 224)
    for head in range(HEADS):
        low = jnp.broadcast_to(pb_ref[block, head : head + 1, 0:128], (8, 128))
        high = jnp.broadcast_to(pb_ref[block, head : head + 1, 97:225], (8, 128))
        strip = jnp.where(
            place < 128,
            jnp.take_along_axis(low, lax.min(place, 127), axis=1),
            jnp.take_along_axis(high, lax.max(place - 97, 0), axis=1),
        )
        strip = strip * LOG2E
        for yj in range(8):
            turn = (128 - (7 - yj) * 8) % 128
            first = pltpu.roll(strip, turn, 1) if turn else strip
            second = pltpu.roll(strip, (turn + 64) % 128, 1)
            yield head, yj, jnp.where(lane < 64, first, second)


def fill_weights(w, wqv, wk):
    wqv[0:128, :] = jnp.transpose(w[:, 0:128].astype(F32)).astype(BF16)
    wqv[128:256, :] = jnp.transpose(w[:, 256:384].astype(F32)).astype(BF16)
    keys = w[:, 128:256].astype(F32)
    turned = pltpu.roll(keys, 64, 1)
    lane = iota((128, 128), 1)
    zero = jnp.zeros((128, 128), F32)
    wk[0:128, 0:128] = jnp.where(lane < 64, keys, zero).astype(BF16)
    wk[0:128, 128:256] = jnp.where(lane < 64, turned, zero).astype(BF16)
    wk[128:256, 0:128] = jnp.where(lane >= 64, turned, zero).astype(BF16)
    wk[128:256, 128:256] = jnp.where(lane >= 64, keys, zero).astype(BF16)


def mask(*conditions):
    lane = iota((64, 128), 1)
    sides = {"1": lane < 64, "2": lane >= 64, "up": (lane & 32) == 0, "down": (lane & 32) > 0}
    sides |= {"left": (lane & 4) == 0, "right": (lane & 4) > 0}
    keep = sides[conditions[0]]
    for name in conditions[1:]:
        keep = keep & sides[name]
    return jnp.where(keep, 1.0, 0.0).astype(BF16)


def side_by_side(tokens, wk):
    pairs = tokens.reshape(-1, 2, 64, 128)
    lanes = cat([cat([pairs[p, 0], pairs[p, 1]], 1) for p in range(pairs.shape[0])])
    return dot(lanes, wk).astype(BF16)


def attention(queries, keys, values, units):
    zero = jnp.zeros((32, 128), BF16)
    scores = []
    for u, (pairs, masks, bias) in enumerate(units):
        q = queries[:, 128 * u : 128 * u + 128]
        for half in range(2):
            r = 64 * half
            rows = []
            for m in masks:
                rows.append(cat([q[r : r + 32] * m[0:32], zero], 1))
                rows.append(cat([zero, q[r + 32 : r + 64] * m[0:32]], 1))
            k = cat([keys[64 * p : 64 * p + 64, 128 * half : 128 * half + 128] for p in pairs], 1)
            scores.append(dot(k, cat(rows)))
    for u, (pairs, masks, bias) in enumerate(units):
        for half in range(2):
            s = scores[2 * u + half] * SCALE + bias[:, 256 * half : 256 * half + 256]
            p = jnp.exp2(s - jnp.max(s, axis=0, keepdims=True))
            part = 1.0 / jnp.sum(p, axis=0, keepdims=True)
            scores[2 * u + half] = (p * part).astype(BF16)
    context = []
    for u, (pairs, masks, bias) in enumerate(units):
        out = []
        for half in range(2):
            r = 64 * half
            p = scores[2 * u + half]
            seen = cat([cat([p[:, 0:128] * m, p[:, 128:256] * m], 1) for m in masks])
            v = cat([values[r : r + 64, 128 * j : 128 * j + 128] for j in pairs], 1)
            ct = dot(v, seen)
            out += [ct[0:32, 0:128], ct[32:64, 128:256]]
        context.append(cat(out).astype(BF16))
    return cat(context, 1)


def finish(z, context, wo, gain, we, ws):
    middle = z + dot(context, wo, TN).astype(BF16).astype(F32)
    normed = layer_norm(middle, gain).astype(BF16)
    size = min(CHUNK, z.shape[0])
    hidden = [dot(normed[i : i + size], we) for i in range(0, z.shape[0], size)]
    hidden = [twice_gelu(h).astype(BF16) for h in hidden]
    return middle + 0.5 * cat([dot(h, ws) for h in hidden])


def half_turn(x):
    return pltpu.roll(x.reshape(-1, 8, 128), 4, 1)


def low_half(shape):
    return iota(shape, 1) < 4


def windows_of(block):
    parts = block.astype(F32).reshape(8, 2, 8, 128)
    return [parts[:, 0].reshape(64, 128), parts[:, 1].reshape(64, 128)]


def shifted_columns(tokens):
    pairs = tokens.reshape(-1, 2, 64, 128)
    a, b = half_turn(pairs[:, 0]), half_turn(pairs[:, 1])
    low = low_half(a.shape)
    return jnp.where(low, a, b).reshape(-1, 128), jnp.where(low, b, a).reshape(-1, 128)


def edges(outer):
    pairs = outer.reshape(-1, 2, 8, 128)
    even, odd = pairs[:, 0], pairs[:, 1]
    low = low_half(even.shape)
    right = jnp.where(low, even, pltpu.roll(odd, 4, 1)).reshape(-1, 128)
    left = jnp.where(low, pltpu.roll(even, 4, 1), odd).reshape(-1, 128)
    return right, left


def goes_first():
    row, rows = lax.axis_index("gy"), lax.axis_size("gy")
    return lax.rem(row, rows // 2) < rows // 8


def own_block(
    x_ref, w_ref, wo_ref, we_ref, ws_ref, ag_ref, pb_ref, hg_ref,
    fa_ref, fright_ref, fleft_ref, na_ref, right_ref, left_ref, bias_ref, wqv_ref, wk_ref,
):
    for head, yj, values in bias_rows(pb_ref, 0):
        bias_ref[yj * 8 : yj * 8 + 8, head * 128 : head * 128 + 128] = values
    fill_weights(w_ref[0], wqv_ref, wk_ref)
    bands = x_ref.shape[0] // WIN
    z = cat([t for b in range(bands) for t in windows_of(x_ref[WIN * b : WIN * b + WIN])])
    normed = layer_norm(z, ag_ref[0:1, :]).astype(BF16)
    qv = dot(wqv_ref[...], normed, NT).astype(BF16)
    keys = side_by_side(normed, wk_ref[...])
    masks = [mask("1"), mask("2")]
    units = [([b], masks, bias_ref[...]) for b in range(bands)]
    context = attention(qv[0:128], keys, qv[128:256], units)
    out = finish(z, context, wo_ref[0], hg_ref[0:1, :], we_ref[0], ws_ref[0])
    fa_ref[...], fb = shifted_columns(out)
    fright_ref[...], fleft_ref[...] = edges(fb)
    na, nb = shifted_columns(layer_norm(out, ag_ref[1:2, :]))
    na_ref[...] = na.astype(BF16)
    right, left = edges(nb)
    right_ref[...] = right.astype(BF16)
    left_ref[...] = left.astype(BF16)


def start_kernel(out_ref):
    out_ref[...] = jnp.zeros(out_ref.shape, jnp.int32)


def edge_rows_kernel(x_ref, start_ref, ag_ref, pb_ref, hg_ref, last_ref, first_ref, sems):
    bottom = x_ref.shape[0] - WIN
    copies = [
        pltpu.make_async_copy(x_ref.at[pl.ds(bottom, WIN)], last_ref, sems.at[0]),
        pltpu.make_async_copy(x_ref.at[pl.ds(0, WIN)], first_ref, sems.at[1]),
    ]
    for copy in copies:
        copy.start()
    for copy in copies:
        copy.wait()


def first_kernel(*refs):
    own_block(*refs[0:8], *refs[10:])


def nothing_kernel(*refs):
    pass


def second_kernel(*refs):
    @pl.when(jnp.logical_not(goes_first()))
    def _():
        own_block(*refs[0:8], *refs[17:])


def halo_kernel(
    up_ref, down_ref, own_right_ref, own_left_ref, bias_ref, wqv_ref, wk_ref, wo_ref, we_ref, ws_ref, ag_ref, hg_ref,
    na_ref, cols_odd_ref, cols_even_ref,
):
    z = cat(windows_of(down_ref[...]) + windows_of(up_ref[...]))
    normed = layer_norm(z, ag_ref[0:1, :]).astype(BF16)
    keys = side_by_side(normed, wk_ref[...])
    values = dot(wqv_ref[128:256, :], normed, NT).astype(BF16)

    def wanted(t):
        return cat([t[0:32], t[160:192], t[64:96], t[224:256]])

    queries = dot(wqv_ref[0:128, :], wanted(normed), NT).astype(BF16)
    masks = [mask("1", "up"), mask("2", "up"), mask("1", "down"), mask("2", "down")]
    context = attention(queries, keys, values, [([0, 1], masks, bias_ref[...])])
    out = finish(wanted(z), context, wo_ref[0], hg_ref[0:1, :], we_ref[0], ws_ref[0])
    na, nb = shifted_columns(layer_norm(out, ag_ref[1:2, :]))
    na_ref[...] = na.astype(BF16)
    right, left = edges(nb)
    n = own_right_ref.shape[0]
    col_odd = lax.rem(lax.axis_index("gx"), 2) == 1
    for at, size, a, b in [(0, n, own_right_ref[...], own_left_ref[...]), (n, 32, right, left)]:
        a, b = a.astype(F32), b.astype(F32)
        cols_odd_ref[at : at + size, :] = jnp.where(col_odd, a, b).astype(BF16)
        cols_even_ref[at : at + size, :] = jnp.where(col_odd, b, a).astype(BF16)


def border_bias(pb_ref, block, tables):
    sub = iota((8, 128), 0)
    lane = iota((8, 128), 1)
    yi = (lane >> 2) & 7
    row, rows = lax.axis_index("gy"), lax.axis_size("gy")
    col, cols = lax.axis_index("gx"), lax.axis_size("gx")
    is_odd = lax.rem(col, 2) == 1
    last_row = (lane >= 96) & (jnp.where(yi < 4, rows - 1, 0) == row)
    for head in range(HEADS):
        low = jnp.broadcast_to(pb_ref[block, head : head + 1, 0:128], (8, 128))
        high = jnp.broadcast_to(pb_ref[block, head : head + 1, 97:225], (8, 128))
        for group in range(8):
            yj = 2 * (group % 4) + (sub >> 2)
            cut_row = last_row & ((yi < 4) != (yj < 4))
            plain = (7 + yi - yj) * 15 + 7 + (lane & 3) - (sub & 3)
            for number, (table, table_v) in enumerate(tables):
                if group < 4 and number == 1:
                    values = kept
                    cut = values
                else:
                    is_right = is_odd if number == 0 else jnp.logical_not(is_odd)
                    place = plain if group < 4 else plain + jnp.where(is_right, -4, 4)
                    values = LOG2E * jnp.where(
                        place < 128,
                        jnp.take_along_axis(low, lax.clamp(0, place, 127), axis=1),
                        jnp.take_along_axis(high, lax.clamp(0, place - 97, 127), axis=1),
                    )
                    if group >= 4:
                        outside = jnp.where(is_right, cols - 1, 0) == col
                        values = values - jnp.where(outside, 100.0 * LOG2E, 0.0)
                    kept = values
                at = (slice(group * 8, group * 8 + 8), slice(head * 128, head * 128 + 128))
                table[at] = values
                if group < 4:
                    cut = values - 100.0 * LOG2E
                else:
                    outside = jnp.where(is_right, cols - 1, 0) == col
                    cut = values - jnp.where(outside, 0.0, 100.0 * LOG2E)
                table_v[at] = jnp.where(cut_row, cut, values)


def middle_kernel(
    fa_ref, na_ref, va_ref, pb_ref, w_ref, wo_ref, we_ref, ws_ref, hg_ref,
    out_ref, bias_odd, bias_oddv, bias_even, bias_evenv, wqv_ref, wk_ref,
    bias_a, bias_av,
):
    sub = iota((8, 128), 0)
    lane = iota((8, 128), 1)
    query_up = (lane & 32) == 0
    row = lax.axis_index("gy")
    last_row = jnp.where(query_up, lax.axis_size("gy") - 1, 0) == row
    for head, yj, values in bias_rows(pb_ref, 1):
        at = (slice(yj * 8, yj * 8 + 8), slice(head * 128, head * 128 + 128))
        cut_row = (lane >= 64) & last_row & (jnp.logical_not(query_up) if yj < 4 else query_up)
        bias_a[at] = values
        bias_av[at] = jnp.where(cut_row, values - 100.0 * LOG2E, values)
    border_bias(pb_ref, 1, ((bias_odd, bias_oddv), (bias_even, bias_evenv)))
    fill_weights(w_ref[1], wqv_ref, wk_ref)
    n = na_ref.shape[0]
    inner = na_ref[32 : n - 32, :]
    first = cat([va_ref[32:64, :], na_ref[0:32, :]])
    last = cat([na_ref[n - 32 : n, :], va_ref[0:32, :]])
    looked_at = cat([inner, last, first, first])
    keys = side_by_side(looked_at, wk_ref[...])
    values = dot(wqv_ref[128:256, :], looked_at, NT).astype(BF16)
    wanted = cat([na_ref[32:n, :], na_ref[0:32, :]])
    queries = dot(wqv_ref[0:128, :], wanted, NT).astype(BF16)
    last_unit = n // 128 - 1
    masks = [mask("1"), mask("2")]
    units = [([u], masks, bias_a[...]) for u in range(last_unit)]
    masks = [mask("1"), mask("2", "up"), mask("2", "down"), jnp.zeros((64, 128), BF16)]
    units.append(([last_unit, last_unit + 1], masks, bias_av[...]))
    context = attention(queries, keys, values, units)
    z = cat([fa_ref[32:n, :], fa_ref[0:32, :]])
    out = finish(z, context, wo_ref[1], hg_ref[1:2, :], we_ref[1], ws_ref[1])
    out = half_turn(out).reshape(n, 128)
    out_ref[32:n, :] = out[0 : n - 32]
    out_ref[0:32, :] = out[n - 32 : n]


def beside_far_border():
    col, cols = lax.axis_index("gx"), lax.axis_size("gx")
    place = lax.rem(col, cols // 2)
    return (place == 0) | (place == cols // 2 - 1)


def middle_early_kernel(*refs):
    @pl.when(jnp.logical_not(beside_far_border()))
    def _():
        middle_kernel(*refs[0:9], *refs[11:])


def middle_late_kernel(*refs):
    @pl.when(beside_far_border())
    def _():
        middle_kernel(*refs[0:9], *refs[16:])


def border_block(z_ref, own_ref, other_ref, bias_ref, bias_v_ref, wqv_ref, wk_ref, wo_ref, we_ref, ws_ref, hg_ref):
    n = z_ref[0].shape[0]

    def in_order(ref):
        return cat([ref[n + 16 : n + 32, :], ref[0:n, :], ref[n : n + 16, :]])

    own, other = in_order(own_ref), in_order(other_ref)
    count = own.shape[0] // 32
    order = [*range(1, count), 0, 0]
    looked_at = cat([t[32 * w : 32 * w + 32] for w in order for t in (own, other)])
    keys = side_by_side(looked_at, wk_ref[...])
    values = dot(wqv_ref[128:256, :], looked_at, NT).astype(BF16)
    wanted = cat([own_ref[16:n, :], own_ref[0:16, :]])
    queries = dot(wqv_ref[0:128, :], wanted, NT).astype(BF16)
    lane = iota((64, 128), 1)

    def keep(condition):
        return jnp.where(condition, 1.0, 0.0).astype(BF16)

    masks = [keep((lane >> 5) == k) for k in range(4)]
    up = (lane & 16) == 0
    last = [keep((lane >= 96) & up), keep((lane >= 96) & jnp.logical_not(up)), keep(lane < 0)]
    units = [([2 * u, 2 * u + 1], masks, bias_ref[...]) for u in range(n // 128 - 1)]
    first = 2 * len(units)
    units.append(([first, first + 1, first + 2], masks[0:3] + last, bias_v_ref[...]))
    context = attention(queries, keys, values, units)
    is_odd = lax.rem(lax.axis_index("gx"), 2) == 1
    z = jnp.where(is_odd, z_ref[0][...], z_ref[1][...])
    z = cat([z[16:n], z[0:16]])
    out = finish(z, context, wo_ref[1], hg_ref[1:2, :], we_ref[1], ws_ref[1])
    return cat([out[n - 16 : n], out[0 : n - 16]])


def odd_border_kernel(fright_ref, fleft_ref, *refs):
    refs[-1][...] = border_block((fright_ref, fleft_ref), *refs[:-2])


def even_border_kernel(fright_ref, fleft_ref, *refs):
    inner_ref, odd_ref, out_ref = refs[-3:]
    even = border_block((fleft_ref, fright_ref), *refs[:-3])
    odd = odd_ref[...]
    is_odd = lax.rem(lax.axis_index("gx"), 2) == 1
    right = jnp.where(is_odd, odd, even).reshape(-1, 8, 128)
    left = jnp.where(is_odd, even, odd).reshape(-1, 8, 128)
    inner = inner_ref[...].reshape(-1, 8, 128)
    right = jnp.stack([pltpu.roll(right, 4, 1), right], axis=1).reshape(inner.shape)
    left = jnp.stack([left, pltpu.roll(left, 4, 1)], axis=1).reshape(inner.shape)
    low = low_half(inner.shape)
    out_ref[:, 0:8, :] = jnp.where(low, left, inner)
    out_ref[:, 8:16, :] = jnp.where(low, inner, right)


def vmem(count):
    return [pl.BlockSpec(memory_space=pltpu.VMEM)] * count


def call(kernel, name, operands, outs, scratch=(), flops=0, aliases=None):
    shapes = [jax.ShapeDtypeStruct(shape, dtype) for shape, dtype in outs]
    return pl.pallas_call(
        kernel,
        out_shape=shapes,
        in_specs=vmem(len(operands)),
        out_specs=vmem(len(outs)),
        scratch_shapes=list(scratch),
        input_output_aliases=aliases or {},
        compiler_params=pltpu.CompilerParams(vmem_limit_bytes=32 * 1024 * 1024),
        cost_estimate=pl.CostEstimate(flops=flops, bytes_accessed=1 << 20, transcendentals=0),
        name=name,
    )(*operands)


def on_device(x, ag, tw, ow, pb, hg, ew, sw):
    height, breadth = x.shape[0], x.shape[1]
    n = height * WIN
    table = ((64, HEADS * 128), F32)
    prepared = [((256, 128), BF16), ((256, 256), BF16)]
    weights = (x, tw, ow, ew, sw, ag, pb, hg)
    kept = [((n, C), F32)] + [((n // 2, C), F32)] * 2 + [((n, C), BF16)] + [((n // 2, C), BF16)] * 2
    kept += [table] + prepared
    rows = [((WIN, breadth, C), BF16)] * 2
    (start,) = call(start_kernel, "start", (), [((8, 128), jnp.int32)], (), 4 * 10**10)
    last, first = call(
        edge_rows_kernel, "edge_rows", (x, start, ag, pb, hg), rows, [pltpu.SemaphoreType.DMA((2,))]
    )

    def run(*operands):
        return call(first_kernel, "first", operands, rows[0:1] + kept, (), 4 * 10**9, {8: 0})

    def skip(*operands):
        return call(nothing_kernel, "nothing", operands[8:9], rows[0:1] + kept, (), 0, {0: 0})

    up = shift(last, "gy", 1)
    first, *state = lax.cond(goes_first(), run, skip, *weights, first)
    down = shift(first, "gy", -1)
    state = call(
        second_kernel, "second", (*weights, *state), kept, (), 4 * 10**9, {8 + i: i for i in range(9)}
    )
    fa, fright, fleft, na, right, left, bias, wqv, wk = state
    va, odd, even = call(
        halo_kernel, "halo", (up, down, right, left, bias, wqv, wk, ow, ew, sw, ag, hg),
        [((64, C), BF16)] + [((n // 2 + 32, C), BF16)] * 2, (), 10**9,
    )
    from_odd = swap(odd, "gx", 1)
    inputs = (fa, na, va, pb, tw, ow, ew, sw, hg)
    made = [((n, C), F32)] + [table] * 4 + prepared
    scratch = [pltpu.VMEM(*table)] * 2
    even, *state = call(
        middle_early_kernel, "middle_early", (*inputs, even), [(even.shape, BF16)] + made, scratch,
        2 * 10**9, {9: 0},
    )
    from_even = swap(even, "gx", 0)
    oa, *tables, wqv, wk = call(
        middle_late_kernel, "middle_late", (*inputs, *state), made, scratch, 2 * 10**9,
        {9 + i: i for i in range(7)},
    )
    rest = (wqv, wk, ow, ew, sw, hg)
    (ob,) = call(
        odd_border_kernel, "odd_border", (fright, fleft, odd, from_odd, *tables[0:2], *rest, even),
        [((n // 2, C), F32)], (), 10**9,
    )
    return call(
        even_border_kernel, "even_border", (fright, fleft, even, from_even, *tables[2:4], *rest, oa, ob),
        [((height, breadth, C), F32)], (), 10**9,
    )[0]


def solution(mesh):
    return jax.shard_map(
        on_device,
        mesh=mesh,
        in_specs=(P("gy", "gx", None), P(), P(), P(), P(), P(), P(), P()),
        out_specs=P("gy", "gx", None),
        check_vma=False,
    )
```

```python
import math

import jax
import jax.numpy as jnp
from jax import lax
from jax.experimental import pallas as pl
from jax.experimental.pallas import tpu as pltpu
from jax.sharding import PartitionSpec as P

C = 128
HEADS = 4
HID = 512
WIN = 8
HD = 32
EPSILON = 1e-05
LOG2E = math.log2(math.e)
SCALE = HD ** (-0.5) * LOG2E
F32 = jnp.float32
BF16 = jnp.bfloat16
NT = (((1,), (1,)), ((), ()))
TN = (((0,), (0,)), ((), ()))
CHUNK = 256


def shift(x, axis, by):
    length = lax.axis_size(axis)
    return lax.ppermute(x, axis, [(i, (i + by) % length) for i in range(length)])


def swap(x, axis, first):
    length = lax.axis_size(axis)
    there = [(i, (i + 1) % length) for i in range(first, length, 2)]
    return lax.ppermute(x, axis, there + [(b, a) for a, b in there])


def iota(shape, dim):
    return lax.broadcasted_iota(jnp.int32, shape, dim)


def dot(a, b, dims=None):
    if dims is None:
        return jnp.dot(a, b, preferred_element_type=F32)
    return lax.dot_general(a, b, dims, preferred_element_type=F32)


def cat(parts, axis=0):
    return jnp.concatenate(parts, axis=axis)


def layer_norm(x, gain):
    center = x - jnp.mean(x, axis=-1, keepdims=True)
    spread = jnp.sum(center * center, axis=-1, keepdims=True)
    return center * lax.rsqrt(spread + C * EPSILON) * (gain * C**0.5)


def twice_gelu(x):
    return x + x * lax.erf(x * (0.5**0.5))


def bias_rows(pb_ref, block):
    sub = iota((8, 128), 0)
    lane = iota((8, 128), 1)
    place = lax.min((lane >> 3) * 15 + 7 + (lane & 7) - sub, 224)
    for head in range(HEADS):
        low = jnp.broadcast_to(pb_ref[block, head : head + 1, 0:128], (8, 128))
        high = jnp.broadcast_to(pb_ref[block, head : head + 1, 97:225], (8, 128))
        strip = jnp.where(
            place < 128,
            jnp.take_along_axis(low, lax.min(place, 127), axis=1),
            jnp.take_along_axis(high, lax.max(place - 97, 0), axis=1),
        )
        strip = strip * LOG2E
        for yj in range(8):
            turn = (128 - (7 - yj) * 8) % 128
            first = pltpu.roll(strip, turn, 1) if turn else strip
            second = pltpu.roll(strip, (turn + 64) % 128, 1)
            yield head, yj, jnp.where(lane < 64, first, second)


def fill_weights(w, wqv, wk):
    wqv[0:128, :] = jnp.transpose(w[:, 0:128].astype(F32)).astype(BF16)
    wqv[128:256, :] = jnp.transpose(w[:, 256:384].astype(F32)).astype(BF16)
    keys = w[:, 128:256].astype(F32)
    turned = pltpu.roll(keys, 64, 1)
    lane = iota((128, 128), 1)
    zero = jnp.zeros((128, 128), F32)
    wk[0:128, 0:128] = jnp.where(lane < 64, keys, zero).astype(BF16)
    wk[0:128, 128:256] = jnp.where(lane < 64, turned, zero).astype(BF16)
    wk[128:256, 0:128] = jnp.where(lane >= 64, turned, zero).astype(BF16)
    wk[128:256, 128:256] = jnp.where(lane >= 64, keys, zero).astype(BF16)


def mask(*conditions):
    lane = iota((64, 128), 1)
    sides = {"1": lane < 64, "2": lane >= 64, "up": (lane & 32) == 0, "down": (lane & 32) > 0}
    sides |= {"left": (lane & 4) == 0, "right": (lane & 4) > 0}
    keep = sides[conditions[0]]
    for name in conditions[1:]:
        keep = keep & sides[name]
    return jnp.where(keep, 1.0, 0.0).astype(BF16)


def side_by_side(tokens, wk):
    pairs = tokens.reshape(-1, 2, 64, 128)
    lanes = cat([cat([pairs[p, 0], pairs[p, 1]], 1) for p in range(pairs.shape[0])])
    return dot(lanes, wk).astype(BF16)


def attention(queries, keys, values, units):
    zero = jnp.zeros((32, 128), BF16)
    scores = []
    for u, (pairs, masks, bias) in enumerate(units):
        q = queries[:, 128 * u : 128 * u + 128]
        for half in range(2):
            r = 64 * half
            rows = []
            for m in masks:
                rows.append(cat([q[r : r + 32] * m[0:32], zero], 1))
                rows.append(cat([zero, q[r + 32 : r + 64] * m[0:32]], 1))
            k = cat([keys[64 * p : 64 * p + 64, 128 * half : 128 * half + 128] for p in pairs], 1)
            scores.append(dot(k, cat(rows)))
    for u, (pairs, masks, bias) in enumerate(units):
        for half in range(2):
            s = scores[2 * u + half] * SCALE + bias[:, 256 * half : 256 * half + 256]
            p = jnp.exp2(s - jnp.max(s, axis=0, keepdims=True))
            part = 1.0 / jnp.sum(p, axis=0, keepdims=True)
            scores[2 * u + half] = (p * part).astype(BF16)
    context = []
    for u, (pairs, masks, bias) in enumerate(units):
        out = []
        for half in range(2):
            r = 64 * half
            p = scores[2 * u + half]
            seen = cat([cat([p[:, 0:128] * m, p[:, 128:256] * m], 1) for m in masks])
            v = cat([values[r : r + 64, 128 * j : 128 * j + 128] for j in pairs], 1)
            ct = dot(v, seen)
            out += [ct[0:32, 0:128], ct[32:64, 128:256]]
        context.append(cat(out).astype(BF16))
    return cat(context, 1)


def finish(z, context, wo, gain, we, ws):
    middle = z + dot(context, wo, TN).astype(BF16).astype(F32)
    normed = layer_norm(middle, gain).astype(BF16)
    size = min(CHUNK, z.shape[0])
    hidden = [dot(normed[i : i + size], we) for i in range(0, z.shape[0], size)]
    hidden = [twice_gelu(h).astype(BF16) for h in hidden]
    return middle + 0.5 * cat([dot(h, ws) for h in hidden])


def half_turn(x):
    return pltpu.roll(x.reshape(-1, 8, 128), 4, 1)


def low_half(shape):
    return iota(shape, 1) < 4


def windows_of(block):
    parts = block.astype(F32).reshape(8, 2, 8, 128)
    return [parts[:, 0].reshape(64, 128), parts[:, 1].reshape(64, 128)]


def shifted_columns(tokens):
    pairs = tokens.reshape(-1, 2, 64, 128)
    a, b = half_turn(pairs[:, 0]), half_turn(pairs[:, 1])
    low = low_half(a.shape)
    return jnp.where(low, a, b).reshape(-1, 128), jnp.where(low, b, a).reshape(-1, 128)


def edges(outer):
    pairs = outer.reshape(-1, 2, 8, 128)
    even, odd = pairs[:, 0], pairs[:, 1]
    low = low_half(even.shape)
    right = jnp.where(low, even, pltpu.roll(odd, 4, 1)).reshape(-1, 128)
    left = jnp.where(low, pltpu.roll(even, 4, 1), odd).reshape(-1, 128)
    return right, left


def goes_first():
    row, rows = lax.axis_index("gy"), lax.axis_size("gy")
    return lax.rem(row, rows // 2) < rows // 8


def own_block(
    x_ref, w_ref, wo_ref, we_ref, ws_ref, ag_ref, pb_ref, hg_ref,
    fa_ref, fright_ref, fleft_ref, na_ref, right_ref, left_ref, bias_ref, wqv_ref, wk_ref,
):
    for head, yj, values in bias_rows(pb_ref, 0):
        bias_ref[yj * 8 : yj * 8 + 8, head * 128 : head * 128 + 128] = values
    fill_weights(w_ref[0], wqv_ref, wk_ref)
    bands = x_ref.shape[0] // WIN
    z = cat([t for b in range(bands) for t in windows_of(x_ref[WIN * b : WIN * b + WIN])])
    normed = layer_norm(z, ag_ref[0:1, :]).astype(BF16)
    qv = dot(wqv_ref[...], normed, NT).astype(BF16)
    keys = side_by_side(normed, wk_ref[...])
    masks = [mask("1"), mask("2")]
    units = [([b], masks, bias_ref[...]) for b in range(bands)]
    context = attention(qv[0:128], keys, qv[128:256], units)
    out = finish(z, context, wo_ref[0], hg_ref[0:1, :], we_ref[0], ws_ref[0])
    fa_ref[...], fb = shifted_columns(out)
    fright_ref[...], fleft_ref[...] = edges(fb)
    na, nb = shifted_columns(layer_norm(out, ag_ref[1:2, :]))
    na_ref[...] = na.astype(BF16)
    right, left = edges(nb)
    right_ref[...] = right.astype(BF16)
    left_ref[...] = left.astype(BF16)


def start_kernel(out_ref):
    out_ref[...] = jnp.zeros(out_ref.shape, jnp.int32)


def edge_rows_kernel(x_ref, start_ref, ag_ref, pb_ref, hg_ref, last_ref, first_ref, sems):
    bottom = x_ref.shape[0] - WIN
    copies = [
        pltpu.make_async_copy(x_ref.at[pl.ds(bottom, WIN)], last_ref, sems.at[0]),
        pltpu.make_async_copy(x_ref.at[pl.ds(0, WIN)], first_ref, sems.at[1]),
    ]
    for copy in copies:
        copy.start()
    for copy in copies:
        copy.wait()


def first_kernel(*refs):
    own_block(*refs[0:8], *refs[10:])


def nothing_kernel(*refs):
    pass


def second_kernel(*refs):
    @pl.when(jnp.logical_not(goes_first()))
    def _():
        own_block(*refs[0:8], *refs[18:])


def halo_kernel(
    up_ref, down_ref, own_right_ref, own_left_ref, bias_ref, wqv_ref, wk_ref, wo_ref, we_ref, ws_ref, ag_ref, hg_ref,
    na_ref, cols_odd_ref, cols_even_ref,
):
    z = cat(windows_of(down_ref[...]) + windows_of(up_ref[...]))
    normed = layer_norm(z, ag_ref[0:1, :]).astype(BF16)
    keys = side_by_side(normed, wk_ref[...])
    values = dot(wqv_ref[128:256, :], normed, NT).astype(BF16)

    def wanted(t):
        return cat([t[0:32], t[160:192], t[64:96], t[224:256]])

    queries = dot(wqv_ref[0:128, :], wanted(normed), NT).astype(BF16)
    masks = [mask("1", "up"), mask("2", "up"), mask("1", "down"), mask("2", "down")]
    context = attention(queries, keys, values, [([0, 1], masks, bias_ref[...])])
    out = finish(wanted(z), context, wo_ref[0], hg_ref[0:1, :], we_ref[0], ws_ref[0])
    na, nb = shifted_columns(layer_norm(out, ag_ref[1:2, :]))
    na_ref[...] = na.astype(BF16)
    right, left = edges(nb)
    n = own_right_ref.shape[0]
    col_odd = lax.rem(lax.axis_index("gx"), 2) == 1
    for at, size, a, b in [(0, n, own_right_ref[...], own_left_ref[...]), (n, 32, right, left)]:
        a, b = a.astype(F32), b.astype(F32)
        cols_odd_ref[at : at + size, :] = jnp.where(col_odd, a, b).astype(BF16)
        cols_even_ref[at : at + size, :] = jnp.where(col_odd, b, a).astype(BF16)


def border_bias(pb_ref, block, tables):
    sub = iota((8, 128), 0)
    lane = iota((8, 128), 1)
    yi = (lane >> 2) & 7
    row, rows = lax.axis_index("gy"), lax.axis_size("gy")
    col, cols = lax.axis_index("gx"), lax.axis_size("gx")
    is_odd = lax.rem(col, 2) == 1
    last_row = (lane >= 96) & (jnp.where(yi < 4, rows - 1, 0) == row)
    for head in range(HEADS):
        low = jnp.broadcast_to(pb_ref[block, head : head + 1, 0:128], (8, 128))
        high = jnp.broadcast_to(pb_ref[block, head : head + 1, 97:225], (8, 128))
        for group in range(8):
            yj = 2 * (group % 4) + (sub >> 2)
            cut_row = last_row & ((yi < 4) != (yj < 4))
            plain = (7 + yi - yj) * 15 + 7 + (lane & 3) - (sub & 3)
            for number, (table, table_v) in enumerate(tables):
                if group < 4 and number == 1:
                    values = kept
                    cut = values
                else:
                    is_right = is_odd if number == 0 else jnp.logical_not(is_odd)
                    place = plain if group < 4 else plain + jnp.where(is_right, -4, 4)
                    values = LOG2E * jnp.where(
                        place < 128,
                        jnp.take_along_axis(low, lax.clamp(0, place, 127), axis=1),
                        jnp.take_along_axis(high, lax.clamp(0, place - 97, 127), axis=1),
                    )
                    if group >= 4:
                        outside = jnp.where(is_right, cols - 1, 0) == col
                        values = values - jnp.where(outside, 100.0 * LOG2E, 0.0)
                    kept = values
                at = (slice(group * 8, group * 8 + 8), slice(head * 128, head * 128 + 128))
                table[at] = values
                if group < 4:
                    cut = values - 100.0 * LOG2E
                else:
                    outside = jnp.where(is_right, cols - 1, 0) == col
                    cut = values - jnp.where(outside, 0.0, 100.0 * LOG2E)
                table_v[at] = jnp.where(cut_row, cut, values)


def middle_kernel(
    fa_ref, na_ref, va_ref, pb_ref, w_ref, wo_ref, we_ref, ws_ref, hg_ref,
    out_ref, bias_odd, bias_oddv, bias_even, bias_evenv, wqv_ref, wk_ref,
    bias_a, bias_av,
):
    sub = iota((8, 128), 0)
    lane = iota((8, 128), 1)
    query_up = (lane & 32) == 0
    row = lax.axis_index("gy")
    last_row = jnp.where(query_up, lax.axis_size("gy") - 1, 0) == row
    for head, yj, values in bias_rows(pb_ref, 1):
        at = (slice(yj * 8, yj * 8 + 8), slice(head * 128, head * 128 + 128))
        cut_row = (lane >= 64) & last_row & (jnp.logical_not(query_up) if yj < 4 else query_up)
        bias_a[at] = values
        bias_av[at] = jnp.where(cut_row, values - 100.0 * LOG2E, values)
    border_bias(pb_ref, 1, ((bias_odd, bias_oddv), (bias_even, bias_evenv)))
    fill_weights(w_ref[1], wqv_ref, wk_ref)
    n = na_ref.shape[0]
    inner = na_ref[32 : n - 32, :]
    first = cat([va_ref[32:64, :], na_ref[0:32, :]])
    last = cat([na_ref[n - 32 : n, :], va_ref[0:32, :]])
    looked_at = cat([inner, last, first, first])
    keys = side_by_side(looked_at, wk_ref[...])
    values = dot(wqv_ref[128:256, :], looked_at, NT).astype(BF16)
    wanted = cat([na_ref[32:n, :], na_ref[0:32, :]])
    queries = dot(wqv_ref[0:128, :], wanted, NT).astype(BF16)
    last_unit = n // 128 - 1
    masks = [mask("1"), mask("2")]
    units = [([u], masks, bias_a[...]) for u in range(last_unit)]
    masks = [mask("1"), mask("2", "up"), mask("2", "down"), jnp.zeros((64, 128), BF16)]
    units.append(([last_unit, last_unit + 1], masks, bias_av[...]))
    context = attention(queries, keys, values, units)
    z = cat([fa_ref[32:n, :], fa_ref[0:32, :]])
    out = finish(z, context, wo_ref[1], hg_ref[1:2, :], we_ref[1], ws_ref[1])
    out = half_turn(out).reshape(n, 128)
    out_ref[32:n, :] = out[0 : n - 32]
    out_ref[0:32, :] = out[n - 32 : n]


def beside_far_border():
    col, cols = lax.axis_index("gx"), lax.axis_size("gx")
    place = lax.rem(col, cols // 2)
    return (place == 0) | (place == cols // 2 - 1)


def middle_early_kernel(*refs):
    @pl.when(jnp.logical_not(beside_far_border()))
    def _():
        middle_kernel(*refs[0:9], *refs[11:])


def middle_late_kernel(*refs):
    @pl.when(beside_far_border())
    def _():
        middle_kernel(*refs[0:9], *refs[16:])


def border_block(z_ref, own_ref, other_ref, bias_ref, bias_v_ref, wqv_ref, wk_ref, wo_ref, we_ref, ws_ref, hg_ref):
    n = z_ref[0].shape[0]

    def in_order(ref):
        return cat([ref[n + 16 : n + 32, :], ref[0:n, :], ref[n : n + 16, :]])

    own, other = in_order(own_ref), in_order(other_ref)
    count = own.shape[0] // 32
    order = [*range(1, count), 0, 0]
    looked_at = cat([t[32 * w : 32 * w + 32] for w in order for t in (own, other)])
    keys = side_by_side(looked_at, wk_ref[...])
    values = dot(wqv_ref[128:256, :], looked_at, NT).astype(BF16)
    wanted = cat([own_ref[16:n, :], own_ref[0:16, :]])
    queries = dot(wqv_ref[0:128, :], wanted, NT).astype(BF16)
    lane = iota((64, 128), 1)

    def keep(condition):
        return jnp.where(condition, 1.0, 0.0).astype(BF16)

    masks = [keep((lane >> 5) == k) for k in range(4)]
    up = (lane & 16) == 0
    last = [keep((lane >= 96) & up), keep((lane >= 96) & jnp.logical_not(up)), keep(lane < 0)]
    units = [([2 * u, 2 * u + 1], masks, bias_ref[...]) for u in range(n // 128 - 1)]
    first = 2 * len(units)
    units.append(([first, first + 1, first + 2], masks[0:3] + last, bias_v_ref[...]))
    context = attention(queries, keys, values, units)
    is_odd = lax.rem(lax.axis_index("gx"), 2) == 1
    z = jnp.where(is_odd, z_ref[0][...], z_ref[1][...])
    z = cat([z[16:n], z[0:16]])
    out = finish(z, context, wo_ref[1], hg_ref[1:2, :], we_ref[1], ws_ref[1])
    return cat([out[n - 16 : n], out[0 : n - 16]])


def odd_border_kernel(fright_ref, fleft_ref, *refs):
    refs[-1][...] = border_block((fright_ref, fleft_ref), *refs[:-2])


def even_border_kernel(fright_ref, fleft_ref, *refs):
    inner_ref, odd_ref, out_ref = refs[-3:]
    even = border_block((fleft_ref, fright_ref), *refs[:-3])
    odd = odd_ref[...]
    is_odd = lax.rem(lax.axis_index("gx"), 2) == 1
    right = jnp.where(is_odd, odd, even).reshape(-1, 8, 128)
    left = jnp.where(is_odd, even, odd).reshape(-1, 8, 128)
    inner = inner_ref[...].reshape(-1, 8, 128)
    right = jnp.stack([pltpu.roll(right, 4, 1), right], axis=1).reshape(inner.shape)
    left = jnp.stack([left, pltpu.roll(left, 4, 1)], axis=1).reshape(inner.shape)
    low = low_half(inner.shape)
    out_ref[:, 0:8, :] = jnp.where(low, left, inner)
    out_ref[:, 8:16, :] = jnp.where(low, inner, right)


def vmem(count):
    return [pl.BlockSpec(memory_space=pltpu.VMEM)] * count


def call(kernel, name, operands, outs, scratch=(), flops=0, aliases=None):
    shapes = [jax.ShapeDtypeStruct(shape, dtype) for shape, dtype in outs]
    return pl.pallas_call(
        kernel,
        out_shape=shapes,
        in_specs=vmem(len(operands)),
        out_specs=vmem(len(outs)),
        scratch_shapes=list(scratch),
        input_output_aliases=aliases or {},
        compiler_params=pltpu.CompilerParams(vmem_limit_bytes=32 * 1024 * 1024),
        cost_estimate=pl.CostEstimate(flops=flops, bytes_accessed=1 << 20, transcendentals=0),
        name=name,
    )(*operands)


def on_device(x, ag, tw, ow, pb, hg, ew, sw):
    height, breadth = x.shape[0], x.shape[1]
    n = height * WIN
    table = ((64, HEADS * 128), F32)
    prepared = [((256, 128), BF16), ((256, 256), BF16)]
    weights = (x, tw, ow, ew, sw, ag, pb, hg)
    kept = [((n, C), F32)] + [((n // 2, C), F32)] * 2 + [((n, C), BF16)] + [((n // 2, C), BF16)] * 2
    kept += [table] + prepared
    rows = [((WIN, breadth, C), BF16)] * 2
    (start,) = call(start_kernel, "start", (), [((8, 128), jnp.int32)], (), 4 * 10**10)
    last, first = call(
        edge_rows_kernel, "edge_rows", (x, start, ag, pb, hg), rows, [pltpu.SemaphoreType.DMA((2,))]
    )

    def run(*operands):
        return call(first_kernel, "first", operands, rows[0:1] + kept, (), 4 * 10**9, {8: 0})

    def skip(*operands):
        return call(nothing_kernel, "nothing", operands[8:9], rows[0:1] + kept, (), 0, {0: 0})

    up = shift(last, "gy", 1)
    first, *state = lax.cond(goes_first(), run, skip, *weights, first)
    down = shift(first, "gy", -1)
    state = call(
        second_kernel, "second", (*weights, *state, up), kept, (), 4 * 10**9, {8 + i: i for i in range(9)}
    )
    fa, fright, fleft, na, right, left, bias, wqv, wk = state
    va, odd, even = call(
        halo_kernel, "halo", (up, down, right, left, bias, wqv, wk, ow, ew, sw, ag, hg),
        [((64, C), BF16)] + [((n // 2 + 32, C), BF16)] * 2, (), 10**9,
    )
    from_odd = swap(odd, "gx", 1)
    inputs = (fa, na, va, pb, tw, ow, ew, sw, hg)
    made = [((n, C), F32)] + [table] * 4 + prepared
    scratch = [pltpu.VMEM(*table)] * 2
    even, *state = call(
        middle_early_kernel, "middle_early", (*inputs, even), [(even.shape, BF16)] + made, scratch,
        2 * 10**9, {9: 0},
    )
    from_even = swap(even, "gx", 0)
    oa, *tables, wqv, wk = call(
        middle_late_kernel, "middle_late", (*inputs, *state), made, scratch, 2 * 10**9,
        {9 + i: i for i in range(7)},
    )
    rest = (wqv, wk, ow, ew, sw, hg)
    (ob,) = call(
        odd_border_kernel, "odd_border", (fright, fleft, odd, from_odd, *tables[0:2], *rest, even),
        [((n // 2, C), F32)], (), 10**9,
    )
    return call(
        even_border_kernel, "even_border", (fright, fleft, even, from_even, *tables[2:4], *rest, oa, ob),
        [((height, breadth, C), F32)], (), 10**9,
    )[0]


def solution(mesh):
    return jax.shard_map(
        on_device,
        mesh=mesh,
        in_specs=(P("gy", "gx", None), P(), P(), P(), P(), P(), P(), P()),
        out_specs=P("gy", "gx", None),
        check_vma=False,
    )
```

```python
import math

import jax
import jax.numpy as jnp
from jax import lax
from jax.experimental import pallas as pl
from jax.experimental.pallas import tpu as pltpu
from jax.sharding import PartitionSpec as P

C = 128
HEADS = 4
HID = 512
WIN = 8
HD = 32
EPSILON = 1e-05
LOG2E = math.log2(math.e)
SCALE = HD ** (-0.5) * LOG2E
F32 = jnp.float32
BF16 = jnp.bfloat16
NT = (((1,), (1,)), ((), ()))
TN = (((0,), (0,)), ((), ()))
CHUNK = 256


def shift(x, axis, by):
    length = lax.axis_size(axis)
    return lax.ppermute(x, axis, [(i, (i + by) % length) for i in range(length)])


def swap(x, axis, first):
    length = lax.axis_size(axis)
    there = [(i, (i + 1) % length) for i in range(first, length, 2)]
    return lax.ppermute(x, axis, there + [(b, a) for a, b in there])


def iota(shape, dim):
    return lax.broadcasted_iota(jnp.int32, shape, dim)


def dot(a, b, dims=None):
    if dims is None:
        return jnp.dot(a, b, preferred_element_type=F32)
    return lax.dot_general(a, b, dims, preferred_element_type=F32)


def cat(parts, axis=0):
    return jnp.concatenate(parts, axis=axis)


def layer_norm(x, gain):
    center = x - jnp.mean(x, axis=-1, keepdims=True)
    spread = jnp.sum(center * center, axis=-1, keepdims=True)
    return center * lax.rsqrt(spread + C * EPSILON) * (gain * C**0.5)


def twice_gelu(x):
    return x + x * lax.erf(x * (0.5**0.5))


def bias_rows(pb_ref, block):
    sub = iota((8, 128), 0)
    lane = iota((8, 128), 1)
    place = lax.min((lane >> 3) * 15 + 7 + (lane & 7) - sub, 224)
    for head in range(HEADS):
        low = jnp.broadcast_to(pb_ref[block, head : head + 1, 0:128], (8, 128))
        high = jnp.broadcast_to(pb_ref[block, head : head + 1, 97:225], (8, 128))
        strip = jnp.where(
            place < 128,
            jnp.take_along_axis(low, lax.min(place, 127), axis=1),
            jnp.take_along_axis(high, lax.max(place - 97, 0), axis=1),
        )
        strip = strip * LOG2E
        for yj in range(8):
            turn = (128 - (7 - yj) * 8) % 128
            first = pltpu.roll(strip, turn, 1) if turn else strip
            second = pltpu.roll(strip, (turn + 64) % 128, 1)
            yield head, yj, jnp.where(lane < 64, first, second)


def fill_weights(w, wqv, wk):
    wqv[0:128, :] = jnp.transpose(w[:, 0:128].astype(F32)).astype(BF16)
    wqv[128:256, :] = jnp.transpose(w[:, 256:384].astype(F32)).astype(BF16)
    keys = w[:, 128:256].astype(F32)
    turned = pltpu.roll(keys, 64, 1)
    lane = iota((128, 128), 1)
    zero = jnp.zeros((128, 128), F32)
    wk[0:128, 0:128] = jnp.where(lane < 64, keys, zero).astype(BF16)
    wk[0:128, 128:256] = jnp.where(lane < 64, turned, zero).astype(BF16)
    wk[128:256, 0:128] = jnp.where(lane >= 64, turned, zero).astype(BF16)
    wk[128:256, 128:256] = jnp.where(lane >= 64, keys, zero).astype(BF16)


def mask(*conditions):
    lane = iota((64, 128), 1)
    sides = {"1": lane < 64, "2": lane >= 64, "up": (lane & 32) == 0, "down": (lane & 32) > 0}
    sides |= {"left": (lane & 4) == 0, "right": (lane & 4) > 0}
    keep = sides[conditions[0]]
    for name in conditions[1:]:
        keep = keep & sides[name]
    return jnp.where(keep, 1.0, 0.0).astype(BF16)


def side_by_side(tokens, wk):
    pairs = tokens.reshape(-1, 2, 64, 128)
    lanes = cat([cat([pairs[p, 0], pairs[p, 1]], 1) for p in range(pairs.shape[0])])
    return dot(lanes, wk).astype(BF16)


def attention(queries, keys, values, units):
    zero = jnp.zeros((32, 128), BF16)
    scores = []
    for u, (pairs, masks, bias) in enumerate(units):
        q = queries[:, 128 * u : 128 * u + 128]
        for half in range(2):
            r = 64 * half
            rows = []
            for m in masks:
                rows.append(cat([q[r : r + 32] * m[0:32], zero], 1))
                rows.append(cat([zero, q[r + 32 : r + 64] * m[0:32]], 1))
            k = cat([keys[64 * p : 64 * p + 64, 128 * half : 128 * half + 128] for p in pairs], 1)
            scores.append(dot(k, cat(rows)))
    for u, (pairs, masks, bias) in enumerate(units):
        for half in range(2):
            s = scores[2 * u + half] * SCALE + bias[:, 256 * half : 256 * half + 256]
            p = jnp.exp2(s - jnp.max(s, axis=0, keepdims=True))
            part = 1.0 / jnp.sum(p, axis=0, keepdims=True)
            scores[2 * u + half] = (p * part).astype(BF16)
    context = []
    for u, (pairs, masks, bias) in enumerate(units):
        out = []
        for half in range(2):
            r = 64 * half
            p = scores[2 * u + half]
            seen = cat([cat([p[:, 0:128] * m, p[:, 128:256] * m], 1) for m in masks])
            v = cat([values[r : r + 64, 128 * j : 128 * j + 128] for j in pairs], 1)
            ct = dot(v, seen)
            out += [ct[0:32, 0:128], ct[32:64, 128:256]]
        context.append(cat(out).astype(BF16))
    return cat(context, 1)


def finish(z, context, wo, gain, we, ws):
    middle = z + dot(context, wo, TN).astype(BF16).astype(F32)
    normed = layer_norm(middle, gain).astype(BF16)
    size = min(CHUNK, z.shape[0])
    hidden = [dot(normed[i : i + size], we) for i in range(0, z.shape[0], size)]
    hidden = [twice_gelu(h).astype(BF16) for h in hidden]
    return middle + 0.5 * cat([dot(h, ws) for h in hidden])


def half_turn(x):
    return pltpu.roll(x.reshape(-1, 8, 128), 4, 1)


def low_half(shape):
    return iota(shape, 1) < 4


def windows_of(block):
    parts = block.astype(F32).reshape(8, 2, 8, 128)
    return [parts[:, 0].reshape(64, 128), parts[:, 1].reshape(64, 128)]


def shifted_columns(tokens):
    pairs = tokens.reshape(-1, 2, 64, 128)
    a, b = half_turn(pairs[:, 0]), half_turn(pairs[:, 1])
    low = low_half(a.shape)
    return jnp.where(low, a, b).reshape(-1, 128), jnp.where(low, b, a).reshape(-1, 128)


def edges(outer):
    pairs = outer.reshape(-1, 2, 8, 128)
    even, odd = pairs[:, 0], pairs[:, 1]
    low = low_half(even.shape)
    right = jnp.where(low, even, pltpu.roll(odd, 4, 1)).reshape(-1, 128)
    left = jnp.where(low, pltpu.roll(even, 4, 1), odd).reshape(-1, 128)
    return right, left


def goes_first():
    row, rows = lax.axis_index("gy"), lax.axis_size("gy")
    return lax.rem(row, rows // 2) < rows // 8


def own_block(
    x_ref, w_ref, wo_ref, we_ref, ws_ref, ag_ref, pb_ref, hg_ref,
    fa_ref, fright_ref, fleft_ref, na_ref, right_ref, left_ref, bias_ref, wqv_ref, wk_ref,
):
    for head, yj, values in bias_rows(pb_ref, 0):
        bias_ref[yj * 8 : yj * 8 + 8, head * 128 : head * 128 + 128] = values
    fill_weights(w_ref[0], wqv_ref, wk_ref)
    bands = x_ref.shape[0] // WIN
    z = cat([t for b in range(bands) for t in windows_of(x_ref[WIN * b : WIN * b + WIN])])
    normed = layer_norm(z, ag_ref[0:1, :]).astype(BF16)
    qv = dot(wqv_ref[...], normed, NT).astype(BF16)
    keys = side_by_side(normed, wk_ref[...])
    masks = [mask("1"), mask("2")]
    units = [([b], masks, bias_ref[...]) for b in range(bands)]
    context = attention(qv[0:128], keys, qv[128:256], units)
    out = finish(z, context, wo_ref[0], hg_ref[0:1, :], we_ref[0], ws_ref[0])
    fa_ref[...], fb = shifted_columns(out)
    fright_ref[...], fleft_ref[...] = edges(fb)
    na, nb = shifted_columns(layer_norm(out, ag_ref[1:2, :]))
    na_ref[...] = na.astype(BF16)
    right, left = edges(nb)
    right_ref[...] = right.astype(BF16)
    left_ref[...] = left.astype(BF16)


def start_kernel(out_ref):
    out_ref[...] = jnp.zeros(out_ref.shape, jnp.int32)


def edge_rows_kernel(x_ref, start_ref, ag_ref, pb_ref, hg_ref, last_ref, first_ref, sems):
    bottom = x_ref.shape[0] - WIN
    copies = [
        pltpu.make_async_copy(x_ref.at[pl.ds(bottom, WIN)], last_ref, sems.at[0]),
        pltpu.make_async_copy(x_ref.at[pl.ds(0, WIN)], first_ref, sems.at[1]),
    ]
    for copy in copies:
        copy.start()
    for copy in copies:
        copy.wait()


def first_kernel(*refs):
    own_block(*refs[0:8], *refs[10:])


def nothing_kernel(*refs):
    pass


def second_kernel(*refs):
    @pl.when(jnp.logical_not(goes_first()))
    def _():
        own_block(*refs[0:8], *refs[18:])


def halo_kernel(
    up_ref, down_ref, own_right_ref, own_left_ref, bias_ref, wqv_ref, wk_ref, wo_ref, we_ref, ws_ref, ag_ref, hg_ref,
    na_ref, cols_odd_ref, cols_even_ref,
):
    z = cat(windows_of(down_ref[...]) + windows_of(up_ref[...]))
    normed = layer_norm(z, ag_ref[0:1, :]).astype(BF16)
    keys = side_by_side(normed, wk_ref[...])
    values = dot(wqv_ref[128:256, :], normed, NT).astype(BF16)

    def wanted(t):
        return cat([t[0:32], t[160:192], t[64:96], t[224:256]])

    queries = dot(wqv_ref[0:128, :], wanted(normed), NT).astype(BF16)
    masks = [mask("1", "up"), mask("2", "up"), mask("1", "down"), mask("2", "down")]
    context = attention(queries, keys, values, [([0, 1], masks, bias_ref[...])])
    out = finish(wanted(z), context, wo_ref[0], hg_ref[0:1, :], we_ref[0], ws_ref[0])
    na, nb = shifted_columns(layer_norm(out, ag_ref[1:2, :]))
    na_ref[...] = na.astype(BF16)
    right, left = edges(nb)
    n = own_right_ref.shape[0]
    col_odd = lax.rem(lax.axis_index("gx"), 2) == 1
    for at, size, a, b in [(0, n, own_right_ref[...], own_left_ref[...]), (n, 32, right, left)]:
        a, b = a.astype(F32), b.astype(F32)
        cols_odd_ref[at : at + size, :] = jnp.where(col_odd, a, b).astype(BF16)
        cols_even_ref[at : at + size, :] = jnp.where(col_odd, b, a).astype(BF16)


def border_bias(pb_ref, block, tables):
    sub = iota((8, 128), 0)
    lane = iota((8, 128), 1)
    yi = (lane >> 2) & 7
    row, rows = lax.axis_index("gy"), lax.axis_size("gy")
    col, cols = lax.axis_index("gx"), lax.axis_size("gx")
    is_odd = lax.rem(col, 2) == 1
    last_row = (lane >= 96) & (jnp.where(yi < 4, rows - 1, 0) == row)
    for head in range(HEADS):
        low = jnp.broadcast_to(pb_ref[block, head : head + 1, 0:128], (8, 128))
        high = jnp.broadcast_to(pb_ref[block, head : head + 1, 97:225], (8, 128))
        for group in range(8):
            yj = 2 * (group % 4) + (sub >> 2)
            cut_row = last_row & ((yi < 4) != (yj < 4))
            plain = (7 + yi - yj) * 15 + 7 + (lane & 3) - (sub & 3)
            for number, (table, table_v) in enumerate(tables):
                if group < 4 and number == 1:
                    values = kept
                    cut = values
                else:
                    is_right = is_odd if number == 0 else jnp.logical_not(is_odd)
                    place = plain if group < 4 else plain + jnp.where(is_right, -4, 4)
                    values = LOG2E * jnp.where(
                        place < 128,
                        jnp.take_along_axis(low, lax.clamp(0, place, 127), axis=1),
                        jnp.take_along_axis(high, lax.clamp(0, place - 97, 127), axis=1),
                    )
                    if group >= 4:
                        outside = jnp.where(is_right, cols - 1, 0) == col
                        values = values - jnp.where(outside, 100.0 * LOG2E, 0.0)
                    kept = values
                at = (slice(group * 8, group * 8 + 8), slice(head * 128, head * 128 + 128))
                table[at] = values
                if group < 4:
                    cut = values - 100.0 * LOG2E
                else:
                    outside = jnp.where(is_right, cols - 1, 0) == col
                    cut = values - jnp.where(outside, 0.0, 100.0 * LOG2E)
                table_v[at] = jnp.where(cut_row, cut, values)


def middle_kernel(
    fa_ref, na_ref, va_ref, pb_ref, w_ref, wo_ref, we_ref, ws_ref, hg_ref,
    out_ref, bias_odd, bias_oddv, bias_even, bias_evenv, wqv_ref, wk_ref,
    bias_a, bias_av,
):
    sub = iota((8, 128), 0)
    lane = iota((8, 128), 1)
    query_up = (lane & 32) == 0
    row = lax.axis_index("gy")
    last_row = jnp.where(query_up, lax.axis_size("gy") - 1, 0) == row
    for head, yj, values in bias_rows(pb_ref, 1):
        at = (slice(yj * 8, yj * 8 + 8), slice(head * 128, head * 128 + 128))
        cut_row = (lane >= 64) & last_row & (jnp.logical_not(query_up) if yj < 4 else query_up)
        bias_a[at] = values
        bias_av[at] = jnp.where(cut_row, values - 100.0 * LOG2E, values)
    border_bias(pb_ref, 1, ((bias_odd, bias_oddv), (bias_even, bias_evenv)))
    fill_weights(w_ref[1], wqv_ref, wk_ref)
    n = na_ref.shape[0]
    inner = na_ref[32 : n - 32, :]
    first = cat([va_ref[32:64, :], na_ref[0:32, :]])
    last = cat([na_ref[n - 32 : n, :], va_ref[0:32, :]])
    looked_at = cat([inner, last, first, first])
    keys = side_by_side(looked_at, wk_ref[...])
    values = dot(wqv_ref[128:256, :], looked_at, NT).astype(BF16)
    wanted = cat([na_ref[32:n, :], na_ref[0:32, :]])
    queries = dot(wqv_ref[0:128, :], wanted, NT).astype(BF16)
    last_unit = n // 128 - 1
    masks = [mask("1"), mask("2")]
    units = [([u], masks, bias_a[...]) for u in range(last_unit)]
    masks = [mask("1"), mask("2", "up"), mask("2", "down"), jnp.zeros((64, 128), BF16)]
    units.append(([last_unit, last_unit + 1], masks, bias_av[...]))
    context = attention(queries, keys, values, units)
    z = cat([fa_ref[32:n, :], fa_ref[0:32, :]])
    out = finish(z, context, wo_ref[1], hg_ref[1:2, :], we_ref[1], ws_ref[1])
    out = half_turn(out).reshape(n, 128)
    out_ref[32:n, :] = out[0 : n - 32]
    out_ref[0:32, :] = out[n - 32 : n]


def waits_in_even_swap():
    col, cols = lax.axis_index("gx"), lax.axis_size("gx")
    place = lax.rem(col, cols // 2)
    return (place == 1) | (place == cols // 2 - 2)


def middle_early_kernel(*refs):
    @pl.when(waits_in_even_swap())
    def _():
        middle_kernel(*refs[0:9], *refs[11:])


def middle_late_kernel(*refs):
    @pl.when(jnp.logical_not(waits_in_even_swap()))
    def _():
        middle_kernel(*refs[0:9], *refs[16:])


def border_block(z_ref, own_ref, other_ref, bias_ref, bias_v_ref, wqv_ref, wk_ref, wo_ref, we_ref, ws_ref, hg_ref):
    n = z_ref[0].shape[0]

    def in_order(ref):
        return cat([ref[n + 16 : n + 32, :], ref[0:n, :], ref[n : n + 16, :]])

    own, other = in_order(own_ref), in_order(other_ref)
    count = own.shape[0] // 32
    order = [*range(1, count), 0, 0]
    looked_at = cat([t[32 * w : 32 * w + 32] for w in order for t in (own, other)])
    keys = side_by_side(looked_at, wk_ref[...])
    values = dot(wqv_ref[128:256, :], looked_at, NT).astype(BF16)
    wanted = cat([own_ref[16:n, :], own_ref[0:16, :]])
    queries = dot(wqv_ref[0:128, :], wanted, NT).astype(BF16)
    lane = iota((64, 128), 1)

    def keep(condition):
        return jnp.where(condition, 1.0, 0.0).astype(BF16)

    masks = [keep((lane >> 5) == k) for k in range(4)]
    up = (lane & 16) == 0
    last = [keep((lane >= 96) & up), keep((lane >= 96) & jnp.logical_not(up)), keep(lane < 0)]
    units = [([2 * u, 2 * u + 1], masks, bias_ref[...]) for u in range(n // 128 - 1)]
    first = 2 * len(units)
    units.append(([first, first + 1, first + 2], masks[0:3] + last, bias_v_ref[...]))
    context = attention(queries, keys, values, units)
    is_odd = lax.rem(lax.axis_index("gx"), 2) == 1
    z = jnp.where(is_odd, z_ref[0][...], z_ref[1][...])
    z = cat([z[16:n], z[0:16]])
    out = finish(z, context, wo_ref[1], hg_ref[1:2, :], we_ref[1], ws_ref[1])
    return cat([out[n - 16 : n], out[0 : n - 16]])


def odd_border_kernel(fright_ref, fleft_ref, *refs):
    refs[-1][...] = border_block((fright_ref, fleft_ref), *refs[:-2])


def even_border_kernel(fright_ref, fleft_ref, *refs):
    inner_ref, odd_ref, out_ref = refs[-3:]
    even = border_block((fleft_ref, fright_ref), *refs[:-3])
    odd = odd_ref[...]
    is_odd = lax.rem(lax.axis_index("gx"), 2) == 1
    right = jnp.where(is_odd, odd, even).reshape(-1, 8, 128)
    left = jnp.where(is_odd, even, odd).reshape(-1, 8, 128)
    inner = inner_ref[...].reshape(-1, 8, 128)
    right = jnp.stack([pltpu.roll(right, 4, 1), right], axis=1).reshape(inner.shape)
    left = jnp.stack([left, pltpu.roll(left, 4, 1)], axis=1).reshape(inner.shape)
    low = low_half(inner.shape)
    out_ref[:, 0:8, :] = jnp.where(low, left, inner)
    out_ref[:, 8:16, :] = jnp.where(low, inner, right)


def vmem(count):
    return [pl.BlockSpec(memory_space=pltpu.VMEM)] * count


def call(kernel, name, operands, outs, scratch=(), flops=0, aliases=None):
    shapes = [jax.ShapeDtypeStruct(shape, dtype) for shape, dtype in outs]
    return pl.pallas_call(
        kernel,
        out_shape=shapes,
        in_specs=vmem(len(operands)),
        out_specs=vmem(len(outs)),
        scratch_shapes=list(scratch),
        input_output_aliases=aliases or {},
        compiler_params=pltpu.CompilerParams(vmem_limit_bytes=32 * 1024 * 1024),
        cost_estimate=pl.CostEstimate(flops=flops, bytes_accessed=1 << 20, transcendentals=0),
        name=name,
    )(*operands)


def on_device(x, ag, tw, ow, pb, hg, ew, sw):
    height, breadth = x.shape[0], x.shape[1]
    n = height * WIN
    table = ((64, HEADS * 128), F32)
    prepared = [((256, 128), BF16), ((256, 256), BF16)]
    weights = (x, tw, ow, ew, sw, ag, pb, hg)
    kept = [((n, C), F32)] + [((n // 2, C), F32)] * 2 + [((n, C), BF16)] + [((n // 2, C), BF16)] * 2
    kept += [table] + prepared
    rows = [((WIN, breadth, C), BF16)] * 2
    (start,) = call(start_kernel, "start", (), [((8, 128), jnp.int32)], (), 4 * 10**10)
    last, first = call(
        edge_rows_kernel, "edge_rows", (x, start, ag, pb, hg), rows, [pltpu.SemaphoreType.DMA((2,))]
    )

    def run(*operands):
        return call(first_kernel, "first", operands, rows[0:1] + kept, (), 4 * 10**9, {8: 0})

    def skip(*operands):
        return call(nothing_kernel, "nothing", operands[8:9], rows[0:1] + kept, (), 0, {0: 0})

    up = shift(last, "gy", 1)
    first, *state = lax.cond(goes_first(), run, skip, *weights, first)
    down = shift(first, "gy", -1)
    state = call(
        second_kernel, "second", (*weights, *state, up), kept, (), 4 * 10**9, {8 + i: i for i in range(9)}
    )
    fa, fright, fleft, na, right, left, bias, wqv, wk = state
    va, odd, even = call(
        halo_kernel, "halo", (up, down, right, left, bias, wqv, wk, ow, ew, sw, ag, hg),
        [((64, C), BF16)] + [((n // 2 + 32, C), BF16)] * 2, (), 10**9,
    )
    from_odd = swap(odd, "gx", 1)
    inputs = (fa, na, va, pb, tw, ow, ew, sw, hg)
    made = [((n, C), F32)] + [table] * 4 + prepared
    scratch = [pltpu.VMEM(*table)] * 2
    even, *state = call(
        middle_early_kernel, "middle_early", (*inputs, even), [(even.shape, BF16)] + made, scratch,
        2 * 10**9, {9: 0},
    )
    from_even = swap(even, "gx", 0)
    oa, *tables, wqv, wk = call(
        middle_late_kernel, "middle_late", (*inputs, *state), made, scratch, 2 * 10**9,
        {9 + i: i for i in range(7)},
    )
    rest = (wqv, wk, ow, ew, sw, hg)
    (ob,) = call(
        odd_border_kernel, "odd_border", (fright, fleft, odd, from_odd, *tables[0:2], *rest, even),
        [((n // 2, C), F32)], (), 10**9,
    )
    return call(
        even_border_kernel, "even_border", (fright, fleft, even, from_even, *tables[2:4], *rest, oa, ob),
        [((height, breadth, C), F32)], (), 10**9,
    )[0]


def solution(mesh):
    return jax.shard_map(
        on_device,
        mesh=mesh,
        in_specs=(P("gy", "gx", None), P(), P(), P(), P(), P(), P(), P()),
        out_specs=P("gy", "gx", None),
        check_vma=False,
    )
```
